128 devices in a mesh: comp: 4 (over y), lon: 32 (over x, z, core).
Axes of the slice: x: 4, y: 4, z: 4, core: 2. Of those that a mesh axis runs over, the one named last changes fastest.
Arguments:
- spectra: float32 [384, 1728, 128], P(('comp', 'lon')), may hold values from 0.05 to 2
- wind_vectors: float32 [384, 2, 128], P(('comp', 'lon')), may hold values from -30 to 30
- slot_block: int32 [384], replicated, may hold values from -1 to 7, as said below
- wet_mask: int32 [128, 256], replicated, may hold values 0 or 1
- depth_class: int32 [128, 2], replicated, may hold values from 0 to 7
Outputs:
- new_spectra: float32 [384, 1728, 128], P(('comp', 'lon'))
The draws below stay inside these ranges and needn't reach their ends.
Inputs may be any that keep to these rules, and one draw needn't show every extreme that they name: `slot_block`: slot k of device c * 32 + r (comp index c, lon index r) holds block v of region (r + k - 1) mod 32, at longitude region * 4 + v // 2 and latitude block v mod 2, or is empty (-1); each of a region's 8 blocks is held by exactly one slot, and each of the three bands k of every region holds at least one block.
All inputs are finite; a program needn't handle non-finite values.
Results may differ from the reference program's by a relative error of at most 0.00002.
Values sent between devices are 32-bit elements; how exact they have to be, the bound alone decides.
A program may use at most 128 MiB of HBM per device.

```python
import math
import jax
import jax.numpy as jnp
from jax import lax

DIRECTION_COUNT = 36
FREQUENCY_COUNT = 48
BLOCK_POINTS = 128
NDEPTH = 8
NSUB = 4
LATB = 2
SPECTRAL_COUNT = 1728
BLK_REG = 8
CAP = 1
SLOTS = 3
TOTAL_SLOTS = 384
GRID_LON = 128
GRID_LAT = 256
N_COMP = 4
N_LON = 32


def draw_slot_block(key, part):
    key = jax.random.fold_in(key, 7)
    incoming = 3 * N_COMP * CAP
    region_keys = jax.random.split(key, N_LON)

    def shuffled(region_key):
        return jax.random.permutation(region_key, incoming).astype(jnp.int32)
    orders = jax.vmap(shuffled)(region_keys)
    by_band = orders.reshape(N_LON, 3, N_COMP * CAP)
    band_least = jnp.min(by_band, axis=2)
    leading = by_band == band_least[:, :, None]
    scores = jnp.where(leading, by_band - incoming, by_band).reshape(N_LON, incoming)
    ranks = jnp.argsort(jnp.argsort(scores, axis=1, stable=True), axis=1, stable=True).astype(jnp.int32)
    device_ids = jnp.arange(N_COMP * N_LON, dtype=jnp.int32)
    src_group = device_ids // N_LON
    src_region = device_ids % N_LON
    slot_numbers = jnp.arange(SLOTS, dtype=jnp.int32)
    band_index = slot_numbers // CAP
    band_slot = slot_numbers % CAP
    dest_region = (src_region[:, None] + band_index[None, :] - 1) % N_LON
    position = band_index[None, :] * (N_COMP * CAP) + src_group[:, None] * CAP + band_slot[None, :]
    values = ranks[dest_region, position]
    return jnp.where(values < BLK_REG, values, -1).reshape(-1).astype(jnp.int32)


def with_ends(result, key, low, top_value):
    spot = [jax.random.randint(jax.random.fold_in(key, axis), (), 0, length) for axis, length in enumerate(result.shape)]
    longest = result.shape.index(max(result.shape))
    neighbour = spot[:longest] + [(spot[longest] + 1) % result.shape[longest]] + spot[longest + 1:]
    return result.at[tuple(spot)].set(low).at[tuple(neighbour)].set(top_value)


def levels(key, shape, cuts, least, largest):
    def one(axis_at, shards_of):
        steps = jax.random.uniform(jax.random.fold_in(jax.random.fold_in(key, 6), axis_at), (shards_of,), jnp.float32, least / len(cuts), largest / len(cuts))
        return jnp.repeat(jnp.exp(steps), shape[axis_at] // shards_of).reshape((-1,) + (1,) * (len(shape) - axis_at - 1))

    gain = one(*cuts[0])
    for cut in cuts[1:]:
        gain = gain * one(*cut)
    return gain


def gaussian(stream_key, dims, spread, reach, cuts=(), held_as=jnp.bfloat16):
    array = jax.random.normal(stream_key, dims, jnp.float32) * spread
    if len(cuts) > 0:
        array = levels(stream_key, dims, cuts, -0.22, 0.18) * array
    return jnp.clip(array, min=-reach, max=reach).astype(held_as)


def setup_inputs(seed: int = 0) -> dict:
    key_list = jax.random.split(jax.random.key(seed), 6)
    spectra = jnp.clip(jnp.exp(math.log(2.0) - 3.6888794 * jax.random.uniform(key_list[0], (TOTAL_SLOTS, SPECTRAL_COUNT, BLOCK_POINTS), jnp.float32) ** levels(key_list[0], (TOTAL_SLOTS, SPECTRAL_COUNT, BLOCK_POINTS), ((0, 128),), -0.2, 0.2)), 0.05, 2.0)
    wind_vectors = gaussian(key_list[1], (TOTAL_SLOTS, 2, BLOCK_POINTS), 8.0, 30.0, ((0, 128),), jnp.float32)
    slot_block = draw_slot_block(jax.random.fold_in(key_list[5], 71), 0)
    wet_mask = with_ends((jax.random.randint(key_list[3], (GRID_LON, GRID_LAT), 0, 4) < 3).astype(jnp.int32), jax.random.fold_in(key_list[3], 1), 0, 1)
    depth_class = with_ends(jax.random.randint(key_list[4], (GRID_LON, LATB), 0, NDEPTH), jax.random.fold_in(key_list[4], 1), 0, NDEPTH - 1).astype(jnp.int32)
    return {"spectra": spectra, "wind_vectors": wind_vectors, "slot_block": slot_block, "wet_mask": wet_mask, "depth_class": depth_class}


GRAVITY = 9.81
FREQ_MIN = 0.0418
FREQ_RATIO = 1.07
GAIN_INPUT = 0.5
DISSIPATION = 0.3
SPEED_LON = 0.45
SPEED_LAT = 0.9
TURN_LAT = 0.3
TURN_DEPTH = 0.4

def frequencies(number):
    return 2.0 * math.pi * FREQ_MIN * FREQ_RATIO ** jnp.arange(number, dtype=jnp.float32)

def directions(number):
    angles = (jnp.arange(number, dtype=jnp.float32) + 0.5) * (2.0 * math.pi / number)
    return (jnp.cos(angles), jnp.sin(angles))

def latitudes(number):
    angles = (-60.0 + (jnp.arange(number, dtype=jnp.float32) + 0.5) * (120.0 / number)) * (math.pi / 180.0)
    return (jnp.cos(angles), jnp.tan(angles))

def speed_table(number, angular_freq):
    depths = 8.0 * 2.0 ** jnp.arange(number, dtype=jnp.float32)
    deep_wave = angular_freq * angular_freq / GRAVITY
    deep_depth = deep_wave[None, :] * depths[:, None]
    wavenumber = deep_wave[None, :] / jnp.sqrt(jnp.tanh(deep_depth))
    twice_kh = 2.0 * wavenumber * depths[:, None]
    kh_factor = 2.0 * twice_kh * jnp.exp(-twice_kh) / (1.0 - jnp.exp(-2.0 * twice_kh))
    group_speed = 0.5 * angular_freq[None, :] / wavenumber * (1.0 + kh_factor)
    return group_speed / jnp.max(group_speed)

def source_terms(energy, wind_vectors, angular_freq, cos_dir, sin_dir):
    weights = angular_freq / (jnp.sum(angular_freq) * cos_dir.shape[0])
    total_energy = lax.optimization_barrier(jnp.sum(energy * weights[None, :, None, None], axis=(1, 2)))
    mean_freq = lax.optimization_barrier(jnp.sum(energy * (weights * angular_freq)[None, :, None, None], axis=(1, 2))) / (total_energy + 1e-06)
    wind_along = wind_vectors[:, 0][:, None, :] * cos_dir[None, :, None] + wind_vectors[:, 1][:, None, :] * sin_dir[None, :, None]
    excess = jnp.maximum(wind_along[:, None] / (GRAVITY / angular_freq)[None, :, None, None] - 1.0, 0.0)
    growth = GAIN_INPUT * (angular_freq / angular_freq[-1])[None, :, None, None] * excess / (1.0 + excess)
    freq_ratio = angular_freq[None, :, None, None] / mean_freq[:, None, None, :]
    damping = DISSIPATION * freq_ratio * freq_ratio * (total_energy / (total_energy + 1.0))[:, None, None, :]
    return energy * (1.0 + growth) / (1.0 + damping)

def transport_lon(energy, cell_speed, wet_cols, cos_dir, cos_lat):
    velocity = SPEED_LON * cell_speed[:, None] * cos_dir[None, :, None, None] / cos_lat
    face_speed = 0.5 * (velocity[:, :, :-1] + velocity[:, :, 1:]) * wet_cols[:-1] * wet_cols[1:]
    fluxes = jnp.maximum(face_speed, 0.0) * energy[:, :, :-1] + jnp.minimum(face_speed, 0.0) * energy[:, :, 1:]
    return energy[:, :, 1:-1] - (fluxes[:, :, 1:] - fluxes[:, :, :-1])

def transport_lat(energy, cell_speed, wet_cols, sin_dir):
    velocity = SPEED_LAT * cell_speed[:, None] * sin_dir[None, :, None, None]
    face_speed = 0.5 * (velocity[..., :-1] + velocity[..., 1:]) * wet_cols[:, :-1] * wet_cols[:, 1:]
    fluxes = jnp.maximum(face_speed, 0.0) * energy[..., :-1] + jnp.minimum(face_speed, 0.0) * energy[..., 1:]
    boundary = jnp.zeros_like(fluxes[..., :1])
    return energy - (jnp.concatenate([fluxes, boundary], -1) - jnp.concatenate([boundary, fluxes], -1))

def turning(energy, cell_speed, east_speed, west_speed, cos_dir, sin_dir, tan_lat):
    turn_rate = TURN_LAT * cell_speed[:, None] * cos_dir[None, :, None, None] * tan_lat + TURN_DEPTH * (east_speed - west_speed)[:, None] * sin_dir[None, :, None, None]
    face_speed = 0.5 * (turn_rate + jnp.roll(turn_rate, -1, 1))
    fluxes = jnp.maximum(face_speed, 0.0) * energy + jnp.minimum(face_speed, 0.0) * jnp.roll(energy, -1, 1)
    return energy - (fluxes - jnp.roll(fluxes, 1, 1))

def substep(energy, cell_speed, wet_cols, cos_dir, sin_dir, cos_lat, tan_lat):
    interior = transport_lon(energy, cell_speed, wet_cols, cos_dir, cos_lat)
    middle = cell_speed[:, 1:-1]
    wet_middle = wet_cols[1:-1]
    interior = transport_lat(interior, middle, wet_middle, sin_dir)
    interior = turning(interior, middle, cell_speed[:, 2:], cell_speed[:, :-2], cos_dir, sin_dir, tan_lat)
    return interior * wet_middle

def periodic(values, dimension):
    count = values.shape[dimension]
    first = lax.slice_in_dim(values, 0, 1, axis=dimension)
    last = lax.slice_in_dim(values, count - 1, count, axis=dimension)
    return jnp.concatenate([last, values, first], axis=dimension)

def reference(spectra, wind_vectors, slot_block, wet_mask, depth_class):
    angular_freq = frequencies(FREQUENCY_COUNT)
    cos_dir, sin_dir = directions(DIRECTION_COUNT)
    cos_lat, tan_lat = latitudes(GRID_LAT)
    device_count = N_COMP * N_LON
    block_count = GRID_LON * LATB

    def force(pieces):
        return source_terms(pieces[0], pieces[1], angular_freq, cos_dir, sin_dir)
    forced_spectra = lax.map(force, (spectra.reshape(device_count, SLOTS, FREQUENCY_COUNT, DIRECTION_COUNT, BLOCK_POINTS), wind_vectors.reshape(device_count, SLOTS, 2, BLOCK_POINTS)))
    forced_spectra = forced_spectra.reshape(TOTAL_SLOTS, FREQUENCY_COUNT, DIRECTION_COUNT, BLOCK_POINTS)
    slot_numbers = jnp.arange(TOTAL_SLOTS, dtype=jnp.int32)
    src_region = slot_numbers // SLOTS % N_LON
    band_index = slot_numbers % SLOTS // CAP
    dest_region = (src_region + band_index - 1) % N_LON
    occupied = slot_block >= 0
    grid_block = jnp.where(occupied, dest_region * BLK_REG + slot_block, block_count).astype(jnp.int32)
    holder = jnp.zeros((block_count + 1,), jnp.int32).at[grid_block].set(slot_numbers)[:block_count]
    blocks = jnp.transpose(jnp.take(forced_spectra, holder, axis=0), (1, 0, 2, 3))
    cell_depth = jnp.repeat(depth_class, BLOCK_POINTS, axis=1)
    cell_speed = jnp.transpose(speed_table(NDEPTH, angular_freq)[cell_depth], (2, 0, 1))
    wet_cols = periodic(wet_mask.astype(jnp.float32), 0)

    def propagate(pieces):
        energy = pieces[0].reshape(GRID_LON, LATB, DIRECTION_COUNT, BLOCK_POINTS).transpose(2, 0, 1, 3).reshape(1, DIRECTION_COUNT, GRID_LON, GRID_LAT)
        speed_cols = periodic(pieces[1][None], 1)
        for substep_index in range(NSUB):
            energy = substep(periodic(energy, 2), speed_cols, wet_cols, cos_dir, sin_dir, cos_lat, tan_lat)
        return energy.reshape(DIRECTION_COUNT, GRID_LON, LATB, BLOCK_POINTS).transpose(1, 2, 0, 3).reshape(block_count, DIRECTION_COUNT, BLOCK_POINTS)
    moved = jnp.transpose(lax.map(propagate, (blocks, cell_speed)), (1, 0, 2, 3))
    return_blocks = jnp.take(moved, jnp.minimum(grid_block, block_count - 1), axis=0)
    return_blocks = return_blocks * occupied.astype(jnp.float32)[:, None, None, None]
    return return_blocks.reshape(TOTAL_SLOTS, SPECTRAL_COUNT, BLOCK_POINTS)
```

```python
import functools

import jax
import jax.numpy as jnp
import numpy as np
from jax import lax
from jax.experimental import pallas as pl
from jax.experimental.pallas import tpu as pltpu
from jax.sharding import PartitionSpec as P

MESH = pl.DeviceIdType.MESH

DIRS = 36
HALF = DIRS // 2
FREQS = 48
GROUPS = 4
REGIONS = 32
SLOTS = 3
SOURCES = GROUPS * SLOTS
POINTS = 128
NDEPTH = 8
NSUB = 4
BLOCKS = 8
GRID_LON = 128
REGION_LONS = GRID_LON // REGIONS
GROUP_FREQS = FREQS // GROUPS
COMPS = FREQS * DIRS
GROUP_COMPS = GROUP_FREQS * DIRS

CHUNK = 2
CHUNKS = GROUP_FREQS // CHUNK
ROWS = CHUNK * DIRS

GRAVITY = 9.81

ORDER = [(q + 27) % DIRS for q in range(DIRS)]
ANGLE = (np.arange(DIRS) + 0.5) * (2.0 * np.pi / DIRS)
COS = np.cos(ANGLE)
SIN = np.sin(ANGLE)
COS_FACE = 0.5 * (COS + np.roll(COS, -1))
SIN_FACE = 0.5 * (SIN + np.roll(SIN, -1))

T_SPEED = 0
T_ALONG = T_SPEED + NDEPTH * FREQS
T_GAIN = T_ALONG + FREQS
T_SQUARE = T_GAIN + FREQS
T_WEIGHT = T_SQUARE + FREQS
T_WEIGHT_FREQ = T_WEIGHT + FREQS
T_SIZE = 640


def scalar_table():
    sigma = 2.0 * np.pi * 0.0418 * 1.07 ** np.arange(FREQS, dtype=np.float64)
    depth = 8.0 * 2.0 ** np.arange(NDEPTH, dtype=np.float64)
    deep = sigma * sigma / GRAVITY
    number = deep[None, :] / np.sqrt(np.tanh(deep[None, :] * depth[:, None]))
    twice = 2.0 * number * depth[:, None]
    factor = 2.0 * twice * np.exp(-twice) / (1.0 - np.exp(-2.0 * twice))
    speed = 0.5 * sigma[None, :] / number * (1.0 + factor)
    speed = speed / speed.max()
    weight = sigma / (sigma.sum() * DIRS)
    table = np.zeros(T_SIZE, np.float64)
    table[T_SPEED:T_ALONG] = speed.reshape(-1)
    table[T_ALONG:T_GAIN] = sigma / GRAVITY
    table[T_GAIN:T_SQUARE] = 0.5 * sigma / sigma[-1]
    table[T_SQUARE:T_WEIGHT] = sigma * sigma
    table[T_WEIGHT:T_WEIGHT_FREQ] = weight
    table[T_WEIGHT_FREQ:T_WEIGHT_FREQ + FREQS] = weight * sigma
    return table.astype(np.float32)


def latitude_table():
    count = 2 * POINTS
    phi = (-60.0 + (np.arange(count) + 0.5) * 120.0 / count) * np.pi / 180.0
    rows = np.concatenate([0.5 * 0.45 / np.cos(phi), 0.3 * np.tan(phi)])
    parts = rows.reshape(2, 1, 2, POINTS)
    return np.broadcast_to(parts, (2, REGION_LONS, 2, POINTS)).reshape(2, 8, POINTS).astype(np.float32)


def wait_bytes(ref, sem):
    pltpu.make_async_copy(ref, ref, sem).wait()


def kernel(
    x, wind, slots, wet, depth, table, lat, out,
    xv, windv, slot_s, wetv, depthv, table_s, latv,
    aux_out, aux_in, scal, near, coef, ordered, field, halo_w, halo_e, back, blocks, outb,
    local_sem, in_send, in_recv, aux_send, aux_recv, halo_send, halo_recv, out_send, out_recv,
    *inb,
):
    me_c = lax.axis_index("comp")
    me_r = lax.axis_index("lon")

    def region(shift):
        return lax.rem(me_r + (shift + REGIONS), REGIONS)

    loads = [
        pltpu.make_async_copy(src, dst, local_sem.at[n])
        for n, (src, dst) in enumerate(
            ((x, xv), (wind, windv), (slots, slot_s), (wet, wetv), (depth, depthv), (table, table_s), (lat, latv))
        )
    ]
    for load in loads:
        load.start()

    barrier = pltpu.get_barrier_semaphore()
    for dg in range(GROUPS):
        for dr in (-1, 0, 1):
            if dg or dr:
                pl.semaphore_signal(
                    barrier, inc=1, device_id=(lax.rem(me_c + dg, GROUPS), region(dr)), device_id_type=MESH
                )
    pl.semaphore_wait(barrier, SOURCES - 1)

    for ch in range(CHUNKS):
        for dg in (2, 1, 3, 0):
            to = lax.rem(me_c + dg, GROUPS)
            for k in range(SLOTS):
                src = x.at[k, pl.ds(to * GROUP_COMPS + ch * ROWS, ROWS)]
                dst = inb[ch].at[me_c * SLOTS + k]
                if dg == 0 and k == 1:
                    pltpu.make_async_copy(src, dst, in_recv.at[ch]).start()
                else:
                    pltpu.make_async_remote_copy(
                        src, dst, in_send.at[ch], in_recv.at[ch], device_id=(to, region(k - 1)), device_id_type=MESH
                    ).start()

    row = lax.broadcasted_iota(jnp.int32, (8, POINTS), 0)
    lane = lax.broadcasted_iota(jnp.int32, (8, POINTS), 1)

    for load in loads:
        load.wait()
    upper = row < 4
    for k in range(SLOTS):
        def pair(p, sums, k=k):
            total, moment = sums
            tiles = [xv[k, pl.ds(pl.multiple_of(p * 72 + 8 * n, 8), 8), :] for n in range(9)]
            first = (tiles[0] + tiles[1]) + (tiles[2] + tiles[3]) + jnp.where(upper, tiles[4], 0.0)
            second = (tiles[5] + tiles[6]) + (tiles[7] + tiles[8]) + jnp.where(upper, 0.0, tiles[4])
            total = total + first * table_s[T_WEIGHT + 2 * p] + second * table_s[T_WEIGHT + 2 * p + 1]
            moment = moment + first * table_s[T_WEIGHT_FREQ + 2 * p] + second * table_s[T_WEIGHT_FREQ + 2 * p + 1]
            return total, moment

        zero = jnp.zeros((8, POINTS), jnp.float32)
        total, moment = lax.fori_loop(0, FREQS // 2, pair, (zero, zero))
        total = jnp.sum(total, axis=0, keepdims=True)
        moment = jnp.sum(moment, axis=0, keepdims=True)
        mean = moment / (total + 1e-6)
        aux_out[k] = zero
        aux_out[k, 0:2, :] = windv[k]
        aux_out[k, 2:3, :] = 0.3 * (total / (total + 1.0)) / (mean * mean)

    for dg in (2, 1, 3, 0):
        to = lax.rem(me_c + dg, GROUPS)
        for k in range(SLOTS):
            dst = aux_in.at[me_c * SLOTS + k]
            if dg == 0 and k == 1:
                pltpu.make_async_copy(aux_out.at[k], dst, aux_recv).start()
            else:
                pltpu.make_async_remote_copy(
                    aux_out.at[k], dst, aux_send, aux_recv, device_id=(to, region(k - 1)), device_id_type=MESH
                ).start()

    for n in range(3):
        for v in range(BLOCKS):
            lon = lax.rem(me_r * REGION_LONS + (v // 2 + n - 1 + GRID_LON), GRID_LON)
            part = v % 2
            rows = pl.ds(pl.multiple_of(lon // 8 * 8, 8), 8)
            here = row == lax.rem(lon, 8)
            levels = jnp.broadcast_to(depthv[rows, part:part + 1].astype(jnp.float32), (8, POINTS))
            near[0, n, v:v + 1, :] = jnp.sum(jnp.where(here, levels, 0.0), axis=0, keepdims=True)
            cells = wetv[rows, part * POINTS:(part + 1) * POINTS].astype(jnp.float32)
            near[1, n, v:v + 1, :] = jnp.sum(jnp.where(here, cells, 0.0), axis=0, keepdims=True)

    def shift_down(value):
        rolled = pltpu.roll(value, 1, 1)
        return jnp.where(lane == 0, pltpu.roll(rolled, 1, 0), rolled)

    def shift_up(value):
        rolled = pltpu.roll(value, POINTS - 1, 1)
        return jnp.where(lane == POINTS - 1, pltpu.roll(rolled, 7, 0), rolled)

    def prepare(i, _):
        speeds = []
        for n in range(3):
            level = near[0, n]
            speed = jnp.zeros((8, POINTS), jnp.float32)
            for d in range(NDEPTH):
                speed = jnp.where(level == float(d), table_s[T_SPEED + d * FREQS + me_c * GROUP_FREQS + i], speed)
            speeds.append(speed)
        west, mid, east = speeds
        wet_west, wet_mid, wet_east = near[1, 0], near[1, 1], near[1, 2]
        coef[i, 0] = latv[0] * (mid + east) * wet_mid * wet_east
        coef[i, 1] = latv[0] * (mid + west) * wet_mid * wet_west
        last = (lax.rem(row, 2) == 1) & (lane == POINTS - 1)
        face = jnp.where(last, 0.0, 0.45 * (mid + shift_up(mid)) * wet_mid * shift_up(wet_mid))
        coef[i, 2] = face
        coef[i, 3] = shift_down(face)
        coef[i, 4] = latv[1] * mid
        coef[i, 5] = 0.4 * (east - west)
        return 0

    lax.fori_loop(0, GROUP_FREQS, prepare, 0)

    held = []
    for s in range(SOURCES):
        held.append(slot_s[((s // SLOTS) * REGIONS + region(1 - s % SLOTS)) * SLOTS + s % SLOTS])
    holder = []
    for v in range(BLOCKS):
        found = jnp.int32(0)
        for s in range(SOURCES):
            found = jnp.where(held[s] == v, jnp.int32(s), found)
        holder.append(found)
    back_row = [jnp.maximum(h, 0) for h in held]

    wait_bytes(aux_in, aux_recv)
    for v in range(BLOCKS):
        for n in range(3):
            scal[n, v:v + 1, :] = aux_in[holder[v]][n:n + 1, :]

    def halo_copies(ch, s):
        freqs = pl.ds(ch * CHUNK, CHUNK)
        return (
            pltpu.make_async_remote_copy(
                field.at[s, freqs, 0:HALF, 6:8, :], halo_w.at[s, freqs, :, 0:2, :],
                halo_send.at[0, s, ch], halo_recv.at[0, s, ch], device_id=(me_c, region(1)), device_id_type=MESH,
            ),
            pltpu.make_async_remote_copy(
                field.at[s, freqs, HALF:DIRS, 0:2, :], halo_e.at[s, freqs, :, 6:8, :],
                halo_send.at[1, s, ch], halo_recv.at[1, s, ch], device_id=(me_c, region(-1)), device_id_type=MESH,
            ),
        )

    def send_halos(ch, s):
        for copy in halo_copies(ch, s):
            copy.start()

    def source_terms(ch):
        wind_x, wind_y, damp = scal[0], scal[1], scal[2]
        for n in range(CHUNK):
            i = ch * CHUNK + n
            f = me_c * GROUP_FREQS + i
            along = table_s[T_ALONG + f]
            gain = table_s[T_GAIN + f]
            scale = 1.0 / (1.0 + damp * table_s[T_SQUARE + f])
            for q in range(DIRS):
                j = ORDER[q]
                energy = ordered[pl.ds(n * DIRS + j, 8, stride=ROWS), :]
                ratio = jnp.maximum((wind_x * float(COS[j]) + wind_y * float(SIN[j])) * along, 1.0)
                field[0, i, q] = energy * ((1.0 + gain) - gain / ratio) * scale

    def substep(ch, s):
        def one(n, _):
            i = ch * CHUNK + n
            east_face, west_face, up_face, down_face = coef[i, 0], coef[i, 1], coef[i, 2], coef[i, 3]
            turn_lat, turn_depth = coef[i, 4], coef[i, 5]
            wet_here = near[1, 1]

            def moved(q):
                j = ORDER[q]
                energy = field[s, i, q]
                if q < HALF:
                    west = jnp.where(row < 2, halo_w[s, i, q], pltpu.roll(energy, 2, 0))
                    flux = east_face * energy - west_face * west
                else:
                    east = jnp.where(row >= 6, halo_e[s, i, q - HALF], pltpu.roll(energy, 6, 0))
                    flux = east_face * east - west_face * energy
                energy = energy - float(COS[j]) * flux
                if SIN[j] > 0:
                    share = up_face * energy
                    flux = share - shift_down(share)
                else:
                    share = down_face * energy
                    flux = shift_up(share) - share
                return energy - float(SIN[j]) * flux

            def turned(q, here, following):
                j = ORDER[q]
                rate = turn_lat * float(COS_FACE[j]) + turn_depth * float(SIN_FACE[j])
                return rate * jnp.where(rate > 0.0, here, following)

            energies = [moved(q) for q in range(DIRS)]
            fluxes = [turned(q, energies[q], energies[(q + 1) % DIRS]) for q in range(DIRS)]
            for q in range(DIRS):
                field[s + 1, i, q] = (energies[q] - (fluxes[q] - fluxes[q - 1])) * wet_here
            return 0

        lax.fori_loop(0, CHUNK, one, 0)

    def send_back(ch):
        for n in range(CHUNK):
            for q in range(DIRS):
                back[pl.ds(n * DIRS + ORDER[q], 8, stride=ROWS), :] = field[NSUB, ch * CHUNK + n, q]
        for v in range(BLOCKS):
            blocks[v] = back[v * ROWS:(v + 1) * ROWS, :]
        for s in range(SOURCES):
            outb[ch, s] = blocks[back_row[s]]
        for dg in (2, 1, 3, 0):
            to = lax.rem(me_c + dg, GROUPS)
            for k in range(SLOTS):
                src = outb.at[ch, to * SLOTS + k]
                dst = out.at[k, pl.ds(me_c * GROUP_COMPS + ch * ROWS, ROWS)]
                if dg == 0 and k == 1:
                    pltpu.make_async_copy(src, dst, out_recv).start()
                else:
                    pltpu.make_async_remote_copy(
                        src, dst, out_send.at[ch], out_recv, device_id=(to, region(1 - k)), device_id_type=MESH
                    ).start()

    def step(t, _):
        def one(n, _):
            s = NSUB - 1 - n
            ch = t - 1 - s

            @pl.when((ch >= 0) & (ch < CHUNKS))
            def _():
                for copy in halo_copies(ch, s):
                    copy.wait_recv()
                substep(ch, s)

                @pl.when(s < NSUB - 1)
                def _():
                    send_halos(ch, s + 1)

                @pl.when(s == NSUB - 1)
                def _():
                    send_back(ch)

            return 0

        lax.fori_loop(0, NSUB, one, 0)

        for ch in range(CHUNKS):
            @pl.when(t == ch)
            def _(ch=ch):
                wait_bytes(inb[ch], in_recv.at[ch])
                for v in range(BLOCKS):
                    ordered[v * ROWS:(v + 1) * ROWS, :] = inb[ch][holder[v]]

        @pl.when(t < CHUNKS)
        def _():
            source_terms(t)
            send_halos(t, 0)

        return 0

    lax.fori_loop(0, CHUNKS + NSUB, step, 0)

    wait_bytes(aux_in.at[0:SOURCES - 1], aux_send)
    for ch in range(CHUNKS):
        wait_bytes(inb[ch].at[0:SOURCES - 1], in_send.at[ch])
        wait_bytes(outb.at[ch, 0:SOURCES - 1], out_send.at[ch])

    def drain(n, _):
        for copy in halo_copies(lax.rem(n, CHUNKS), n // CHUNKS):
            copy.wait_send()
        return 0

    lax.fori_loop(0, CHUNKS * NSUB, drain, 0)
    wait_bytes(out, out_recv)


def per_device(spectra, wind_vectors, slot_block, wet_mask, depth_class):
    hbm = pl.BlockSpec(memory_space=pltpu.HBM)
    f32 = jnp.float32
    dma = pltpu.SemaphoreType.DMA
    moved = pl.pallas_call(
        kernel,
        out_shape=jax.ShapeDtypeStruct((SLOTS, COMPS, POINTS), f32),
        in_specs=[hbm] * 7,
        out_specs=hbm,
        scratch_shapes=[
            pltpu.VMEM((SLOTS, COMPS, POINTS), f32),
            pltpu.VMEM((SLOTS, 2, POINTS), f32),
            pltpu.SMEM((GROUPS * REGIONS * SLOTS,), jnp.int32),
            pltpu.VMEM((GRID_LON, 2 * POINTS), jnp.int32),
            pltpu.VMEM((GRID_LON, 2), jnp.int32),
            pltpu.SMEM((T_SIZE,), f32),
            pltpu.VMEM((2, 8, POINTS), f32),
            pltpu.VMEM((SLOTS, 8, POINTS), f32),
            pltpu.VMEM((SOURCES, 8, POINTS), f32),
            pltpu.VMEM((3, 8, POINTS), f32),
            pltpu.VMEM((2, 3, 8, POINTS), f32),
            pltpu.VMEM((GROUP_FREQS, 6, 8, POINTS), f32),
            pltpu.VMEM((BLOCKS * ROWS, POINTS), f32),
            pltpu.VMEM((NSUB + 1, GROUP_FREQS, DIRS, 8, POINTS), f32),
            pltpu.VMEM((NSUB, GROUP_FREQS, HALF, 8, POINTS), f32),
            pltpu.VMEM((NSUB, GROUP_FREQS, HALF, 8, POINTS), f32),
            pltpu.VMEM((BLOCKS * ROWS, POINTS), f32),
            pltpu.VMEM((BLOCKS, ROWS, POINTS), f32),
            pltpu.VMEM((CHUNKS, SOURCES, ROWS, POINTS), f32),
            dma((7,)),
            dma((CHUNKS,)),
            dma((CHUNKS,)),
            dma,
            dma,
            dma((2, NSUB, CHUNKS)),
            dma((2, NSUB, CHUNKS)),
            dma((CHUNKS,)),
            dma,
        ] + [pltpu.VMEM((SOURCES, ROWS, POINTS), f32) for _ in range(CHUNKS)],
        compiler_params=pltpu.CompilerParams(
            collective_id=0, has_side_effects=True, vmem_limit_bytes=62 * 1024 * 1024
        ),
        name="wave_step",
    )(spectra, wind_vectors, slot_block, wet_mask, depth_class, scalar_table(), latitude_table())
    first = (lax.axis_index("comp") * REGIONS + lax.axis_index("lon")) * SLOTS
    mine = lax.dynamic_slice_in_dim(slot_block, first, SLOTS)
    return jnp.where(mine[:, None, None] >= 0, moved, 0.0)


def solution(mesh):
    return jax.shard_map(
        per_device,
        mesh=mesh,
        in_specs=(P(("comp", "lon"), None, None), P(("comp", "lon"), None, None), P(), P(), P()),
        out_specs=P(("comp", "lon"), None, None),
        check_vma=False,
    )
```

```python
import functools

import jax
import jax.numpy as jnp
import numpy as np
from jax import lax
from jax.experimental import pallas as pl
from jax.experimental.pallas import tpu as pltpu
from jax.sharding import PartitionSpec as P

MESH = pl.DeviceIdType.MESH

DIRS = 36
HALF = DIRS // 2
FREQS = 48
GROUPS = 4
REGIONS = 32
SLOTS = 3
SOURCES = GROUPS * SLOTS
POINTS = 128
NDEPTH = 8
NSUB = 4
BLOCKS = 8
GRID_LON = 128
REGION_LONS = GRID_LON // REGIONS
GROUP_FREQS = FREQS // GROUPS
COMPS = FREQS * DIRS
GROUP_COMPS = GROUP_FREQS * DIRS

CHUNK = 2
CHUNKS = GROUP_FREQS // CHUNK
ROWS = CHUNK * DIRS

GRAVITY = 9.81

ORDER = [(q + 27) % DIRS for q in range(DIRS)]
ANGLE = (np.arange(DIRS) + 0.5) * (2.0 * np.pi / DIRS)
COS = np.cos(ANGLE)
SIN = np.sin(ANGLE)
COS_FACE = 0.5 * (COS + np.roll(COS, -1))
SIN_FACE = 0.5 * (SIN + np.roll(SIN, -1))

T_SPEED = 0
T_ALONG = T_SPEED + NDEPTH * FREQS
T_GAIN = T_ALONG + FREQS
T_SQUARE = T_GAIN + FREQS
T_WEIGHT = T_SQUARE + FREQS
T_WEIGHT_FREQ = T_WEIGHT + FREQS
T_SIZE = 640

WEST, MID, EAST, BESIDE = range(4)


def scalar_table():
    sigma = 2.0 * np.pi * 0.0418 * 1.07 ** np.arange(FREQS, dtype=np.float64)
    depth = 8.0 * 2.0 ** np.arange(NDEPTH, dtype=np.float64)
    deep = sigma * sigma / GRAVITY
    number = deep[None, :] / np.sqrt(np.tanh(deep[None, :] * depth[:, None]))
    twice = 2.0 * number * depth[:, None]
    factor = 2.0 * twice * np.exp(-twice) / (1.0 - np.exp(-2.0 * twice))
    speed = 0.5 * sigma[None, :] / number * (1.0 + factor)
    speed = speed / speed.max()
    weight = sigma / (sigma.sum() * DIRS)
    table = np.zeros(T_SIZE, np.float64)
    table[T_SPEED:T_ALONG] = speed.reshape(-1)
    table[T_ALONG:T_GAIN] = sigma / GRAVITY
    table[T_GAIN:T_SQUARE] = 0.5 * sigma / sigma[-1]
    table[T_SQUARE:T_WEIGHT] = sigma * sigma
    table[T_WEIGHT:T_WEIGHT_FREQ] = weight
    table[T_WEIGHT_FREQ:T_WEIGHT_FREQ + FREQS] = weight * sigma
    return table.astype(np.float32)


def latitude_table():
    count = 2 * POINTS
    phi = (-60.0 + (np.arange(count) + 0.5) * 120.0 / count) * np.pi / 180.0
    rows = np.concatenate([0.5 * 0.45 / np.cos(phi), 0.3 * np.tan(phi)])
    parts = rows.reshape(2, 1, 2, POINTS)
    return np.broadcast_to(parts, (2, REGION_LONS, 2, POINTS)).reshape(2, 8, POINTS).astype(np.float32)


def wait_bytes(ref, sem):
    pltpu.make_async_copy(ref, ref, sem).wait()


def kernel(
    x, wind, slots, wet, depth, table, lat, out,
    xv, windv, slot_s, wetv, depthv, table_s, latv,
    aux_out, aux_in, scal, cells, speeds, coef, ordered, field, halo_w, halo_e, one_on, two_on, three_on, back, blocks, outb,
    local_sem, in_send, in_recv, aux_send, aux_recv, halo_send, halo_recv, out_send, out_recv,
    *inb,
):
    me_c = lax.axis_index("comp")
    me_r = lax.axis_index("lon")

    def region(shift):
        return lax.rem(me_r + (shift + REGIONS), REGIONS)

    loads = [
        pltpu.make_async_copy(src, dst, local_sem.at[n])
        for n, (src, dst) in enumerate(
            ((x, xv), (wind, windv), (slots, slot_s), (wet, wetv), (depth, depthv), (table, table_s), (lat, latv))
        )
    ]
    for load in loads:
        load.start()

    barrier = pltpu.get_barrier_semaphore()
    for dg in range(GROUPS):
        for dr in (-1, 0, 1):
            if dg or dr:
                pl.semaphore_signal(
                    barrier, inc=1, device_id=(lax.rem(me_c + dg, GROUPS), region(dr)), device_id_type=MESH
                )
    pl.semaphore_wait(barrier, SOURCES - 1)

    for ch in range(CHUNKS):
        for dg in (2, 1, 3, 0):
            to = lax.rem(me_c + dg, GROUPS)
            for k in range(SLOTS):
                src = x.at[k, pl.ds(to * GROUP_COMPS + ch * ROWS, ROWS)]
                dst = inb[ch].at[me_c * SLOTS + k]
                if dg == 0 and k == 1:
                    pltpu.make_async_copy(src, dst, in_recv.at[ch]).start()
                else:
                    pltpu.make_async_remote_copy(
                        src, dst, in_send.at[ch], in_recv.at[ch], device_id=(to, region(k - 1)), device_id_type=MESH
                    ).start()

    row = lax.broadcasted_iota(jnp.int32, (8, POINTS), 0)
    lane = lax.broadcasted_iota(jnp.int32, (8, POINTS), 1)

    for load in loads:
        load.wait()
    upper = row < 4
    for k in range(SLOTS):
        def pair(p, sums, k=k):
            total, moment = sums
            tiles = [xv[k, pl.ds(pl.multiple_of(p * 72 + 8 * n, 8), 8), :] for n in range(9)]
            first = (tiles[0] + tiles[1]) + (tiles[2] + tiles[3]) + jnp.where(upper, tiles[4], 0.0)
            second = (tiles[5] + tiles[6]) + (tiles[7] + tiles[8]) + jnp.where(upper, 0.0, tiles[4])
            total = total + first * table_s[T_WEIGHT + 2 * p] + second * table_s[T_WEIGHT + 2 * p + 1]
            moment = moment + first * table_s[T_WEIGHT_FREQ + 2 * p] + second * table_s[T_WEIGHT_FREQ + 2 * p + 1]
            return total, moment

        zero = jnp.zeros((8, POINTS), jnp.float32)
        total, moment = lax.fori_loop(0, FREQS // 2, pair, (zero, zero))
        total = jnp.sum(total, axis=0, keepdims=True)
        moment = jnp.sum(moment, axis=0, keepdims=True)
        mean = moment / (total + 1e-6)
        aux_out[k] = zero
        aux_out[k, 0:2, :] = windv[k]
        aux_out[k, 2:3, :] = 0.3 * (total / (total + 1.0)) / (mean * mean)

    for dg in (2, 1, 3, 0):
        to = lax.rem(me_c + dg, GROUPS)
        for k in range(SLOTS):
            dst = aux_in.at[me_c * SLOTS + k]
            if dg == 0 and k == 1:
                pltpu.make_async_copy(aux_out.at[k], dst, aux_recv).start()
            else:
                pltpu.make_async_remote_copy(
                    aux_out.at[k], dst, aux_send, aux_recv, device_id=(to, region(k - 1)), device_id_type=MESH
                ).start()

    for n in range(16):
        lon = lax.rem(me_r * REGION_LONS + (n - 6 + GRID_LON), GRID_LON)
        levels = jnp.where(lane[0:2] == lon, depthv[...].astype(jnp.float32), 0.0)
        cells[0, 2 * n:2 * n + 2, :] = jnp.broadcast_to(jnp.sum(levels, axis=1, keepdims=True), (2, POINTS))
        rows = pl.ds(pl.multiple_of(lon // 8 * 8, 8), 8)
        here = row == lax.rem(lon, 8)
        for part in range(2):
            wet_rows = wetv[rows, part * POINTS:(part + 1) * POINTS].astype(jnp.float32)
            cells[1, 2 * n + part:2 * n + part + 1, :] = jnp.sum(
                jnp.where(here, wet_rows, 0.0), axis=0, keepdims=True
            )

    def from_lon(values, start):
        return values[2 * (start + 6):2 * (start + 6) + 8]

    def shift_down(value):
        rolled = pltpu.roll(value, 1, 1)
        return jnp.where(lane == 0, pltpu.roll(rolled, 1, 0), rolled)

    def shift_up(value):
        rolled = pltpu.roll(value, POINTS - 1, 1)
        return jnp.where(lane == POINTS - 1, pltpu.roll(rolled, 7, 0), rolled)

    last = (lax.rem(row, 2) == 1) & (lane == POINTS - 1)
    wets = cells.at[1]

    def prepare(i, _):
        for m in range(4):
            level = cells[0, 8 * m:8 * m + 8]
            speed = jnp.zeros((8, POINTS), jnp.float32)
            for d in range(NDEPTH):
                speed = jnp.where(level == float(d), table_s[T_SPEED + d * FREQS + me_c * GROUP_FREQS + i], speed)
            speeds[8 * m:8 * m + 8] = speed
        made = []
        for part, start in enumerate((-REGION_LONS, 0, REGION_LONS)):
            west, mid, east = (from_lon(speeds, start + n) for n in (-1, 0, 1))
            wet_west, wet_mid, wet_east = (from_lon(wets, start + n) for n in (-1, 0, 1))
            face = jnp.where(last, 0.0, 0.45 * (mid + shift_up(mid)) * wet_mid * shift_up(wet_mid))
            made.append((
                latv[0] * (mid + east) * wet_mid * wet_east,
                latv[0] * (mid + west) * wet_mid * wet_west,
                face,
                shift_down(face),
                latv[1] * mid,
                0.4 * (east - west),
            ))
        for n in range(6):
            for part in range(3):
                coef[i, part, n] = made[part][n]
            coef[i, BESIDE, n] = jnp.where(row < 4, made[EAST][n], made[WEST][n])
        return 0

    lax.fori_loop(0, GROUP_FREQS, prepare, 0)

    held = []
    for s in range(SOURCES):
        held.append(slot_s[((s // SLOTS) * REGIONS + region(1 - s % SLOTS)) * SLOTS + s % SLOTS])
    holder = []
    for v in range(BLOCKS):
        found = jnp.int32(0)
        for s in range(SOURCES):
            found = jnp.where(held[s] == v, jnp.int32(s), found)
        holder.append(found)
    back_row = [jnp.maximum(h, 0) for h in held]

    wait_bytes(aux_in, aux_recv)
    for v in range(BLOCKS):
        for n in range(3):
            scal[n, v:v + 1, :] = aux_in[holder[v]][n:n + 1, :]

    def halo_copies(ch):
        freqs = pl.ds(ch * CHUNK, CHUNK)
        return [
            pltpu.make_async_remote_copy(
                field.at[freqs], halo.at[freqs], halo_send.at[n, ch], halo_recv.at[n, ch],
                device_id=(me_c, region(shift)), device_id_type=MESH,
            )
            for n, (halo, shift) in enumerate(((halo_w, 1), (halo_e, -1)))
        ]

    def send_halos(ch):
        for copy in halo_copies(ch):
            copy.start()

    def source_terms(ch):
        wind_x, wind_y, damp = scal[0], scal[1], scal[2]
        for n in range(CHUNK):
            i = ch * CHUNK + n
            f = me_c * GROUP_FREQS + i
            along = table_s[T_ALONG + f]
            gain = table_s[T_GAIN + f]
            scale = 1.0 / (1.0 + damp * table_s[T_SQUARE + f])
            for q in range(DIRS):
                j = ORDER[q]
                energy = ordered[pl.ds(n * DIRS + j, 8, stride=ROWS), :]
                ratio = jnp.maximum((wind_x * float(COS[j]) + wind_y * float(SIN[j])) * along, 1.0)
                field[i, q] = energy * ((1.0 + gain) - gain / ratio) * scale

    def along_lon(q, parts, coefs, ring):
        turn = 2 if q < HALF else 6
        rolled = [pltpu.roll(part, turn, 0) for part in parts]
        edge = row < 2 if q < HALF else row >= 6
        moved = []
        for n, part in enumerate(parts):
            other = n - 1 if q < HALF else n + 1
            if ring:
                beside = jnp.where(edge, rolled[other % len(parts)], rolled[n])
            elif 0 <= other < len(parts):
                beside = jnp.where(edge, rolled[other], rolled[n])
            else:
                beside = rolled[n]
            from_west, from_east = (beside, part) if q < HALF else (part, beside)
            flux = coefs[n][0] * from_east - coefs[n][1] * from_west
            moved.append(part - float(COS[ORDER[q]]) * flux)
        return moved

    def along_lat(q, energy, coefs):
        sine = float(SIN[ORDER[q]])
        if sine > 0:
            share = coefs[2] * energy
            flux = share - shift_down(share)
        else:
            share = coefs[3] * energy
            flux = shift_up(share) - share
        return energy - sine * flux

    def refracted(moved, coefs, store):
        first = moved(0)
        here = first
        opening = before = None
        for q in range(DIRS):
            following = moved(q + 1) if q + 1 < DIRS else first
            j = ORDER[q]
            fluxes = []
            for n, part in enumerate(here):
                rate = coefs[n][4] * float(COS_FACE[j]) + coefs[n][5] * float(SIN_FACE[j])
                fluxes.append(rate * jnp.where(rate > 0.0, part, following[n]))
            if q == 0:
                opening = fluxes
            else:
                for n, part in enumerate(here):
                    store(q, n, part - (fluxes[n] - before[n]))
            before = fluxes
            here = following
        for n, part in enumerate(first):
            store(0, n, part - (opening[n] - before[n]))

    def propagate(ch):
        def one(n, _):
            i = ch * CHUNK + n
            west, mid, east, beside = ([coef[i, part, m] for m in range(6)] for part in range(4))
            wet_here = from_lon(wets, 0)
            wide = (west, mid, east)
            narrow = (mid, beside)

            def first_step(q):
                parts = along_lon(q, (halo_w[i, q], field[i, q], halo_e[i, q]), wide, False)
                return [along_lat(q, part, c) for part, c in zip(parts, wide)]

            def second_step(q):
                parts = along_lon(q, [one_on[part, q] for part in range(3)], wide, False)
                parts = (parts[MID], jnp.where(row < 4, parts[EAST], parts[WEST]))
                return [along_lat(q, part, c) for part, c in zip(parts, narrow)]

            def third_step(q):
                parts = along_lon(q, (two_on[0, q], two_on[1, q]), narrow, True)
                return [along_lat(q, part, c) for part, c in zip(parts, narrow)]

            def fourth_step(q):
                parts = along_lon(q, (three_on[0, q], three_on[1, q]), narrow, True)
                return [along_lat(q, parts[0], mid)]

            def to(buffer):
                def store(q, part, energy):
                    buffer[part, q] = energy
                return store

            def to_back(q, part, energy):
                back[pl.ds(n * DIRS + ORDER[q], 8, stride=ROWS), :] = energy * wet_here

            refracted(first_step, wide, to(one_on))
            refracted(second_step, narrow, to(two_on))
            refracted(third_step, narrow, to(three_on))
            refracted(fourth_step, (mid,), to_back)
            return 0

        lax.fori_loop(0, CHUNK, one, 0)

    def send_back(ch):
        for v in range(BLOCKS):
            blocks[v] = back[v * ROWS:(v + 1) * ROWS, :]
        for s in range(SOURCES):
            outb[ch, s] = blocks[back_row[s]]
        for dg in (2, 1, 3, 0):
            to = lax.rem(me_c + dg, GROUPS)
            for k in range(SLOTS):
                src = outb.at[ch, to * SLOTS + k]
                dst = out.at[k, pl.ds(me_c * GROUP_COMPS + ch * ROWS, ROWS)]
                if dg == 0 and k == 1:
                    pltpu.make_async_copy(src, dst, out_recv).start()
                else:
                    pltpu.make_async_remote_copy(
                        src, dst, out_send.at[ch], out_recv, device_id=(to, region(1 - k)), device_id_type=MESH
                    ).start()

    def step(t, _):
        for ch in range(CHUNKS):
            @pl.when(t == ch)
            def _(ch=ch):
                wait_bytes(inb[ch], in_recv.at[ch])
                for v in range(BLOCKS):
                    ordered[v * ROWS:(v + 1) * ROWS, :] = inb[ch][holder[v]]

        @pl.when(t < CHUNKS)
        def _():
            source_terms(t)
            send_halos(t)

        @pl.when(t >= 1)
        def _():
            for copy in halo_copies(t - 1):
                copy.wait_recv()
            propagate(t - 1)
            send_back(t - 1)

        return 0

    lax.fori_loop(0, CHUNKS + 1, step, 0)

    wait_bytes(aux_in.at[0:SOURCES - 1], aux_send)
    for ch in range(CHUNKS):
        wait_bytes(inb[ch].at[0:SOURCES - 1], in_send.at[ch])
        wait_bytes(outb.at[ch, 0:SOURCES - 1], out_send.at[ch])

    def drain(n, _):
        for copy in halo_copies(n):
            copy.wait_send()
        return 0

    lax.fori_loop(0, CHUNKS, drain, 0)
    wait_bytes(out, out_recv)


def finish(slots, moved, out, zeros, sems):
    first = (lax.axis_index("comp") * REGIONS + lax.axis_index("lon")) * SLOTS
    zeros[...] = jnp.zeros_like(zeros)
    for k in range(SLOTS):
        held = slots[first + k] >= 0

        @pl.when(held)
        def _(k=k):
            pltpu.make_async_copy(moved.at[k], out.at[k], sems.at[k]).start()

        @pl.when(jnp.logical_not(held))
        def _(k=k):
            pltpu.make_async_copy(zeros, out.at[k], sems.at[k]).start()

    for k in range(SLOTS):
        wait_bytes(out.at[k], sems.at[k])


def per_device(spectra, wind_vectors, slot_block, wet_mask, depth_class):
    hbm = pl.BlockSpec(memory_space=pltpu.HBM)
    vmem = pl.BlockSpec(memory_space=pltpu.VMEM)
    f32 = jnp.float32
    dma = pltpu.SemaphoreType.DMA
    scratch = [
        pltpu.VMEM((SLOTS, COMPS, POINTS), f32),
        pltpu.VMEM((SLOTS, 2, POINTS), f32),
        pltpu.SMEM((GROUPS * REGIONS * SLOTS,), jnp.int32),
        pltpu.VMEM((GRID_LON, 2 * POINTS), jnp.int32),
        pltpu.VMEM((2, GRID_LON), jnp.int32),
        pltpu.SMEM((T_SIZE,), f32),
        pltpu.VMEM((2, 8, POINTS), f32),
        pltpu.VMEM((SLOTS, 8, POINTS), f32),
        pltpu.VMEM((SOURCES, 8, POINTS), f32),
        pltpu.VMEM((3, 8, POINTS), f32),
        pltpu.VMEM((2, 32, POINTS), f32),
        pltpu.VMEM((32, POINTS), f32),
        pltpu.VMEM((GROUP_FREQS, 4, 6, 8, POINTS), f32),
        pltpu.VMEM((BLOCKS * ROWS, POINTS), f32),
        pltpu.VMEM((GROUP_FREQS, DIRS, 8, POINTS), f32),
        pltpu.VMEM((GROUP_FREQS, DIRS, 8, POINTS), f32),
        pltpu.VMEM((GROUP_FREQS, DIRS, 8, POINTS), f32),
        pltpu.VMEM((3, DIRS, 8, POINTS), f32),
        pltpu.VMEM((2, DIRS, 8, POINTS), f32),
        pltpu.VMEM((2, DIRS, 8, POINTS), f32),
        pltpu.VMEM((BLOCKS * ROWS, POINTS), f32),
        pltpu.VMEM((BLOCKS, ROWS, POINTS), f32),
        pltpu.VMEM((CHUNKS, SOURCES, ROWS, POINTS), f32),
        dma((7,)),
        dma((CHUNKS,)),
        dma((CHUNKS,)),
        dma,
        dma,
        dma((2, CHUNKS)),
        dma((2, CHUNKS)),
        dma((CHUNKS,)),
        dma,
    ] + [pltpu.VMEM((SOURCES, ROWS, POINTS), f32) for _ in range(CHUNKS)]
    given = (spectra, wind_vectors, slot_block, wet_mask, depth_class.T, scalar_table(), latitude_table())
    moved = pl.pallas_call(
        kernel,
        out_shape=pltpu.VMEM((SLOTS, COMPS, POINTS), f32),
        in_specs=[hbm] * 7,
        out_specs=vmem,
        scratch_shapes=scratch,
        compiler_params=pltpu.CompilerParams(
            collective_id=0, has_side_effects=True, vmem_limit_bytes=40 * 1024 * 1024
        ),
        name="wave_step",
    )(*[pltpu.with_memory_space_constraint(jnp.asarray(array), pltpu.HBM) for array in given])
    return pl.pallas_call(
        finish,
        out_shape=jax.ShapeDtypeStruct((SLOTS, COMPS, POINTS), f32),
        in_specs=[pl.BlockSpec(memory_space=pltpu.SMEM), vmem],
        out_specs=hbm,
        scratch_shapes=[pltpu.VMEM((COMPS, POINTS), f32), dma((SLOTS,))],
        compiler_params=pltpu.CompilerParams(vmem_limit_bytes=8 * 1024 * 1024),
        name="finish",
    )(slot_block, pltpu.with_memory_space_constraint(moved, pltpu.VMEM))


def solution(mesh):
    return jax.shard_map(
        per_device,
        mesh=mesh,
        in_specs=(P(("comp", "lon"), None, None), P(("comp", "lon"), None, None), P(), P(), P()),
        out_specs=P(("comp", "lon"), None, None),
        check_vma=False,
    )
```

```python
import functools

import jax
import jax.numpy as jnp
import numpy as np
from jax import lax
from jax.experimental import pallas as pl
from jax.experimental.pallas import tpu as pltpu
from jax.sharding import PartitionSpec as P

MESH = pl.DeviceIdType.MESH

DIRS = 36
HALF = DIRS // 2
FREQS = 48
GROUPS = 4
REGIONS = 32
SLOTS = 3
SOURCES = GROUPS * SLOTS
POINTS = 128
NDEPTH = 8
NSUB = 4
BLOCKS = 8
GRID_LON = 128
REGION_LONS = GRID_LON // REGIONS
GROUP_FREQS = FREQS // GROUPS
COMPS = FREQS * DIRS
GROUP_COMPS = GROUP_FREQS * DIRS

CHUNK = 2
CHUNKS = GROUP_FREQS // CHUNK
ROWS = CHUNK * DIRS

GRAVITY = 9.81

ORDER = [(q + 27) % DIRS for q in range(DIRS)]
ANGLE = (np.arange(DIRS) + 0.5) * (2.0 * np.pi / DIRS)
COS = np.cos(ANGLE)
SIN = np.sin(ANGLE)
COS_FACE = 0.5 * (COS + np.roll(COS, -1))
SIN_FACE = 0.5 * (SIN + np.roll(SIN, -1))

T_SPEED = 0
T_ALONG = T_SPEED + NDEPTH * FREQS
T_GAIN = T_ALONG + FREQS
T_SQUARE = T_GAIN + FREQS
T_WEIGHT = T_SQUARE + FREQS
T_WEIGHT_FREQ = T_WEIGHT + FREQS
T_SIZE = 640
LAG = 2
WINDOW = 3

WEST, MID, EAST, BESIDE = range(4)


def scalar_table():
    sigma = 2.0 * np.pi * 0.0418 * 1.07 ** np.arange(FREQS, dtype=np.float64)
    depth = 8.0 * 2.0 ** np.arange(NDEPTH, dtype=np.float64)
    deep = sigma * sigma / GRAVITY
    number = deep[None, :] / np.sqrt(np.tanh(deep[None, :] * depth[:, None]))
    twice = 2.0 * number * depth[:, None]
    factor = 2.0 * twice * np.exp(-twice) / (1.0 - np.exp(-2.0 * twice))
    speed = 0.5 * sigma[None, :] / number * (1.0 + factor)
    speed = speed / speed.max()
    weight = sigma / (sigma.sum() * DIRS)
    table = np.zeros(T_SIZE, np.float64)
    table[T_SPEED:T_ALONG] = speed.reshape(-1)
    table[T_ALONG:T_GAIN] = sigma / GRAVITY
    table[T_GAIN:T_SQUARE] = 0.5 * sigma / sigma[-1]
    table[T_SQUARE:T_WEIGHT] = sigma * sigma
    table[T_WEIGHT:T_WEIGHT_FREQ] = weight
    table[T_WEIGHT_FREQ:T_WEIGHT_FREQ + FREQS] = weight * sigma
    return table.astype(np.float32)


def latitude_table():
    count = 2 * POINTS
    phi = (-60.0 + (np.arange(count) + 0.5) * 120.0 / count) * np.pi / 180.0
    rows = np.concatenate([0.5 * 0.45 / np.cos(phi), 0.3 * np.tan(phi)])
    parts = rows.reshape(2, 1, 2, POINTS)
    return np.broadcast_to(parts, (2, REGION_LONS, 2, POINTS)).reshape(2, 8, POINTS).astype(np.float32)


def wait_bytes(ref, sem):
    pltpu.make_async_copy(ref, ref, sem).wait()


def kernel(
    x, wind, slots, wet, depth, table, lat, out,
    xv, windv, slot_s, wetv, depthv, table_s, latv,
    aux_out, aux_in, scal, cells, speeds, coef, ordered, field, halo_w, halo_e, one_on, two_on, three_on, back, blocks, outb,
    local_sem, in_send, in_recv, aux_send, aux_recv, halo_send, halo_recv, out_send, out_recv,
    *inb,
):
    me_c = lax.axis_index("comp")
    me_r = lax.axis_index("lon")

    def region(shift):
        return lax.rem(me_r + (shift + REGIONS), REGIONS)

    loads = [
        pltpu.make_async_copy(src, dst, local_sem.at[n])
        for n, (src, dst) in enumerate(
            ((x, xv), (wind, windv), (slots, slot_s), (wet, wetv), (depth, depthv), (table, table_s), (lat, latv))
        )
    ]
    for load in loads:
        load.start()

    barrier = pltpu.get_barrier_semaphore()
    for dg in range(GROUPS):
        for dr in (-1, 0, 1):
            if dg or dr:
                pl.semaphore_signal(
                    barrier, inc=1, device_id=(lax.rem(me_c + dg, GROUPS), region(dr)), device_id_type=MESH
                )
    pl.semaphore_wait(barrier, SOURCES - 1)

    def send_in(ch):
        for dg in (2, 1, 3, 0):
            to = lax.rem(me_c + dg, GROUPS)
            for k in range(SLOTS):
                src = x.at[k, pl.ds(to * GROUP_COMPS + ch * ROWS, ROWS)]
                dst = inb[ch].at[me_c * SLOTS + k]
                if dg == 0 and k == 1:
                    pltpu.make_async_copy(src, dst, in_recv.at[ch]).start()
                else:
                    pltpu.make_async_remote_copy(
                        src, dst, in_send.at[ch], in_recv.at[ch], device_id=(to, region(k - 1)), device_id_type=MESH
                    ).start()

    for ch in range(min(WINDOW, CHUNKS)):
        send_in(ch)

    row = lax.broadcasted_iota(jnp.int32, (8, POINTS), 0)
    lane = lax.broadcasted_iota(jnp.int32, (8, POINTS), 1)

    for load in loads:
        load.wait()
    upper = row < 4
    for k in range(SLOTS):
        def pair(p, sums, k=k):
            total, moment = sums
            tiles = [xv[k, pl.ds(pl.multiple_of(p * 72 + 8 * n, 8), 8), :] for n in range(9)]
            first = (tiles[0] + tiles[1]) + (tiles[2] + tiles[3]) + jnp.where(upper, tiles[4], 0.0)
            second = (tiles[5] + tiles[6]) + (tiles[7] + tiles[8]) + jnp.where(upper, 0.0, tiles[4])
            total = total + first * table_s[T_WEIGHT + 2 * p] + second * table_s[T_WEIGHT + 2 * p + 1]
            moment = moment + first * table_s[T_WEIGHT_FREQ + 2 * p] + second * table_s[T_WEIGHT_FREQ + 2 * p + 1]
            return total, moment

        zero = jnp.zeros((8, POINTS), jnp.float32)
        total, moment = lax.fori_loop(0, FREQS // 2, pair, (zero, zero))
        total = jnp.sum(total, axis=0, keepdims=True)
        moment = jnp.sum(moment, axis=0, keepdims=True)
        mean = moment / (total + 1e-6)
        aux_out[k] = zero
        aux_out[k, 0:2, :] = windv[k]
        aux_out[k, 2:3, :] = 0.3 * (total / (total + 1.0)) / (mean * mean)

    for dg in (2, 1, 3, 0):
        to = lax.rem(me_c + dg, GROUPS)
        for k in range(SLOTS):
            dst = aux_in.at[me_c * SLOTS + k]
            if dg == 0 and k == 1:
                pltpu.make_async_copy(aux_out.at[k], dst, aux_recv).start()
            else:
                pltpu.make_async_remote_copy(
                    aux_out.at[k], dst, aux_send, aux_recv, device_id=(to, region(k - 1)), device_id_type=MESH
                ).start()

    for n in range(16):
        lon = lax.rem(me_r * REGION_LONS + (n - 6 + GRID_LON), GRID_LON)
        levels = jnp.where(lane[0:2] == lon, depthv[...].astype(jnp.float32), 0.0)
        cells[0, 2 * n:2 * n + 2, :] = jnp.broadcast_to(jnp.sum(levels, axis=1, keepdims=True), (2, POINTS))
        rows = pl.ds(pl.multiple_of(lon // 8 * 8, 8), 8)
        here = row == lax.rem(lon, 8)
        for part in range(2):
            wet_rows = wetv[rows, part * POINTS:(part + 1) * POINTS].astype(jnp.float32)
            cells[1, 2 * n + part:2 * n + part + 1, :] = jnp.sum(
                jnp.where(here, wet_rows, 0.0), axis=0, keepdims=True
            )

    def from_lon(values, start):
        return values[2 * (start + 6):2 * (start + 6) + 8]

    def shift_down(value):
        rolled = pltpu.roll(value, 1, 1)
        return jnp.where(lane == 0, pltpu.roll(rolled, 1, 0), rolled)

    def shift_up(value):
        rolled = pltpu.roll(value, POINTS - 1, 1)
        return jnp.where(lane == POINTS - 1, pltpu.roll(rolled, 7, 0), rolled)

    last = (lax.rem(row, 2) == 1) & (lane == POINTS - 1)
    wets = cells.at[1]

    def prepare(i, _):
        for m in range(4):
            level = cells[0, 8 * m:8 * m + 8]
            speed = jnp.zeros((8, POINTS), jnp.float32)
            for d in range(NDEPTH):
                speed = jnp.where(level == float(d), table_s[T_SPEED + d * FREQS + me_c * GROUP_FREQS + i], speed)
            speeds[8 * m:8 * m + 8] = speed
        made = []
        for part, start in enumerate((-REGION_LONS, 0, REGION_LONS)):
            west, mid, east = (from_lon(speeds, start + n) for n in (-1, 0, 1))
            wet_west, wet_mid, wet_east = (from_lon(wets, start + n) for n in (-1, 0, 1))
            face = jnp.where(last, 0.0, 0.45 * (mid + shift_up(mid)) * wet_mid * shift_up(wet_mid))
            made.append((
                latv[0] * (mid + east) * wet_mid * wet_east,
                latv[0] * (mid + west) * wet_mid * wet_west,
                face,
                shift_down(face),
                latv[1] * mid,
                0.4 * (east - west),
            ))
        for n in range(6):
            for part in range(3):
                coef[i, part, n] = made[part][n]
            coef[i, BESIDE, n] = jnp.where(row < 4, made[EAST][n], made[WEST][n])
        return 0

    lax.fori_loop(0, GROUP_FREQS, prepare, 0)

    held = []
    for s in range(SOURCES):
        held.append(slot_s[((s // SLOTS) * REGIONS + region(1 - s % SLOTS)) * SLOTS + s % SLOTS])
    holder = []
    for v in range(BLOCKS):
        found = jnp.int32(0)
        for s in range(SOURCES):
            found = jnp.where(held[s] == v, jnp.int32(s), found)
        holder.append(found)
    back_row = [jnp.maximum(h, 0) for h in held]
    kept = [jnp.where(h >= 0, jnp.float32(1.0), jnp.float32(0.0)) for h in held]

    wait_bytes(aux_in, aux_recv)
    for v in range(BLOCKS):
        for n in range(3):
            scal[n, v:v + 1, :] = aux_in[holder[v]][n:n + 1, :]

    def halo_copies(ch):
        freqs = pl.ds(ch * CHUNK, CHUNK)
        return [
            pltpu.make_async_remote_copy(
                field.at[freqs], halo.at[freqs], halo_send.at[n, ch], halo_recv.at[n, ch],
                device_id=(me_c, region(shift)), device_id_type=MESH,
            )
            for n, (halo, shift) in enumerate(((halo_w, 1), (halo_e, -1)))
        ]

    def send_halos(ch):
        for copy in halo_copies(ch):
            copy.start()

    def source_terms(ch):
        wind_x, wind_y, damp = scal[0], scal[1], scal[2]
        for n in range(CHUNK):
            i = ch * CHUNK + n
            f = me_c * GROUP_FREQS + i
            along = table_s[T_ALONG + f]
            gain = table_s[T_GAIN + f]
            scale = 1.0 / (1.0 + damp * table_s[T_SQUARE + f])
            for q in range(DIRS):
                j = ORDER[q]
                energy = ordered[pl.ds(n * DIRS + j, 8, stride=ROWS), :]
                ratio = jnp.maximum((wind_x * float(COS[j]) + wind_y * float(SIN[j])) * along, 1.0)
                field[i, q] = energy * ((1.0 + gain) - gain / ratio) * scale

    def along_lon(q, parts, coefs, ring):
        turn = 2 if q < HALF else 6
        rolled = [pltpu.roll(part, turn, 0) for part in parts]
        edge = row < 2 if q < HALF else row >= 6
        moved = []
        for n, part in enumerate(parts):
            other = n - 1 if q < HALF else n + 1
            if ring:
                beside = jnp.where(edge, rolled[other % len(parts)], rolled[n])
            elif 0 <= other < len(parts):
                beside = jnp.where(edge, rolled[other], rolled[n])
            else:
                beside = rolled[n]
            from_west, from_east = (beside, part) if q < HALF else (part, beside)
            flux = coefs[n][0] * from_east - coefs[n][1] * from_west
            moved.append(part - float(COS[ORDER[q]]) * flux)
        return moved

    def along_lat(q, energy, coefs):
        sine = float(SIN[ORDER[q]])
        if sine > 0:
            share = coefs[2] * energy
            flux = share - shift_down(share)
        else:
            share = coefs[3] * energy
            flux = shift_up(share) - share
        return energy - sine * flux

    def refracted(moved, coefs, store):
        first = moved(0)
        here = first
        opening = before = None
        for q in range(DIRS):
            following = moved(q + 1) if q + 1 < DIRS else first
            j = ORDER[q]
            fluxes = []
            for n, part in enumerate(here):
                rate = coefs[n][4] * float(COS_FACE[j]) + coefs[n][5] * float(SIN_FACE[j])
                fluxes.append(rate * jnp.where(rate > 0.0, part, following[n]))
            if q == 0:
                opening = fluxes
            else:
                for n, part in enumerate(here):
                    store(q, n, part - (fluxes[n] - before[n]))
            before = fluxes
            here = following
        for n, part in enumerate(first):
            store(0, n, part - (opening[n] - before[n]))

    def propagate(ch):
        def one(n, _):
            i = ch * CHUNK + n
            west, mid, east, beside = ([coef[i, part, m] for m in range(6)] for part in range(4))
            wet_here = from_lon(wets, 0)
            wide = (west, mid, east)
            narrow = (mid, beside)

            def first_step(q):
                parts = along_lon(q, (halo_w[i, q], field[i, q], halo_e[i, q]), wide, False)
                return [along_lat(q, part, c) for part, c in zip(parts, wide)]

            def second_step(q):
                parts = along_lon(q, [one_on[part, q] for part in range(3)], wide, False)
                parts = (parts[MID], jnp.where(row < 4, parts[EAST], parts[WEST]))
                return [along_lat(q, part, c) for part, c in zip(parts, narrow)]

            def third_step(q):
                parts = along_lon(q, (two_on[0, q], two_on[1, q]), narrow, True)
                return [along_lat(q, part, c) for part, c in zip(parts, narrow)]

            def fourth_step(q):
                parts = along_lon(q, (three_on[0, q], three_on[1, q]), narrow, True)
                return [along_lat(q, parts[0], mid)]

            def to(buffer):
                def store(q, part, energy):
                    buffer[part, q] = energy
                return store

            def to_back(q, part, energy):
                back[pl.ds(n * DIRS + ORDER[q], 8, stride=ROWS), :] = energy * wet_here

            refracted(first_step, wide, to(one_on))
            refracted(second_step, narrow, to(two_on))
            refracted(third_step, narrow, to(three_on))
            refracted(fourth_step, (mid,), to_back)
            return 0

        lax.fori_loop(0, CHUNK, one, 0)

    def send_back(ch):
        for v in range(BLOCKS):
            blocks[v] = back[v * ROWS:(v + 1) * ROWS, :]
        for s in range(SOURCES):
            outb[ch, s] = blocks[back_row[s]] * kept[s]
        for dg in (2, 1, 3, 0):
            to = lax.rem(me_c + dg, GROUPS)
            for k in range(SLOTS):
                src = outb.at[ch, to * SLOTS + k]
                dst = out.at[k, pl.ds(me_c * GROUP_COMPS + ch * ROWS, ROWS)]
                if dg == 0 and k == 1:
                    pltpu.make_async_copy(src, dst, out_recv).start()
                else:
                    pltpu.make_async_remote_copy(
                        src, dst, out_send.at[ch], out_recv, device_id=(to, region(1 - k)), device_id_type=MESH
                    ).start()

    def step(t, _):
        for ch in range(CHUNKS):
            @pl.when(t == ch)
            def _(ch=ch):
                wait_bytes(inb[ch], in_recv.at[ch])
                if ch + WINDOW < CHUNKS:
                    wait_bytes(inb[ch].at[0:SOURCES - 1], in_send.at[ch])
                    send_in(ch + WINDOW)
                for v in range(BLOCKS):
                    ordered[v * ROWS:(v + 1) * ROWS, :] = inb[ch][holder[v]]

        @pl.when(t < CHUNKS)
        def _():
            source_terms(t)
            send_halos(t)

        @pl.when(t >= LAG)
        def _():
            for copy in halo_copies(t - LAG):
                copy.wait_recv()
            propagate(t - LAG)
            send_back(t - LAG)

        return 0

    lax.fori_loop(0, CHUNKS + LAG, step, 0)

    wait_bytes(aux_in.at[0:SOURCES - 1], aux_send)
    for ch in range(CHUNKS):
        if ch + WINDOW >= CHUNKS:
            wait_bytes(inb[ch].at[0:SOURCES - 1], in_send.at[ch])
        wait_bytes(outb.at[ch, 0:SOURCES - 1], out_send.at[ch])

    def drain(n, _):
        for copy in halo_copies(n):
            copy.wait_send()
        return 0

    lax.fori_loop(0, CHUNKS, drain, 0)
    wait_bytes(out, out_recv)


def finish(moved, out, sems):
    copies = [pltpu.make_async_copy(moved.at[k], out.at[k], sems.at[k]) for k in range(SLOTS)]
    for copy in copies:
        copy.start()
    for copy in copies:
        copy.wait()


def per_device(spectra, wind_vectors, slot_block, wet_mask, depth_class):
    hbm = pl.BlockSpec(memory_space=pltpu.HBM)
    vmem = pl.BlockSpec(memory_space=pltpu.VMEM)
    f32 = jnp.float32
    dma = pltpu.SemaphoreType.DMA
    scratch = [
        pltpu.VMEM((SLOTS, COMPS, POINTS), f32),
        pltpu.VMEM((SLOTS, 2, POINTS), f32),
        pltpu.SMEM((GROUPS * REGIONS * SLOTS,), jnp.int32),
        pltpu.VMEM((GRID_LON, 2 * POINTS), jnp.int32),
        pltpu.VMEM((2, GRID_LON), jnp.int32),
        pltpu.SMEM((T_SIZE,), f32),
        pltpu.VMEM((2, 8, POINTS), f32),
        pltpu.VMEM((SLOTS, 8, POINTS), f32),
        pltpu.VMEM((SOURCES, 8, POINTS), f32),
        pltpu.VMEM((3, 8, POINTS), f32),
        pltpu.VMEM((2, 32, POINTS), f32),
        pltpu.VMEM((32, POINTS), f32),
        pltpu.VMEM((GROUP_FREQS, 4, 6, 8, POINTS), f32),
        pltpu.VMEM((BLOCKS * ROWS, POINTS), f32),
        pltpu.VMEM((GROUP_FREQS, DIRS, 8, POINTS), f32),
        pltpu.VMEM((GROUP_FREQS, DIRS, 8, POINTS), f32),
        pltpu.VMEM((GROUP_FREQS, DIRS, 8, POINTS), f32),
        pltpu.VMEM((3, DIRS, 8, POINTS), f32),
        pltpu.VMEM((2, DIRS, 8, POINTS), f32),
        pltpu.VMEM((2, DIRS, 8, POINTS), f32),
        pltpu.VMEM((BLOCKS * ROWS, POINTS), f32),
        pltpu.VMEM((BLOCKS, ROWS, POINTS), f32),
        pltpu.VMEM((CHUNKS, SOURCES, ROWS, POINTS), f32),
        dma((7,)),
        dma((CHUNKS,)),
        dma((CHUNKS,)),
        dma,
        dma,
        dma((2, CHUNKS)),
        dma((2, CHUNKS)),
        dma((CHUNKS,)),
        dma,
    ] + [pltpu.VMEM((SOURCES, ROWS, POINTS), f32) for _ in range(CHUNKS)]
    given = (spectra, wind_vectors, slot_block, wet_mask, depth_class.T, scalar_table(), latitude_table())
    moved = pl.pallas_call(
        kernel,
        out_shape=pltpu.VMEM((SLOTS, COMPS, POINTS), f32),
        in_specs=[hbm] * 7,
        out_specs=vmem,
        scratch_shapes=scratch,
        compiler_params=pltpu.CompilerParams(
            collective_id=0, has_side_effects=True, vmem_limit_bytes=40 * 1024 * 1024
        ),
        name="wave_step",
    )(*[pltpu.with_memory_space_constraint(jnp.asarray(array), pltpu.HBM) for array in given])
    return pl.pallas_call(
        finish,
        out_shape=jax.ShapeDtypeStruct((SLOTS, COMPS, POINTS), f32),
        in_specs=[vmem],
        out_specs=hbm,
        scratch_shapes=[dma((SLOTS,))],
        compiler_params=pltpu.CompilerParams(vmem_limit_bytes=8 * 1024 * 1024),
        name="finish",
    )(pltpu.with_memory_space_constraint(moved, pltpu.VMEM))


def solution(mesh):
    return jax.shard_map(
        per_device,
        mesh=mesh,
        in_specs=(P(("comp", "lon"), None, None), P(("comp", "lon"), None, None), P(), P(), P()),
        out_specs=P(("comp", "lon"), None, None),
        check_vma=False,
    )
```

```python
import functools

import jax
import jax.numpy as jnp
import numpy as np
from jax import lax
from jax.experimental import pallas as pl
from jax.experimental.pallas import tpu as pltpu
from jax.sharding import PartitionSpec as P

MESH = pl.DeviceIdType.MESH

DIRS = 36
HALF = DIRS // 2
FREQS = 48
GROUPS = 4
REGIONS = 32
SLOTS = 3
SOURCES = GROUPS * SLOTS
POINTS = 128
NDEPTH = 8
NSUB = 4
BLOCKS = 8
GRID_LON = 128
REGION_LONS = GRID_LON // REGIONS
GROUP_FREQS = FREQS // GROUPS
COMPS = FREQS * DIRS
GROUP_COMPS = GROUP_FREQS * DIRS

CHUNK = 2
CHUNKS = GROUP_FREQS // CHUNK
ROWS = CHUNK * DIRS

GRAVITY = 9.81

ORDER = [(q + 27) % DIRS for q in range(DIRS)]
ANGLE = (np.arange(DIRS) + 0.5) * (2.0 * np.pi / DIRS)
COS = np.cos(ANGLE)
SIN = np.sin(ANGLE)
COS_FACE = 0.5 * (COS + np.roll(COS, -1))
SIN_FACE = 0.5 * (SIN + np.roll(SIN, -1))

T_SPEED = 0
T_ALONG = T_SPEED + NDEPTH * FREQS
T_GAIN = T_ALONG + FREQS
T_SQUARE = T_GAIN + FREQS
T_WEIGHT = T_SQUARE + FREQS
T_WEIGHT_FREQ = T_WEIGHT + FREQS
T_SIZE = 640
LAG = 2
WINDOW = 3

WEST, MID, EAST, BESIDE = range(4)


def scalar_table():
    sigma = 2.0 * np.pi * 0.0418 * 1.07 ** np.arange(FREQS, dtype=np.float64)
    depth = 8.0 * 2.0 ** np.arange(NDEPTH, dtype=np.float64)
    deep = sigma * sigma / GRAVITY
    number = deep[None, :] / np.sqrt(np.tanh(deep[None, :] * depth[:, None]))
    twice = 2.0 * number * depth[:, None]
    factor = 2.0 * twice * np.exp(-twice) / (1.0 - np.exp(-2.0 * twice))
    speed = 0.5 * sigma[None, :] / number * (1.0 + factor)
    speed = speed / speed.max()
    weight = sigma / (sigma.sum() * DIRS)
    table = np.zeros(T_SIZE, np.float64)
    table[T_SPEED:T_ALONG] = speed.reshape(-1)
    table[T_ALONG:T_GAIN] = sigma / GRAVITY
    table[T_GAIN:T_SQUARE] = 0.5 * sigma / sigma[-1]
    table[T_SQUARE:T_WEIGHT] = sigma * sigma
    table[T_WEIGHT:T_WEIGHT_FREQ] = weight
    table[T_WEIGHT_FREQ:T_WEIGHT_FREQ + FREQS] = weight * sigma
    return table.astype(np.float32)


def latitude_table():
    count = 2 * POINTS
    phi = (-60.0 + (np.arange(count) + 0.5) * 120.0 / count) * np.pi / 180.0
    rows = np.concatenate([0.5 * 0.45 / np.cos(phi), 0.3 * np.tan(phi)])
    parts = rows.reshape(2, 1, 2, POINTS)
    return np.broadcast_to(parts, (2, REGION_LONS, 2, POINTS)).reshape(2, 8, POINTS).astype(np.float32)


def wait_bytes(ref, sem):
    pltpu.make_async_copy(ref, ref, sem).wait()


def kernel(
    x, wind, slots, wet, depth, table, lat, out,
    xv, windv, slot_s, wetv, depthv, table_s, latv,
    aux_out, aux_in, scal, cells, speeds, coef, ordered, field, halo_w, halo_e, one_on, two_on, three_on, back, blocks, outb,
    local_sem, in_send, in_recv, aux_send, aux_recv, halo_send, halo_recv, out_send, out_recv, ready,
    *inb,
):
    me_c = lax.axis_index("comp")
    me_r = lax.axis_index("lon")

    def region(shift):
        return lax.rem(me_r + (shift + REGIONS), REGIONS)

    def across(dg):
        return lax.rem(me_c + jnp.where(lax.rem(me_r, 2) == 0, dg, (GROUPS - dg) % GROUPS), GROUPS)

    loads = [
        pltpu.make_async_copy(src, dst, local_sem.at[n])
        for n, (src, dst) in enumerate(
            ((x, xv), (wind, windv), (slots, slot_s), (wet, wetv), (depth, depthv), (table, table_s), (lat, latv))
        )
    ]
    barrier = pltpu.get_barrier_semaphore()
    for dg in range(GROUPS):
        for dr in (-1, 0, 1):
            if (dg == 0) != (dr == 0):
                pl.semaphore_signal(
                    barrier, inc=1, device_id=(lax.rem(me_c + dg, GROUPS), region(dr)), device_id_type=MESH
                )
    for load in loads:
        load.start()
    pl.semaphore_wait(barrier, GROUPS + 1)

    def send_in(ch, slots=(0, 2, 1)):
        for k, dg in [(k, dg) for k in slots for dg in (1, 2, 3, 0)]:
            to = across(dg)
            if True:
                src = x.at[k, pl.ds(to * GROUP_COMPS + ch * ROWS, ROWS)]
                dst = inb[ch].at[me_c * SLOTS + k]
                if dg == 0 and k == 1:
                    pltpu.make_async_copy(src, dst, in_recv.at[ch]).start()
                else:
                    pltpu.make_async_remote_copy(
                        src, dst, in_send.at[ch], in_recv.at[ch], device_id=(to, region(k - 1)), device_id_type=MESH
                    ).start()

    for dg in range(1, GROUPS):
        pl.semaphore_signal(ready, inc=1, device_id=(lax.rem(me_c + dg, GROUPS), me_r), device_id_type=MESH)
    for ch in range(min(WINDOW, CHUNKS)):
        send_in(ch, (1,))
    pl.semaphore_wait(ready, GROUPS - 1)
    for ch in range(min(WINDOW, CHUNKS)):
        send_in(ch, (0, 2))

    row = lax.broadcasted_iota(jnp.int32, (8, POINTS), 0)
    lane = lax.broadcasted_iota(jnp.int32, (8, POINTS), 1)

    for load in loads:
        load.wait()
    upper = row < 4
    for k in range(SLOTS):
        def pair(p, sums, k=k):
            total, moment = sums
            tiles = [xv[k, pl.ds(pl.multiple_of(p * 72 + 8 * n, 8), 8), :] for n in range(9)]
            first = (tiles[0] + tiles[1]) + (tiles[2] + tiles[3]) + jnp.where(upper, tiles[4], 0.0)
            second = (tiles[5] + tiles[6]) + (tiles[7] + tiles[8]) + jnp.where(upper, 0.0, tiles[4])
            total = total + first * table_s[T_WEIGHT + 2 * p] + second * table_s[T_WEIGHT + 2 * p + 1]
            moment = moment + first * table_s[T_WEIGHT_FREQ + 2 * p] + second * table_s[T_WEIGHT_FREQ + 2 * p + 1]
            return total, moment

        zero = jnp.zeros((8, POINTS), jnp.float32)
        total, moment = lax.fori_loop(0, FREQS // 2, pair, (zero, zero))
        total = jnp.sum(total, axis=0, keepdims=True)
        moment = jnp.sum(moment, axis=0, keepdims=True)
        mean = moment / (total + 1e-6)
        aux_out[k] = zero
        aux_out[k, 0:2, :] = windv[k]
        aux_out[k, 2:3, :] = 0.3 * (total / (total + 1.0)) / (mean * mean)

    for dg in (2, 1, 3, 0):
        to = lax.rem(me_c + dg, GROUPS)
        for k in range(SLOTS):
            dst = aux_in.at[me_c * SLOTS + k]
            if dg == 0 and k == 1:
                pltpu.make_async_copy(aux_out.at[k], dst, aux_recv).start()
            else:
                pltpu.make_async_remote_copy(
                    aux_out.at[k], dst, aux_send, aux_recv, device_id=(to, region(k - 1)), device_id_type=MESH
                ).start()

    for n in range(16):
        lon = lax.rem(me_r * REGION_LONS + (n - 6 + GRID_LON), GRID_LON)
        levels = jnp.where(lane[0:2] == lon, depthv[...].astype(jnp.float32), 0.0)
        cells[0, 2 * n:2 * n + 2, :] = jnp.broadcast_to(jnp.sum(levels, axis=1, keepdims=True), (2, POINTS))
        rows = pl.ds(pl.multiple_of(lon // 8 * 8, 8), 8)
        here = row == lax.rem(lon, 8)
        for part in range(2):
            wet_rows = wetv[rows, part * POINTS:(part + 1) * POINTS].astype(jnp.float32)
            cells[1, 2 * n + part:2 * n + part + 1, :] = jnp.sum(
                jnp.where(here, wet_rows, 0.0), axis=0, keepdims=True
            )

    def from_lon(values, start):
        return values[2 * (start + 6):2 * (start + 6) + 8]

    def shift_down(value):
        rolled = pltpu.roll(value, 1, 1)
        return jnp.where(lane == 0, pltpu.roll(rolled, 1, 0), rolled)

    def shift_up(value):
        rolled = pltpu.roll(value, POINTS - 1, 1)
        return jnp.where(lane == POINTS - 1, pltpu.roll(rolled, 7, 0), rolled)

    last = (lax.rem(row, 2) == 1) & (lane == POINTS - 1)
    wets = cells.at[1]

    def prepare(i, _):
        for m in range(4):
            level = cells[0, 8 * m:8 * m + 8]
            speed = jnp.zeros((8, POINTS), jnp.float32)
            for d in range(NDEPTH):
                speed = jnp.where(level == float(d), table_s[T_SPEED + d * FREQS + me_c * GROUP_FREQS + i], speed)
            speeds[8 * m:8 * m + 8] = speed
        made = []
        for part, start in enumerate((-REGION_LONS, 0, REGION_LONS)):
            west, mid, east = (from_lon(speeds, start + n) for n in (-1, 0, 1))
            wet_west, wet_mid, wet_east = (from_lon(wets, start + n) for n in (-1, 0, 1))
            face = jnp.where(last, 0.0, 0.45 * (mid + shift_up(mid)) * wet_mid * shift_up(wet_mid))
            made.append((
                latv[0] * (mid + east) * wet_mid * wet_east,
                latv[0] * (mid + west) * wet_mid * wet_west,
                face,
                shift_down(face),
                latv[1] * mid,
                0.4 * (east - west),
            ))
        for n in range(6):
            for part in range(3):
                coef[i, part, n] = made[part][n]
            coef[i, BESIDE, n] = jnp.where(row < 4, made[EAST][n], made[WEST][n])
        return 0

    lax.fori_loop(0, GROUP_FREQS, prepare, 0)

    held = []
    for s in range(SOURCES):
        held.append(slot_s[((s // SLOTS) * REGIONS + region(1 - s % SLOTS)) * SLOTS + s % SLOTS])
    holder = []
    for v in range(BLOCKS):
        found = jnp.int32(0)
        for s in range(SOURCES):
            found = jnp.where(held[s] == v, jnp.int32(s), found)
        holder.append(found)
    back_row = [jnp.maximum(h, 0) for h in held]
    kept = [jnp.where(h >= 0, jnp.float32(1.0), jnp.float32(0.0)) for h in held]

    wait_bytes(aux_in, aux_recv)
    for v in range(BLOCKS):
        for n in range(3):
            scal[n, v:v + 1, :] = aux_in[holder[v]][n:n + 1, :]

    def halo_copies(ch):
        freqs = pl.ds(ch * CHUNK, CHUNK)
        return [
            pltpu.make_async_remote_copy(
                field.at[freqs], halo.at[freqs], halo_send.at[n, ch], halo_recv.at[n, ch],
                device_id=(me_c, region(shift)), device_id_type=MESH,
            )
            for n, (halo, shift) in enumerate(((halo_w, 1), (halo_e, -1)))
        ]

    def send_halos(ch):
        for copy in halo_copies(ch):
            copy.start()

    def source_terms(ch):
        wind_x, wind_y, damp = scal[0], scal[1], scal[2]
        for n in range(CHUNK):
            i = ch * CHUNK + n
            f = me_c * GROUP_FREQS + i
            along = table_s[T_ALONG + f]
            gain = table_s[T_GAIN + f]
            scale = 1.0 / (1.0 + damp * table_s[T_SQUARE + f])
            for q in range(DIRS):
                j = ORDER[q]
                energy = ordered[pl.ds(n * DIRS + j, 8, stride=ROWS), :]
                ratio = jnp.maximum((wind_x * float(COS[j]) + wind_y * float(SIN[j])) * along, 1.0)
                field[i, q] = energy * ((1.0 + gain) - gain / ratio) * scale

    def along_lon(q, parts, coefs, ring):
        turn = 2 if q < HALF else 6
        rolled = [pltpu.roll(part, turn, 0) for part in parts]
        edge = row < 2 if q < HALF else row >= 6
        moved = []
        for n, part in enumerate(parts):
            other = n - 1 if q < HALF else n + 1
            if ring:
                beside = jnp.where(edge, rolled[other % len(parts)], rolled[n])
            elif 0 <= other < len(parts):
                beside = jnp.where(edge, rolled[other], rolled[n])
            else:
                beside = rolled[n]
            from_west, from_east = (beside, part) if q < HALF else (part, beside)
            flux = coefs[n][0] * from_east - coefs[n][1] * from_west
            moved.append(part - float(COS[ORDER[q]]) * flux)
        return moved

    def along_lat(q, energy, coefs):
        sine = float(SIN[ORDER[q]])
        if sine > 0:
            share = coefs[2] * energy
            flux = share - shift_down(share)
        else:
            share = coefs[3] * energy
            flux = shift_up(share) - share
        return energy - sine * flux

    def refracted(moved, coefs, store):
        first = moved(0)
        here = first
        opening = before = None
        for q in range(DIRS):
            following = moved(q + 1) if q + 1 < DIRS else first
            j = ORDER[q]
            fluxes = []
            for n, part in enumerate(here):
                rate = coefs[n][4] * float(COS_FACE[j]) + coefs[n][5] * float(SIN_FACE[j])
                fluxes.append(rate * jnp.where(rate > 0.0, part, following[n]))
            if q == 0:
                opening = fluxes
            else:
                for n, part in enumerate(here):
                    store(q, n, part - (fluxes[n] - before[n]))
            before = fluxes
            here = following
        for n, part in enumerate(first):
            store(0, n, part - (opening[n] - before[n]))

    def propagate(ch):
        def one(n, _):
            i = ch * CHUNK + n
            west, mid, east, beside = ([coef[i, part, m] for m in range(6)] for part in range(4))
            wet_here = from_lon(wets, 0)
            wide = (west, mid, east)
            narrow = (mid, beside)

            def first_step(q):
                parts = along_lon(q, (halo_w[i, q], field[i, q], halo_e[i, q]), wide, False)
                return [along_lat(q, part, c) for part, c in zip(parts, wide)]

            def second_step(q):
                parts = along_lon(q, [one_on[part, q] for part in range(3)], wide, False)
                parts = (parts[MID], jnp.where(row < 4, parts[EAST], parts[WEST]))
                return [along_lat(q, part, c) for part, c in zip(parts, narrow)]

            def third_step(q):
                parts = along_lon(q, (two_on[0, q], two_on[1, q]), narrow, True)
                return [along_lat(q, part, c) for part, c in zip(parts, narrow)]

            def fourth_step(q):
                parts = along_lon(q, (three_on[0, q], three_on[1, q]), narrow, True)
                return [along_lat(q, parts[0], mid)]

            def to(buffer):
                def store(q, part, energy):
                    buffer[part, q] = energy
                return store

            def to_back(q, part, energy):
                back[pl.ds(n * DIRS + ORDER[q], 8, stride=ROWS), :] = energy * wet_here

            refracted(first_step, wide, to(one_on))
            refracted(second_step, narrow, to(two_on))
            refracted(third_step, narrow, to(three_on))
            refracted(fourth_step, (mid,), to_back)
            return 0

        lax.fori_loop(0, CHUNK, one, 0)

    def send_back(ch):
        for v in range(BLOCKS):
            blocks[v] = back[v * ROWS:(v + 1) * ROWS, :]
        for s in range(SOURCES):
            outb[ch, s] = blocks[back_row[s]] * kept[s]
        for k, dg in [(k, dg) for k in (0, 2, 1) for dg in (1, 2, 3, 0)]:
            to = across(dg)
            if True:
                src = outb.at[ch, to * SLOTS + k]
                dst = out.at[k, pl.ds(me_c * GROUP_COMPS + ch * ROWS, ROWS)]
                if dg == 0 and k == 1:
                    pltpu.make_async_copy(src, dst, out_recv).start()
                else:
                    pltpu.make_async_remote_copy(
                        src, dst, out_send.at[ch], out_recv, device_id=(to, region(1 - k)), device_id_type=MESH
                    ).start()

    def step(t, _):
        for ch in range(CHUNKS):
            @pl.when(t == ch)
            def _(ch=ch):
                if ch + WINDOW < CHUNKS:
                    wait_bytes(inb[ch].at[0:SOURCES - 1], in_send.at[ch])
                    send_in(ch + WINDOW)
                wait_bytes(inb[ch], in_recv.at[ch])
                for v in range(BLOCKS):
                    ordered[v * ROWS:(v + 1) * ROWS, :] = inb[ch][holder[v]]

        @pl.when(t < CHUNKS)
        def _():
            source_terms(t)
            send_halos(t)

        @pl.when(t >= LAG)
        def _():
            for copy in halo_copies(t - LAG):
                copy.wait_recv()
            propagate(t - LAG)
            send_back(t - LAG)

        return 0

    lax.fori_loop(0, CHUNKS + LAG, step, 0)

    wait_bytes(aux_in.at[0:SOURCES - 1], aux_send)
    for ch in range(CHUNKS):
        if ch + WINDOW >= CHUNKS:
            wait_bytes(inb[ch].at[0:SOURCES - 1], in_send.at[ch])
        wait_bytes(outb.at[ch, 0:SOURCES - 1], out_send.at[ch])

    def drain(n, _):
        for copy in halo_copies(n):
            copy.wait_send()
        return 0

    lax.fori_loop(0, CHUNKS, drain, 0)
    wait_bytes(out, out_recv)


def finish(moved, out, sems):
    copies = [pltpu.make_async_copy(moved.at[k], out.at[k], sems.at[k]) for k in range(SLOTS)]
    for copy in copies:
        copy.start()
    for copy in copies:
        copy.wait()


def per_device(spectra, wind_vectors, slot_block, wet_mask, depth_class):
    hbm = pl.BlockSpec(memory_space=pltpu.HBM)
    vmem = pl.BlockSpec(memory_space=pltpu.VMEM)
    f32 = jnp.float32
    dma = pltpu.SemaphoreType.DMA
    scratch = [
        pltpu.VMEM((SLOTS, COMPS, POINTS), f32),
        pltpu.VMEM((SLOTS, 2, POINTS), f32),
        pltpu.SMEM((GROUPS * REGIONS * SLOTS,), jnp.int32),
        pltpu.VMEM((GRID_LON, 2 * POINTS), jnp.int32),
        pltpu.VMEM((2, GRID_LON), jnp.int32),
        pltpu.SMEM((T_SIZE,), f32),
        pltpu.VMEM((2, 8, POINTS), f32),
        pltpu.VMEM((SLOTS, 8, POINTS), f32),
        pltpu.VMEM((SOURCES, 8, POINTS), f32),
        pltpu.VMEM((3, 8, POINTS), f32),
        pltpu.VMEM((2, 32, POINTS), f32),
        pltpu.VMEM((32, POINTS), f32),
        pltpu.VMEM((GROUP_FREQS, 4, 6, 8, POINTS), f32),
        pltpu.VMEM((BLOCKS * ROWS, POINTS), f32),
        pltpu.VMEM((GROUP_FREQS, DIRS, 8, POINTS), f32),
        pltpu.VMEM((GROUP_FREQS, DIRS, 8, POINTS), f32),
        pltpu.VMEM((GROUP_FREQS, DIRS, 8, POINTS), f32),
        pltpu.VMEM((3, DIRS, 8, POINTS), f32),
        pltpu.VMEM((2, DIRS, 8, POINTS), f32),
        pltpu.VMEM((2, DIRS, 8, POINTS), f32),
        pltpu.VMEM((BLOCKS * ROWS, POINTS), f32),
        pltpu.VMEM((BLOCKS, ROWS, POINTS), f32),
        pltpu.VMEM((CHUNKS, SOURCES, ROWS, POINTS), f32),
        dma((7,)),
        dma((CHUNKS,)),
        dma((CHUNKS,)),
        dma,
        dma,
        dma((2, CHUNKS)),
        dma((2, CHUNKS)),
        dma((CHUNKS,)),
        dma,
        pltpu.SemaphoreType.REGULAR,
    ] + [pltpu.VMEM((SOURCES, ROWS, POINTS), f32) for _ in range(CHUNKS)]
    given = (spectra, wind_vectors, slot_block, wet_mask, depth_class.T, scalar_table(), latitude_table())
    moved = pl.pallas_call(
        kernel,
        out_shape=pltpu.VMEM((SLOTS, COMPS, POINTS), f32),
        in_specs=[hbm] * 7,
        out_specs=vmem,
        scratch_shapes=scratch,
        compiler_params=pltpu.CompilerParams(
            collective_id=0, has_side_effects=True, vmem_limit_bytes=40 * 1024 * 1024
        ),
        name="wave_step",
    )(*[pltpu.with_memory_space_constraint(jnp.asarray(array), pltpu.HBM) for array in given])
    return pl.pallas_call(
        finish,
        out_shape=jax.ShapeDtypeStruct((SLOTS, COMPS, POINTS), f32),
        in_specs=[vmem],
        out_specs=hbm,
        scratch_shapes=[dma((SLOTS,))],
        compiler_params=pltpu.CompilerParams(vmem_limit_bytes=8 * 1024 * 1024),
        name="finish",
    )(pltpu.with_memory_space_constraint(moved, pltpu.VMEM))


def solution(mesh):
    return jax.shard_map(
        per_device,
        mesh=mesh,
        in_specs=(P(("comp", "lon"), None, None), P(("comp", "lon"), None, None), P(), P(), P()),
        out_specs=P(("comp", "lon"), None, None),
        check_vma=False,
    )
```

```python
import functools

import jax
import jax.numpy as jnp
import numpy as np
from jax import lax
from jax.experimental import pallas as pl
from jax.experimental.pallas import tpu as pltpu
from jax.sharding import PartitionSpec as P

MESH = pl.DeviceIdType.MESH

DIRS = 36
HALF = DIRS // 2
FREQS = 48
GROUPS = 4
REGIONS = 32
SLOTS = 3
SOURCES = GROUPS * SLOTS
POINTS = 128
NDEPTH = 8
NSUB = 4
BLOCKS = 8
GRID_LON = 128
REGION_LONS = GRID_LON // REGIONS
GROUP_FREQS = FREQS // GROUPS
COMPS = FREQS * DIRS
GROUP_COMPS = GROUP_FREQS * DIRS

CHUNK = 2
CHUNKS = GROUP_FREQS // CHUNK
ROWS = CHUNK * DIRS

GRAVITY = 9.81

ORDER = [(q + 27) % DIRS for q in range(DIRS)]
ANGLE = (np.arange(DIRS) + 0.5) * (2.0 * np.pi / DIRS)
COS = np.cos(ANGLE)
SIN = np.sin(ANGLE)
COS_FACE = 0.5 * (COS + np.roll(COS, -1))
SIN_FACE = 0.5 * (SIN + np.roll(SIN, -1))

T_SPEED = 0
T_ALONG = T_SPEED + NDEPTH * FREQS
T_GAIN = T_ALONG + FREQS
T_SQUARE = T_GAIN + FREQS
T_WEIGHT = T_SQUARE + FREQS
T_WEIGHT_FREQ = T_WEIGHT + FREQS
T_SIZE = 640
LAG = 2
WINDOW = 3

WEST, MID, EAST, BESIDE = range(4)


def scalar_table():
    sigma = 2.0 * np.pi * 0.0418 * 1.07 ** np.arange(FREQS, dtype=np.float64)
    depth = 8.0 * 2.0 ** np.arange(NDEPTH, dtype=np.float64)
    deep = sigma * sigma / GRAVITY
    number = deep[None, :] / np.sqrt(np.tanh(deep[None, :] * depth[:, None]))
    twice = 2.0 * number * depth[:, None]
    factor = 2.0 * twice * np.exp(-twice) / (1.0 - np.exp(-2.0 * twice))
    speed = 0.5 * sigma[None, :] / number * (1.0 + factor)
    speed = speed / speed.max()
    weight = sigma / (sigma.sum() * DIRS)
    table = np.zeros(T_SIZE, np.float64)
    table[T_SPEED:T_ALONG] = speed.reshape(-1)
    table[T_ALONG:T_GAIN] = sigma / GRAVITY
    table[T_GAIN:T_SQUARE] = 0.5 * sigma / sigma[-1]
    table[T_SQUARE:T_WEIGHT] = sigma * sigma
    table[T_WEIGHT:T_WEIGHT_FREQ] = weight
    table[T_WEIGHT_FREQ:T_WEIGHT_FREQ + FREQS] = weight * sigma
    return table.astype(np.float32)


def latitude_table():
    count = 2 * POINTS
    phi = (-60.0 + (np.arange(count) + 0.5) * 120.0 / count) * np.pi / 180.0
    rows = np.concatenate([0.5 * 0.45 / np.cos(phi), 0.3 * np.tan(phi)])
    parts = rows.reshape(2, 1, 2, POINTS)
    return np.broadcast_to(parts, (2, REGION_LONS, 2, POINTS)).reshape(2, 8, POINTS).astype(np.float32)


def wait_bytes(ref, sem):
    pltpu.make_async_copy(ref, ref, sem).wait()


def kernel(
    x, wind, slots, wet, depth, table, lat, out,
    xv, windv, slot_s, wetv, depthv, table_s, latv,
    aux_out, aux_in, scal, cells, speeds, coef, ordered, field, halo_w, halo_e, one_on, two_on, three_on, back, blocks, outb,
    local_sem, in_send, in_recv, aux_send, aux_recv, halo_send, halo_recv, out_send, out_recv, ready,
    *inb,
):
    me_c = lax.axis_index("comp")
    me_r = lax.axis_index("lon")

    def region(shift):
        return lax.rem(me_r + (shift + REGIONS), REGIONS)

    def across(dg):
        return lax.rem(me_c + jnp.where(lax.rem(me_r, 2) == 0, dg, (GROUPS - dg) % GROUPS), GROUPS)

    loads = [
        pltpu.make_async_copy(src, dst, local_sem.at[n])
        for n, (src, dst) in enumerate(
            ((x, xv), (wind, windv), (slots, slot_s), (wet, wetv), (depth, depthv), (table, table_s), (lat, latv))
        )
    ]
    barrier = pltpu.get_barrier_semaphore()
    for dg in range(GROUPS):
        for dr in (-1, 0, 1):
            if (dg == 0) != (dr == 0):
                pl.semaphore_signal(
                    barrier, inc=1, device_id=(lax.rem(me_c + dg, GROUPS), region(dr)), device_id_type=MESH
                )
    for load in loads:
        load.start()
    pl.semaphore_wait(barrier, GROUPS + 1)

    def send_in(ch, slots=(0, 2, 1)):
        for k, dg in [(k, dg) for k in slots for dg in (1, 2, 3, 0)]:
            to = across(dg)
            if True:
                src = x.at[k, pl.ds(to * GROUP_COMPS + ch * ROWS, ROWS)]
                dst = inb[ch].at[me_c * SLOTS + k]
                if dg == 0 and k == 1:
                    pltpu.make_async_copy(src, dst, in_recv.at[ch]).start()
                else:
                    pltpu.make_async_remote_copy(
                        src, dst, in_send.at[ch], in_recv.at[ch], device_id=(to, region(k - 1)), device_id_type=MESH
                    ).start()

    for dg in range(1, GROUPS):
        pl.semaphore_signal(ready, inc=1, device_id=(lax.rem(me_c + dg, GROUPS), me_r), device_id_type=MESH)
    for ch in range(2):
        send_in(ch, (1,))
    pl.semaphore_wait(ready, GROUPS - 1)
    for ch in range(2):
        send_in(ch, (0, 2))
    for ch in range(2, 2):
        send_in(ch)

    row = lax.broadcasted_iota(jnp.int32, (8, POINTS), 0)
    lane = lax.broadcasted_iota(jnp.int32, (8, POINTS), 1)

    for load in loads:
        load.wait()
    upper = row < 4
    for k in range(SLOTS):
        def pair(p, sums, k=k):
            total, moment = sums
            tiles = [xv[k, pl.ds(pl.multiple_of(p * 72 + 8 * n, 8), 8), :] for n in range(9)]
            first = (tiles[0] + tiles[1]) + (tiles[2] + tiles[3]) + jnp.where(upper, tiles[4], 0.0)
            second = (tiles[5] + tiles[6]) + (tiles[7] + tiles[8]) + jnp.where(upper, 0.0, tiles[4])
            total = total + first * table_s[T_WEIGHT + 2 * p] + second * table_s[T_WEIGHT + 2 * p + 1]
            moment = moment + first * table_s[T_WEIGHT_FREQ + 2 * p] + second * table_s[T_WEIGHT_FREQ + 2 * p + 1]
            return total, moment

        zero = jnp.zeros((8, POINTS), jnp.float32)
        total, moment = lax.fori_loop(0, FREQS // 2, pair, (zero, zero))
        total = jnp.sum(total, axis=0, keepdims=True)
        moment = jnp.sum(moment, axis=0, keepdims=True)
        mean = moment / (total + 1e-6)
        aux_out[k, 3:4, :] = zero[0:1]
        aux_out[k, 0:2, :] = windv[k]
        aux_out[k, 2:3, :] = 0.3 * (total / (total + 1.0)) / (mean * mean)

    for dg in (2, 1, 3, 0):
        to = lax.rem(me_c + dg, GROUPS)
        for k in range(SLOTS):
            dst = aux_in.at[me_c * SLOTS + k]
            if dg == 0 and k == 1:
                pltpu.make_async_copy(aux_out.at[k], dst, aux_recv).start()
            else:
                pltpu.make_async_remote_copy(
                    aux_out.at[k], dst, aux_send, aux_recv, device_id=(to, region(k - 1)), device_id_type=MESH
                ).start()

    for ch in range(2, WINDOW):
        send_in(ch)

    for n in range(16):
        lon = lax.rem(me_r * REGION_LONS + (n - 6 + GRID_LON), GRID_LON)
        levels = jnp.where(lane[0:2] == lon, depthv[...].astype(jnp.float32), 0.0)
        cells[0, 2 * n:2 * n + 2, :] = jnp.broadcast_to(jnp.sum(levels, axis=1, keepdims=True), (2, POINTS))
        rows = pl.ds(pl.multiple_of(lon // 8 * 8, 8), 8)
        here = row == lax.rem(lon, 8)
        for part in range(2):
            wet_rows = wetv[rows, part * POINTS:(part + 1) * POINTS].astype(jnp.float32)
            cells[1, 2 * n + part:2 * n + part + 1, :] = jnp.sum(
                jnp.where(here, wet_rows, 0.0), axis=0, keepdims=True
            )

    def from_lon(values, start):
        return values[2 * (start + 6):2 * (start + 6) + 8]

    def shift_down(value):
        rolled = pltpu.roll(value, 1, 1)
        return jnp.where(lane == 0, pltpu.roll(rolled, 1, 0), rolled)

    def shift_up(value):
        rolled = pltpu.roll(value, POINTS - 1, 1)
        return jnp.where(lane == POINTS - 1, pltpu.roll(rolled, 7, 0), rolled)

    last = (lax.rem(row, 2) == 1) & (lane == POINTS - 1)
    wets = cells.at[1]

    def prepare(i, _):
        for m in range(4):
            level = cells[0, 8 * m:8 * m + 8]
            speed = jnp.zeros((8, POINTS), jnp.float32)
            for d in range(NDEPTH):
                speed = jnp.where(level == float(d), table_s[T_SPEED + d * FREQS + me_c * GROUP_FREQS + i], speed)
            speeds[8 * m:8 * m + 8] = speed
        made = []
        for part, start in enumerate((-REGION_LONS, 0, REGION_LONS)):
            west, mid, east = (from_lon(speeds, start + n) for n in (-1, 0, 1))
            wet_west, wet_mid, wet_east = (from_lon(wets, start + n) for n in (-1, 0, 1))
            face = jnp.where(last, 0.0, 0.45 * (mid + shift_up(mid)) * wet_mid * shift_up(wet_mid))
            made.append((
                latv[0] * (mid + east) * wet_mid * wet_east,
                latv[0] * (mid + west) * wet_mid * wet_west,
                face,
                shift_down(face),
                latv[1] * mid,
                0.4 * (east - west),
            ))
        for n in range(6):
            for part in range(3):
                coef[i, part, n] = made[part][n]
            coef[i, BESIDE, n] = jnp.where(row < 4, made[EAST][n], made[WEST][n])
        return 0

    lax.fori_loop(0, GROUP_FREQS, prepare, 0)

    held = []
    for s in range(SOURCES):
        held.append(slot_s[((s // SLOTS) * REGIONS + region(1 - s % SLOTS)) * SLOTS + s % SLOTS])
    holder = []
    for v in range(BLOCKS):
        found = jnp.int32(0)
        for s in range(SOURCES):
            found = jnp.where(held[s] == v, jnp.int32(s), found)
        holder.append(found)
    back_row = [jnp.maximum(h, 0) for h in held]
    kept = [jnp.where(h >= 0, jnp.float32(1.0), jnp.float32(0.0)) for h in held]

    def halo_copies(ch):
        freqs = pl.ds(ch * CHUNK, CHUNK)
        return [
            pltpu.make_async_remote_copy(
                field.at[freqs], halo.at[freqs], halo_send.at[n, ch], halo_recv.at[n, ch],
                device_id=(me_c, region(shift)), device_id_type=MESH,
            )
            for n, (halo, shift) in enumerate(((halo_w, 1), (halo_e, -1)))
        ]

    def send_halos(ch):
        for copy in halo_copies(ch):
            copy.start()

    def source_terms(ch):
        wind_x, wind_y, damp = scal[0], scal[1], scal[2]
        for n in range(CHUNK):
            i = ch * CHUNK + n
            f = me_c * GROUP_FREQS + i
            along = table_s[T_ALONG + f]
            gain = table_s[T_GAIN + f]
            scale = 1.0 / (1.0 + damp * table_s[T_SQUARE + f])
            for q in range(DIRS):
                j = ORDER[q]
                energy = ordered[pl.ds(n * DIRS + j, 8, stride=ROWS), :]
                ratio = jnp.maximum((wind_x * float(COS[j]) + wind_y * float(SIN[j])) * along, 1.0)
                field[i, q] = energy * ((1.0 + gain) - gain / ratio) * scale

    def along_lon(q, parts, coefs, ring):
        turn = 2 if q < HALF else 6
        rolled = [pltpu.roll(part, turn, 0) for part in parts]
        edge = row < 2 if q < HALF else row >= 6
        moved = []
        for n, part in enumerate(parts):
            other = n - 1 if q < HALF else n + 1
            if ring:
                beside = jnp.where(edge, rolled[other % len(parts)], rolled[n])
            elif 0 <= other < len(parts):
                beside = jnp.where(edge, rolled[other], rolled[n])
            else:
                beside = rolled[n]
            from_west, from_east = (beside, part) if q < HALF else (part, beside)
            flux = coefs[n][0] * from_east - coefs[n][1] * from_west
            moved.append(part - float(COS[ORDER[q]]) * flux)
        return moved

    def along_lat(q, energy, coefs):
        sine = float(SIN[ORDER[q]])
        if sine > 0:
            share = coefs[2] * energy
            flux = share - shift_down(share)
        else:
            share = coefs[3] * energy
            flux = shift_up(share) - share
        return energy - sine * flux

    def refracted(moved, coefs, store):
        first = moved(0)
        here = first
        opening = before = None
        for q in range(DIRS):
            following = moved(q + 1) if q + 1 < DIRS else first
            j = ORDER[q]
            fluxes = []
            for n, part in enumerate(here):
                rate = coefs[n][4] * float(COS_FACE[j]) + coefs[n][5] * float(SIN_FACE[j])
                fluxes.append(rate * jnp.where(rate > 0.0, part, following[n]))
            if q == 0:
                opening = fluxes
            else:
                for n, part in enumerate(here):
                    store(q, n, part - (fluxes[n] - before[n]))
            before = fluxes
            here = following
        for n, part in enumerate(first):
            store(0, n, part - (opening[n] - before[n]))

    def propagate(ch):
        def one(n, _):
            i = ch * CHUNK + n
            west, mid, east, beside = ([coef[i, part, m] for m in range(6)] for part in range(4))
            wet_here = from_lon(wets, 0)
            wide = (west, mid, east)
            narrow = (mid, beside)

            def first_step(q):
                parts = along_lon(q, (halo_w[i, q], field[i, q], halo_e[i, q]), wide, False)
                return [along_lat(q, part, c) for part, c in zip(parts, wide)]

            def second_step(q):
                parts = along_lon(q, [one_on[part, q] for part in range(3)], wide, False)
                parts = (parts[MID], jnp.where(row < 4, parts[EAST], parts[WEST]))
                return [along_lat(q, part, c) for part, c in zip(parts, narrow)]

            def third_step(q):
                parts = along_lon(q, (two_on[0, q], two_on[1, q]), narrow, True)
                return [along_lat(q, part, c) for part, c in zip(parts, narrow)]

            def fourth_step(q):
                parts = along_lon(q, (three_on[0, q], three_on[1, q]), narrow, True)
                return [along_lat(q, parts[0], mid)]

            def to(buffer):
                def store(q, part, energy):
                    buffer[part, q] = energy
                return store

            def to_back(q, part, energy):
                back[pl.ds(n * DIRS + ORDER[q], 8, stride=ROWS), :] = energy * wet_here

            refracted(first_step, wide, to(one_on))
            refracted(second_step, narrow, to(two_on))
            refracted(third_step, narrow, to(three_on))
            refracted(fourth_step, (mid,), to_back)
            return 0

        lax.fori_loop(0, CHUNK, one, 0)

    def send_back(ch):
        for v in range(BLOCKS):
            blocks[v] = back[v * ROWS:(v + 1) * ROWS, :]
        for s in range(SOURCES):
            outb[ch, s] = blocks[back_row[s]] * kept[s]
        for k, dg in [(k, dg) for k in (0, 2, 1) for dg in (1, 2, 3, 0)]:
            to = across(dg)
            if True:
                src = outb.at[ch, to * SLOTS + k]
                dst = out.at[k, pl.ds(me_c * GROUP_COMPS + ch * ROWS, ROWS)]
                if dg == 0 and k == 1:
                    pltpu.make_async_copy(src, dst, out_recv).start()
                else:
                    pltpu.make_async_remote_copy(
                        src, dst, out_send.at[ch], out_recv, device_id=(to, region(1 - k)), device_id_type=MESH
                    ).start()

    def step(t, _):
        for ch in range(CHUNKS):
            @pl.when(t == ch)
            def _(ch=ch):
                if ch + WINDOW < CHUNKS:
                    wait_bytes(inb[ch].at[0:SOURCES - 1], in_send.at[ch])
                    send_in(ch + WINDOW)
                wait_bytes(inb[ch], in_recv.at[ch])
                for v in range(BLOCKS):
                    ordered[v * ROWS:(v + 1) * ROWS, :] = inb[ch][holder[v]]
                if ch == 0:
                    wait_bytes(aux_in, aux_recv)
                    for v in range(BLOCKS):
                        for n in range(3):
                            scal[n, v:v + 1, :] = aux_in[holder[v]][n:n + 1, :]

        @pl.when(t < CHUNKS)
        def _():
            source_terms(t)
            send_halos(t)

        @pl.when(t >= LAG)
        def _():
            for copy in halo_copies(t - LAG):
                copy.wait_recv()
            propagate(t - LAG)
            send_back(t - LAG)

        return 0

    lax.fori_loop(0, CHUNKS + LAG, step, 0)

    wait_bytes(aux_in.at[0:SOURCES - 1], aux_send)
    for ch in range(CHUNKS):
        if ch + WINDOW >= CHUNKS:
            wait_bytes(inb[ch].at[0:SOURCES - 1], in_send.at[ch])
        wait_bytes(outb.at[ch, 0:SOURCES - 1], out_send.at[ch])

    def drain(n, _):
        for copy in halo_copies(n):
            copy.wait_send()
        return 0

    lax.fori_loop(0, CHUNKS, drain, 0)
    wait_bytes(out, out_recv)


def finish(moved, out, sems):
    copies = [pltpu.make_async_copy(moved.at[k], out.at[k], sems.at[k]) for k in range(SLOTS)]
    for copy in copies:
        copy.start()
    for copy in copies:
        copy.wait()


def per_device(spectra, wind_vectors, slot_block, wet_mask, depth_class):
    hbm = pl.BlockSpec(memory_space=pltpu.HBM)
    vmem = pl.BlockSpec(memory_space=pltpu.VMEM)
    f32 = jnp.float32
    dma = pltpu.SemaphoreType.DMA
    scratch = [
        pltpu.VMEM((SLOTS, COMPS, POINTS), f32),
        pltpu.VMEM((SLOTS, 2, POINTS), f32),
        pltpu.SMEM((GROUPS * REGIONS * SLOTS,), jnp.int32),
        pltpu.VMEM((GRID_LON, 2 * POINTS), jnp.int32),
        pltpu.VMEM((2, GRID_LON), jnp.int32),
        pltpu.SMEM((T_SIZE,), f32),
        pltpu.VMEM((2, 8, POINTS), f32),
        pltpu.VMEM((SLOTS, 4, POINTS), f32),
        pltpu.VMEM((SOURCES, 4, POINTS), f32),
        pltpu.VMEM((3, 8, POINTS), f32),
        pltpu.VMEM((2, 32, POINTS), f32),
        pltpu.VMEM((32, POINTS), f32),
        pltpu.VMEM((GROUP_FREQS, 4, 6, 8, POINTS), f32),
        pltpu.VMEM(((BLOCKS + 1) * ROWS, POINTS), f32),
        pltpu.VMEM((GROUP_FREQS, DIRS, 8, POINTS), f32),
        pltpu.VMEM((GROUP_FREQS, DIRS, 8, POINTS), f32),
        pltpu.VMEM((GROUP_FREQS, DIRS, 8, POINTS), f32),
        pltpu.VMEM((3, DIRS, 8, POINTS), f32),
        pltpu.VMEM((2, DIRS, 8, POINTS), f32),
        pltpu.VMEM((2, DIRS, 8, POINTS), f32),
        pltpu.VMEM(((BLOCKS + 1) * ROWS, POINTS), f32),
        pltpu.VMEM((BLOCKS, ROWS, POINTS), f32),
        pltpu.VMEM((CHUNKS, SOURCES, ROWS, POINTS), f32),
        dma((7,)),
        dma((CHUNKS,)),
        dma((CHUNKS,)),
        dma,
        dma,
        dma((2, CHUNKS)),
        dma((2, CHUNKS)),
        dma((CHUNKS,)),
        dma,
        pltpu.SemaphoreType.REGULAR,
    ] + [pltpu.VMEM((SOURCES, ROWS, POINTS), f32) for _ in range(CHUNKS)]
    given = (spectra, wind_vectors, slot_block, wet_mask, depth_class.T, scalar_table(), latitude_table())
    moved = pl.pallas_call(
        kernel,
        out_shape=pltpu.VMEM((SLOTS, COMPS, POINTS), f32),
        in_specs=[hbm] * 7,
        out_specs=vmem,
        scratch_shapes=scratch,
        compiler_params=pltpu.CompilerParams(
            collective_id=0, has_side_effects=True, vmem_limit_bytes=40 * 1024 * 1024
        ),
        name="wave_step",
    )(*[pltpu.with_memory_space_constraint(jnp.asarray(array), pltpu.HBM) for array in given])
    return pl.pallas_call(
        finish,
        out_shape=jax.ShapeDtypeStruct((SLOTS, COMPS, POINTS), f32),
        in_specs=[vmem],
        out_specs=hbm,
        scratch_shapes=[dma((SLOTS,))],
        compiler_params=pltpu.CompilerParams(vmem_limit_bytes=8 * 1024 * 1024),
        name="finish",
    )(pltpu.with_memory_space_constraint(moved, pltpu.VMEM))


def solution(mesh):
    return jax.shard_map(
        per_device,
        mesh=mesh,
        in_specs=(P(("comp", "lon"), None, None), P(("comp", "lon"), None, None), P(), P(), P()),
        out_specs=P(("comp", "lon"), None, None),
        check_vma=False,
    )
```

```python
import functools

import jax
import jax.numpy as jnp
import numpy as np
from jax import lax
from jax.experimental import pallas as pl
from jax.experimental.pallas import tpu as pltpu
from jax.sharding import PartitionSpec as P

MESH = pl.DeviceIdType.MESH

DIRS = 36
HALF = DIRS // 2
FREQS = 48
GROUPS = 4
REGIONS = 32
SLOTS = 3
SOURCES = GROUPS * SLOTS
POINTS = 128
NDEPTH = 8
NSUB = 4
BLOCKS = 8
GRID_LON = 128
REGION_LONS = GRID_LON // REGIONS
GROUP_FREQS = FREQS // GROUPS
COMPS = FREQS * DIRS
GROUP_COMPS = GROUP_FREQS * DIRS

CHUNK = 2
CHUNKS = GROUP_FREQS // CHUNK
ROWS = CHUNK * DIRS

GRAVITY = 9.81

ORDER = [(q + 27) % DIRS for q in range(DIRS)]
ANGLE = (np.arange(DIRS) + 0.5) * (2.0 * np.pi / DIRS)
COS = np.cos(ANGLE)
SIN = np.sin(ANGLE)
COS_FACE = 0.5 * (COS + np.roll(COS, -1))
SIN_FACE = 0.5 * (SIN + np.roll(SIN, -1))

T_SPEED = 0
T_ALONG = T_SPEED + NDEPTH * FREQS
T_GAIN = T_ALONG + FREQS
T_SQUARE = T_GAIN + FREQS
T_WEIGHT = T_SQUARE + FREQS
T_WEIGHT_FREQ = T_WEIGHT + FREQS
T_SIZE = 640
LAG = 2
WINDOW = 3
EARLY = 2

WEST, MID, EAST, BESIDE = range(4)


def scalar_table():
    sigma = 2.0 * np.pi * 0.0418 * 1.07 ** np.arange(FREQS, dtype=np.float64)
    depth = 8.0 * 2.0 ** np.arange(NDEPTH, dtype=np.float64)
    deep = sigma * sigma / GRAVITY
    number = deep[None, :] / np.sqrt(np.tanh(deep[None, :] * depth[:, None]))
    twice = 2.0 * number * depth[:, None]
    factor = 2.0 * twice * np.exp(-twice) / (1.0 - np.exp(-2.0 * twice))
    speed = 0.5 * sigma[None, :] / number * (1.0 + factor)
    speed = speed / speed.max()
    weight = sigma / (sigma.sum() * DIRS)
    table = np.zeros(T_SIZE, np.float64)
    table[T_SPEED:T_ALONG] = speed.reshape(-1)
    table[T_ALONG:T_GAIN] = sigma / GRAVITY
    table[T_GAIN:T_SQUARE] = 0.5 * sigma / sigma[-1]
    table[T_SQUARE:T_WEIGHT] = sigma * sigma
    table[T_WEIGHT:T_WEIGHT_FREQ] = weight
    table[T_WEIGHT_FREQ:T_WEIGHT_FREQ + FREQS] = weight * sigma
    return table.astype(np.float32)


def latitude_table():
    count = 2 * POINTS
    phi = (-60.0 + (np.arange(count) + 0.5) * 120.0 / count) * np.pi / 180.0
    rows = np.concatenate([0.5 * 0.45 / np.cos(phi), 0.3 * np.tan(phi)])
    parts = rows.reshape(2, 1, 2, POINTS)
    return np.broadcast_to(parts, (2, REGION_LONS, 2, POINTS)).reshape(2, 8, POINTS).astype(np.float32)


def wait_bytes(ref, sem):
    pltpu.make_async_copy(ref, ref, sem).wait()


def kernel(
    x, wind, slots, wet, depth, table, lat, out,
    xv, windv, slot_s, wetv, depthv, table_s, latv,
    aux_out, aux_in, scal, cells, speeds, coef, ordered, field, halo_w, halo_e, one_on, two_on, three_on, back, blocks, outb,
    local_sem, in_send, in_recv, aux_send, aux_recv, halo_send, halo_recv, out_send, out_recv, ready, far,
    *inb,
):
    me_c = lax.axis_index("comp")
    me_r = lax.axis_index("lon")

    def region(shift):
        return lax.rem(me_r + (shift + REGIONS), REGIONS)

    def across(dg):
        return lax.rem(me_c + jnp.where(lax.rem(me_r, 2) == 0, dg, (GROUPS - dg) % GROUPS), GROUPS)

    loads = [
        pltpu.make_async_copy(src, dst, local_sem.at[n])
        for n, (src, dst) in enumerate(
            ((x, xv), (wind, windv), (slots, slot_s), (wet, wetv), (depth, depthv), (table, table_s), (lat, latv))
        )
    ]
    odd = lax.rem(me_r, 2)
    beside_r = me_r + 1 - 2 * odd
    beyond_r = region(2 * odd - 1)
    leader = me_c == GROUPS - 1

    barrier = pltpu.get_barrier_semaphore()
    for dg in range(1, GROUPS):
        pl.semaphore_signal(barrier, inc=1, device_id=(lax.rem(me_c + dg, GROUPS), me_r), device_id_type=MESH)
    pl.semaphore_signal(barrier, inc=1, device_id=(me_c, beside_r), device_id_type=MESH)

    @pl.when(leader)
    def _():
        pl.semaphore_signal(barrier, inc=1, device_id=(me_c, beyond_r), device_id_type=MESH)

    for load in loads:
        load.start()
    pl.semaphore_wait(barrier, jnp.where(leader, GROUPS + 1, GROUPS))

    def send_in(ch, slots=(0, 2, 1)):
        for k, dg in [(k, dg) for k in slots for dg in (1, 2, 3, 0)]:
            to = across(dg)
            if True:
                src = x.at[k, pl.ds(to * GROUP_COMPS + ch * ROWS, ROWS)]
                dst = inb[ch].at[me_c * SLOTS + k]
                if dg == 0 and isinstance(k, int) and k == 1:
                    pltpu.make_async_copy(src, dst, in_recv.at[ch]).start()
                else:
                    pltpu.make_async_remote_copy(
                        src, dst, in_send.at[ch], in_recv.at[ch], device_id=(to, region(k - 1)), device_id_type=MESH
                    ).start()

    @pl.when(leader)
    def _():
        pl.semaphore_signal(far, inc=1, device_id=(me_c, beyond_r), device_id_type=MESH)

    for dg in range(1, GROUPS):
        pl.semaphore_signal(ready, inc=1, device_id=(lax.rem(me_c + dg, GROUPS), me_r), device_id_type=MESH)
    for ch in range(EARLY):
        send_in(ch, (1,))
    pl.semaphore_wait(ready, GROUPS - 1)
    for ch in range(EARLY):
        send_in(ch, (2 - 2 * odd,))
    @pl.when(leader)
    def _():
        pl.semaphore_wait(far, 1)
        for dg in range(1, GROUPS):
            pl.semaphore_signal(far, inc=1, device_id=(lax.rem(me_c + dg, GROUPS), me_r), device_id_type=MESH)

    row = lax.broadcasted_iota(jnp.int32, (8, POINTS), 0)
    lane = lax.broadcasted_iota(jnp.int32, (8, POINTS), 1)

    for load in loads:
        load.wait()
    upper = row < 4
    for k in range(SLOTS):
        def pair(p, sums, k=k):
            total, moment = sums
            tiles = [xv[k, pl.ds(pl.multiple_of(p * 72 + 8 * n, 8), 8), :] for n in range(9)]
            first = (tiles[0] + tiles[1]) + (tiles[2] + tiles[3]) + jnp.where(upper, tiles[4], 0.0)
            second = (tiles[5] + tiles[6]) + (tiles[7] + tiles[8]) + jnp.where(upper, 0.0, tiles[4])
            total = total + first * table_s[T_WEIGHT + 2 * p] + second * table_s[T_WEIGHT + 2 * p + 1]
            moment = moment + first * table_s[T_WEIGHT_FREQ + 2 * p] + second * table_s[T_WEIGHT_FREQ + 2 * p + 1]
            return total, moment

        zero = jnp.zeros((8, POINTS), jnp.float32)
        total, moment = lax.fori_loop(0, FREQS // 2, pair, (zero, zero))
        total = jnp.sum(total, axis=0, keepdims=True)
        moment = jnp.sum(moment, axis=0, keepdims=True)
        mean = moment / (total + 1e-6)
        aux_out[k, 3:4, :] = zero[0:1]
        aux_out[k, 0:2, :] = windv[k]
        aux_out[k, 2:3, :] = 0.3 * (total / (total + 1.0)) / (mean * mean)

    @pl.when(jnp.logical_not(leader))
    def _():
        pl.semaphore_wait(far, 1)

    for ch in range(EARLY):
        send_in(ch, (2 * odd,))

    for dg in (2, 1, 3, 0):
        to = lax.rem(me_c + dg, GROUPS)
        for k in range(SLOTS):
            dst = aux_in.at[me_c * SLOTS + k]
            if dg == 0 and k == 1:
                pltpu.make_async_copy(aux_out.at[k], dst, aux_recv).start()
            else:
                pltpu.make_async_remote_copy(
                    aux_out.at[k], dst, aux_send, aux_recv, device_id=(to, region(k - 1)), device_id_type=MESH
                ).start()

    for ch in range(EARLY, WINDOW):
        send_in(ch)

    for n in range(16):
        lon = lax.rem(me_r * REGION_LONS + (n - 6 + GRID_LON), GRID_LON)
        levels = jnp.where(lane[0:2] == lon, depthv[...].astype(jnp.float32), 0.0)
        cells[0, 2 * n:2 * n + 2, :] = jnp.broadcast_to(jnp.sum(levels, axis=1, keepdims=True), (2, POINTS))
        rows = pl.ds(pl.multiple_of(lon // 8 * 8, 8), 8)
        here = row == lax.rem(lon, 8)
        for part in range(2):
            wet_rows = wetv[rows, part * POINTS:(part + 1) * POINTS].astype(jnp.float32)
            cells[1, 2 * n + part:2 * n + part + 1, :] = jnp.sum(
                jnp.where(here, wet_rows, 0.0), axis=0, keepdims=True
            )

    def from_lon(values, start):
        return values[2 * (start + 6):2 * (start + 6) + 8]

    def shift_down(value):
        rolled = pltpu.roll(value, 1, 1)
        return jnp.where(lane == 0, pltpu.roll(rolled, 1, 0), rolled)

    def shift_up(value):
        rolled = pltpu.roll(value, POINTS - 1, 1)
        return jnp.where(lane == POINTS - 1, pltpu.roll(rolled, 7, 0), rolled)

    last = (lax.rem(row, 2) == 1) & (lane == POINTS - 1)
    wets = cells.at[1]

    def prepare(i, _):
        for m in range(4):
            level = cells[0, 8 * m:8 * m + 8]
            speed = jnp.zeros((8, POINTS), jnp.float32)
            for d in range(NDEPTH):
                speed = jnp.where(level == float(d), table_s[T_SPEED + d * FREQS + me_c * GROUP_FREQS + i], speed)
            speeds[8 * m:8 * m + 8] = speed
        made = []
        for part, start in enumerate((-REGION_LONS, 0, REGION_LONS)):
            west, mid, east = (from_lon(speeds, start + n) for n in (-1, 0, 1))
            wet_west, wet_mid, wet_east = (from_lon(wets, start + n) for n in (-1, 0, 1))
            face = jnp.where(last, 0.0, 0.45 * (mid + shift_up(mid)) * wet_mid * shift_up(wet_mid))
            made.append((
                latv[0] * (mid + east) * wet_mid * wet_east,
                latv[0] * (mid + west) * wet_mid * wet_west,
                face,
                shift_down(face),
                latv[1] * mid,
                0.4 * (east - west),
            ))
        for n in range(6):
            for part in range(3):
                coef[i, part, n] = made[part][n]
            coef[i, BESIDE, n] = jnp.where(row < 4, made[EAST][n], made[WEST][n])
        return 0

    lax.fori_loop(0, GROUP_FREQS, prepare, 0)

    held = []
    for s in range(SOURCES):
        held.append(slot_s[((s // SLOTS) * REGIONS + region(1 - s % SLOTS)) * SLOTS + s % SLOTS])
    holder = []
    for v in range(BLOCKS):
        found = jnp.int32(0)
        for s in range(SOURCES):
            found = jnp.where(held[s] == v, jnp.int32(s), found)
        holder.append(found)
    back_row = [jnp.maximum(h, 0) for h in held]
    kept = [jnp.where(h >= 0, jnp.float32(1.0), jnp.float32(0.0)) for h in held]

    def halo_copies(ch):
        freqs = pl.ds(ch * CHUNK, CHUNK)
        return [
            pltpu.make_async_remote_copy(
                field.at[freqs], halo.at[freqs], halo_send.at[n, ch], halo_recv.at[n, ch],
                device_id=(me_c, region(shift)), device_id_type=MESH,
            )
            for n, (halo, shift) in enumerate(((halo_w, 1), (halo_e, -1)))
        ]

    def send_halos(ch):
        for copy in halo_copies(ch):
            copy.start()

    def source_terms(ch):
        wind_x, wind_y, damp = scal[0], scal[1], scal[2]
        for n in range(CHUNK):
            i = ch * CHUNK + n
            f = me_c * GROUP_FREQS + i
            along = table_s[T_ALONG + f]
            gain = table_s[T_GAIN + f]
            scale = 1.0 / (1.0 + damp * table_s[T_SQUARE + f])
            for q in range(DIRS):
                j = ORDER[q]
                energy = ordered[pl.ds(n * DIRS + j, 8, stride=ROWS), :]
                ratio = jnp.maximum((wind_x * float(COS[j]) + wind_y * float(SIN[j])) * along, 1.0)
                field[i, q] = energy * ((1.0 + gain) - gain / ratio) * scale

    def along_lon(q, parts, coefs, ring):
        turn = 2 if q < HALF else 6
        rolled = [pltpu.roll(part, turn, 0) for part in parts]
        edge = row < 2 if q < HALF else row >= 6
        moved = []
        for n, part in enumerate(parts):
            other = n - 1 if q < HALF else n + 1
            if ring:
                beside = jnp.where(edge, rolled[other % len(parts)], rolled[n])
            elif 0 <= other < len(parts):
                beside = jnp.where(edge, rolled[other], rolled[n])
            else:
                beside = rolled[n]
            from_west, from_east = (beside, part) if q < HALF else (part, beside)
            flux = coefs[n][0] * from_east - coefs[n][1] * from_west
            moved.append(part - float(COS[ORDER[q]]) * flux)
        return moved

    def along_lat(q, energy, coefs):
        sine = float(SIN[ORDER[q]])
        if sine > 0:
            share = coefs[2] * energy
            flux = share - shift_down(share)
        else:
            share = coefs[3] * energy
            flux = shift_up(share) - share
        return energy - sine * flux

    def refracted(moved, coefs, store):
        first = moved(0)
        here = first
        opening = before = None
        for q in range(DIRS):
            following = moved(q + 1) if q + 1 < DIRS else first
            j = ORDER[q]
            fluxes = []
            for n, part in enumerate(here):
                rate = coefs[n][4] * float(COS_FACE[j]) + coefs[n][5] * float(SIN_FACE[j])
                fluxes.append(rate * jnp.where(rate > 0.0, part, following[n]))
            if q == 0:
                opening = fluxes
            else:
                for n, part in enumerate(here):
                    store(q, n, part - (fluxes[n] - before[n]))
            before = fluxes
            here = following
        for n, part in enumerate(first):
            store(0, n, part - (opening[n] - before[n]))

    def propagate(ch):
        def one(n, _):
            i = ch * CHUNK + n
            west, mid, east, beside = ([coef[i, part, m] for m in range(6)] for part in range(4))
            wet_here = from_lon(wets, 0)
            wide = (west, mid, east)
            narrow = (mid, beside)

            def first_step(q):
                parts = along_lon(q, (halo_w[i, q], field[i, q], halo_e[i, q]), wide, False)
                return [along_lat(q, part, c) for part, c in zip(parts, wide)]

            def second_step(q):
                parts = along_lon(q, [one_on[part, q] for part in range(3)], wide, False)
                parts = (parts[MID], jnp.where(row < 4, parts[EAST], parts[WEST]))
                return [along_lat(q, part, c) for part, c in zip(parts, narrow)]

            def third_step(q):
                parts = along_lon(q, (two_on[0, q], two_on[1, q]), narrow, True)
                return [along_lat(q, part, c) for part, c in zip(parts, narrow)]

            def fourth_step(q):
                parts = along_lon(q, (three_on[0, q], three_on[1, q]), narrow, True)
                return [along_lat(q, parts[0], mid)]

            def to(buffer):
                def store(q, part, energy):
                    buffer[part, q] = energy
                return store

            def to_back(q, part, energy):
                back[pl.ds(n * DIRS + ORDER[q], 8, stride=ROWS), :] = energy * wet_here

            refracted(first_step, wide, to(one_on))
            refracted(second_step, narrow, to(two_on))
            refracted(third_step, narrow, to(three_on))
            refracted(fourth_step, (mid,), to_back)
            return 0

        lax.fori_loop(0, CHUNK, one, 0)

    def send_back(ch):
        for v in range(BLOCKS):
            blocks[v] = back[v * ROWS:(v + 1) * ROWS, :]
        for s in range(SOURCES):
            outb[ch, s] = blocks[back_row[s]] * kept[s]
        for k, dg in [(k, dg) for k in (0, 2, 1) for dg in (1, 2, 3, 0)]:
            to = across(dg)
            if True:
                src = outb.at[ch, to * SLOTS + k]
                dst = out.at[k, pl.ds(me_c * GROUP_COMPS + ch * ROWS, ROWS)]
                if dg == 0 and k == 1:
                    pltpu.make_async_copy(src, dst, out_recv).start()
                else:
                    pltpu.make_async_remote_copy(
                        src, dst, out_send.at[ch], out_recv, device_id=(to, region(1 - k)), device_id_type=MESH
                    ).start()

    def step(t, _):
        for ch in range(CHUNKS):
            @pl.when(t == ch)
            def _(ch=ch):
                if ch + WINDOW < CHUNKS:
                    wait_bytes(inb[ch].at[0:SOURCES - 1], in_send.at[ch])
                    send_in(ch + WINDOW)
                wait_bytes(inb[ch], in_recv.at[ch])
                for v in range(BLOCKS):
                    ordered[v * ROWS:(v + 1) * ROWS, :] = inb[ch][holder[v]]
                if ch == 0:
                    wait_bytes(aux_in, aux_recv)
                    for v in range(BLOCKS):
                        for n in range(3):
                            scal[n, v:v + 1, :] = aux_in[holder[v]][n:n + 1, :]

        @pl.when(t < CHUNKS)
        def _():
            source_terms(t)
            send_halos(t)

        @pl.when(t >= LAG)
        def _():
            for copy in halo_copies(t - LAG):
                copy.wait_recv()
            propagate(t - LAG)
            send_back(t - LAG)

        return 0

    lax.fori_loop(0, CHUNKS + LAG, step, 0)

    wait_bytes(aux_in.at[0:SOURCES - 1], aux_send)
    for ch in range(CHUNKS):
        if ch + WINDOW >= CHUNKS:
            wait_bytes(inb[ch].at[0:SOURCES - 1], in_send.at[ch])
        wait_bytes(outb.at[ch, 0:SOURCES - 1], out_send.at[ch])

    def drain(n, _):
        for copy in halo_copies(n):
            copy.wait_send()
        return 0

    lax.fori_loop(0, CHUNKS, drain, 0)
    wait_bytes(out, out_recv)


def finish(moved, out, sems):
    copies = [pltpu.make_async_copy(moved.at[k], out.at[k], sems.at[k]) for k in range(SLOTS)]
    for copy in copies:
        copy.start()
    for copy in copies:
        copy.wait()


def per_device(spectra, wind_vectors, slot_block, wet_mask, depth_class):
    hbm = pl.BlockSpec(memory_space=pltpu.HBM)
    vmem = pl.BlockSpec(memory_space=pltpu.VMEM)
    f32 = jnp.float32
    dma = pltpu.SemaphoreType.DMA
    scratch = [
        pltpu.VMEM((SLOTS, COMPS, POINTS), f32),
        pltpu.VMEM((SLOTS, 2, POINTS), f32),
        pltpu.SMEM((GROUPS * REGIONS * SLOTS,), jnp.int32),
        pltpu.VMEM((GRID_LON, 2 * POINTS), jnp.int32),
        pltpu.VMEM((2, GRID_LON), jnp.int32),
        pltpu.SMEM((T_SIZE,), f32),
        pltpu.VMEM((2, 8, POINTS), f32),
        pltpu.VMEM((SLOTS, 4, POINTS), f32),
        pltpu.VMEM((SOURCES, 4, POINTS), f32),
        pltpu.VMEM((3, 8, POINTS), f32),
        pltpu.VMEM((2, 32, POINTS), f32),
        pltpu.VMEM((32, POINTS), f32),
        pltpu.VMEM((GROUP_FREQS, 4, 6, 8, POINTS), f32),
        pltpu.VMEM(((BLOCKS + 1) * ROWS, POINTS), f32),
        pltpu.VMEM((GROUP_FREQS, DIRS, 8, POINTS), f32),
        pltpu.VMEM((GROUP_FREQS, DIRS, 8, POINTS), f32),
        pltpu.VMEM((GROUP_FREQS, DIRS, 8, POINTS), f32),
        pltpu.VMEM((3, DIRS, 8, POINTS), f32),
        pltpu.VMEM((2, DIRS, 8, POINTS), f32),
        pltpu.VMEM((2, DIRS, 8, POINTS), f32),
        pltpu.VMEM(((BLOCKS + 1) * ROWS, POINTS), f32),
        pltpu.VMEM((BLOCKS, ROWS, POINTS), f32),
        pltpu.VMEM((CHUNKS, SOURCES, ROWS, POINTS), f32),
        dma((7,)),
        dma((CHUNKS,)),
        dma((CHUNKS,)),
        dma,
        dma,
        dma((2, CHUNKS)),
        dma((2, CHUNKS)),
        dma((CHUNKS,)),
        dma,
        pltpu.SemaphoreType.REGULAR,
        pltpu.SemaphoreType.REGULAR,
    ] + [pltpu.VMEM((SOURCES, ROWS, POINTS), f32) for _ in range(CHUNKS)]
    given = (spectra, wind_vectors, slot_block, wet_mask, depth_class.T, scalar_table(), latitude_table())
    moved = pl.pallas_call(
        kernel,
        out_shape=pltpu.VMEM((SLOTS, COMPS, POINTS), f32),
        in_specs=[hbm] * 7,
        out_specs=vmem,
        scratch_shapes=scratch,
        compiler_params=pltpu.CompilerParams(
            collective_id=0, has_side_effects=True, vmem_limit_bytes=40 * 1024 * 1024
        ),
        name="wave_step",
    )(*[pltpu.with_memory_space_constraint(jnp.asarray(array), pltpu.HBM) for array in given])
    return pl.pallas_call(
        finish,
        out_shape=jax.ShapeDtypeStruct((SLOTS, COMPS, POINTS), f32),
        in_specs=[vmem],
        out_specs=hbm,
        scratch_shapes=[dma((SLOTS,))],
        compiler_params=pltpu.CompilerParams(vmem_limit_bytes=8 * 1024 * 1024),
        name="finish",
    )(pltpu.with_memory_space_constraint(moved, pltpu.VMEM))


def solution(mesh):
    return jax.shard_map(
        per_device,
        mesh=mesh,
        in_specs=(P(("comp", "lon"), None, None), P(("comp", "lon"), None, None), P(), P(), P()),
        out_specs=P(("comp", "lon"), None, None),
        check_vma=False,
    )
```

```python
import functools

import jax
import jax.numpy as jnp
import numpy as np
from jax import lax
from jax.experimental import pallas as pl
from jax.experimental.pallas import tpu as pltpu
from jax.sharding import PartitionSpec as P

MESH = pl.DeviceIdType.MESH

DIRS = 36
HALF = DIRS // 2
FREQS = 48
GROUPS = 4
REGIONS = 32
SLOTS = 3
SOURCES = GROUPS * SLOTS
POINTS = 128
NDEPTH = 8
NSUB = 4
BLOCKS = 8
GRID_LON = 128
REGION_LONS = GRID_LON // REGIONS
GROUP_FREQS = FREQS // GROUPS
COMPS = FREQS * DIRS
GROUP_COMPS = GROUP_FREQS * DIRS

CHUNK = 2
CHUNKS = GROUP_FREQS // CHUNK
ROWS = CHUNK * DIRS

GRAVITY = 9.81

ORDER = [(q + 27) % DIRS for q in range(DIRS)]
ANGLE = (np.arange(DIRS) + 0.5) * (2.0 * np.pi / DIRS)
COS = np.cos(ANGLE)
SIN = np.sin(ANGLE)
COS_FACE = 0.5 * (COS + np.roll(COS, -1))
SIN_FACE = 0.5 * (SIN + np.roll(SIN, -1))

T_SPEED = 0
T_ALONG = T_SPEED + NDEPTH * FREQS
T_GAIN = T_ALONG + FREQS
T_SQUARE = T_GAIN + FREQS
T_WEIGHT = T_SQUARE + FREQS
T_WEIGHT_FREQ = T_WEIGHT + FREQS
T_SIZE = 640
LAG = 2
WINDOW = 3

WEST, MID, EAST, BESIDE = range(4)


def scalar_table():
    sigma = 2.0 * np.pi * 0.0418 * 1.07 ** np.arange(FREQS, dtype=np.float64)
    depth = 8.0 * 2.0 ** np.arange(NDEPTH, dtype=np.float64)
    deep = sigma * sigma / GRAVITY
    number = deep[None, :] / np.sqrt(np.tanh(deep[None, :] * depth[:, None]))
    twice = 2.0 * number * depth[:, None]
    factor = 2.0 * twice * np.exp(-twice) / (1.0 - np.exp(-2.0 * twice))
    speed = 0.5 * sigma[None, :] / number * (1.0 + factor)
    speed = speed / speed.max()
    weight = sigma / (sigma.sum() * DIRS)
    table = np.zeros(T_SIZE, np.float64)
    table[T_SPEED:T_ALONG] = speed.reshape(-1)
    table[T_ALONG:T_GAIN] = sigma / GRAVITY
    table[T_GAIN:T_SQUARE] = 0.5 * sigma / sigma[-1]
    table[T_SQUARE:T_WEIGHT] = sigma * sigma
    table[T_WEIGHT:T_WEIGHT_FREQ] = weight
    table[T_WEIGHT_FREQ:T_WEIGHT_FREQ + FREQS] = weight * sigma
    return table.astype(np.float32)


def latitude_table():
    count = 2 * POINTS
    phi = (-60.0 + (np.arange(count) + 0.5) * 120.0 / count) * np.pi / 180.0
    rows = np.concatenate([0.5 * 0.45 / np.cos(phi), 0.3 * np.tan(phi)])
    parts = rows.reshape(2, 1, 2, POINTS)
    return np.broadcast_to(parts, (2, REGION_LONS, 2, POINTS)).reshape(2, 8, POINTS).astype(np.float32)


def wait_bytes(ref, sem):
    pltpu.make_async_copy(ref, ref, sem).wait()


def kernel(
    x, wind, slots, wet, depth, table, lat, out,
    xv, windv, slot_s, wetv, depthv, table_s, latv,
    aux_out, aux_in, scal, cells, speeds, coef, ordered, field, halo_w, halo_e, one_on, two_on, three_on, back, blocks, outb,
    local_sem, in_send, in_recv, aux_send, aux_recv, halo_send, halo_recv, out_send, out_recv, ready,
    *inb,
):
    me_c = lax.axis_index("comp")
    me_r = lax.axis_index("lon")

    def region(shift):
        return lax.rem(me_r + (shift + REGIONS), REGIONS)

    def across(dg):
        return lax.rem(me_c + jnp.where(lax.rem(me_r, 2) == 0, dg, (GROUPS - dg) % GROUPS), GROUPS)

    loads = [
        pltpu.make_async_copy(src, dst, local_sem.at[n])
        for n, (src, dst) in enumerate(
            ((x, xv), (wind, windv), (slots, slot_s), (wet, wetv), (depth, depthv), (table, table_s), (lat, latv))
        )
    ]
    barrier = pltpu.get_barrier_semaphore()
    for dg in range(GROUPS):
        for dr in (-1, 0, 1):
            if (dg == 0) != (dr == 0):
                pl.semaphore_signal(
                    barrier, inc=1, device_id=(lax.rem(me_c + dg, GROUPS), region(dr)), device_id_type=MESH
                )
    for load in loads:
        load.start()
    pl.semaphore_wait(barrier, GROUPS + 1)

    def send_in(ch, slots=(0, 2, 1)):
        for k, dg in [(k, dg) for k in slots for dg in (1, 2, 3, 0)]:
            to = across(dg)
            if True:
                src = x.at[k, pl.ds(to * GROUP_COMPS + ch * ROWS, ROWS)]
                dst = inb[ch].at[me_c * SLOTS + k]
                if dg == 0 and k == 1:
                    pltpu.make_async_copy(src, dst, in_recv.at[ch]).start()
                else:
                    pltpu.make_async_remote_copy(
                        src, dst, in_send.at[ch], in_recv.at[ch], device_id=(to, region(k - 1)), device_id_type=MESH
                    ).start()

    for dg in range(1, GROUPS):
        pl.semaphore_signal(ready, inc=1, device_id=(lax.rem(me_c + dg, GROUPS), me_r), device_id_type=MESH)
    for ch in range(2):
        send_in(ch, (1,))
    pl.semaphore_wait(ready, GROUPS - 1)
    for ch in range(2):
        send_in(ch, (0, 2))
    for ch in range(2, 2):
        send_in(ch)

    row = lax.broadcasted_iota(jnp.int32, (8, POINTS), 0)
    lane = lax.broadcasted_iota(jnp.int32, (8, POINTS), 1)

    for load in loads:
        load.wait()
    upper = row < 4
    for k in range(SLOTS):
        def pair(p, sums, k=k):
            total, moment = sums
            tiles = [xv[k, pl.ds(pl.multiple_of(p * 72 + 8 * n, 8), 8), :] for n in range(9)]
            first = (tiles[0] + tiles[1]) + (tiles[2] + tiles[3]) + jnp.where(upper, tiles[4], 0.0)
            second = (tiles[5] + tiles[6]) + (tiles[7] + tiles[8]) + jnp.where(upper, 0.0, tiles[4])
            total = total + first * table_s[T_WEIGHT + 2 * p] + second * table_s[T_WEIGHT + 2 * p + 1]
            moment = moment + first * table_s[T_WEIGHT_FREQ + 2 * p] + second * table_s[T_WEIGHT_FREQ + 2 * p + 1]
            return total, moment

        zero = jnp.zeros((8, POINTS), jnp.float32)
        total, moment = lax.fori_loop(0, FREQS // 2, pair, (zero, zero))
        total = jnp.sum(total, axis=0, keepdims=True)
        moment = jnp.sum(moment, axis=0, keepdims=True)
        mean = moment / (total + 1e-6)
        aux_out[k, 3:4, :] = zero[0:1]
        aux_out[k, 0:2, :] = windv[k]
        aux_out[k, 2:3, :] = 0.3 * (total / (total + 1.0)) / (mean * mean)

    for dg in (2, 1, 3, 0):
        to = lax.rem(me_c + dg, GROUPS)
        for k in range(SLOTS):
            dst = aux_in.at[me_c * SLOTS + k]
            if dg == 0 and k == 1:
                pltpu.make_async_copy(aux_out.at[k], dst, aux_recv).start()
            else:
                pltpu.make_async_remote_copy(
                    aux_out.at[k], dst, aux_send, aux_recv, device_id=(to, region(k - 1)), device_id_type=MESH
                ).start()

    for ch in range(2, WINDOW):
        send_in(ch)

    for n in range(16):
        lon = lax.rem(me_r * REGION_LONS + (n - 6 + GRID_LON), GRID_LON)
        levels = jnp.where(lane[0:2] == lon, depthv[...].astype(jnp.float32), 0.0)
        cells[0, 2 * n:2 * n + 2, :] = jnp.broadcast_to(jnp.sum(levels, axis=1, keepdims=True), (2, POINTS))
        rows = pl.ds(pl.multiple_of(lon // 8 * 8, 8), 8)
        here = row == lax.rem(lon, 8)
        for part in range(2):
            wet_rows = wetv[rows, part * POINTS:(part + 1) * POINTS].astype(jnp.float32)
            cells[1, 2 * n + part:2 * n + part + 1, :] = jnp.sum(
                jnp.where(here, wet_rows, 0.0), axis=0, keepdims=True
            )

    def from_lon(values, start):
        return values[2 * (start + 6):2 * (start + 6) + 8]

    def shift_down(value):
        rolled = pltpu.roll(value, 1, 1)
        return jnp.where(lane == 0, pltpu.roll(rolled, 1, 0), rolled)

    def shift_up(value):
        rolled = pltpu.roll(value, POINTS - 1, 1)
        return jnp.where(lane == POINTS - 1, pltpu.roll(rolled, 7, 0), rolled)

    last = (lax.rem(row, 2) == 1) & (lane == POINTS - 1)
    wets = cells.at[1]

    def prepare(i, _):
        for m in range(4):
            level = cells[0, 8 * m:8 * m + 8]
            speed = jnp.zeros((8, POINTS), jnp.float32)
            for d in range(NDEPTH):
                speed = jnp.where(level == float(d), table_s[T_SPEED + d * FREQS + me_c * GROUP_FREQS + i], speed)
            speeds[8 * m:8 * m + 8] = speed
        made = []
        for part, start in enumerate((-REGION_LONS, 0, REGION_LONS)):
            west, mid, east = (from_lon(speeds, start + n) for n in (-1, 0, 1))
            wet_west, wet_mid, wet_east = (from_lon(wets, start + n) for n in (-1, 0, 1))
            face = jnp.where(last, 0.0, 0.45 * (mid + shift_up(mid)) * wet_mid * shift_up(wet_mid))
            made.append((
                latv[0] * (mid + east) * wet_mid * wet_east,
                latv[0] * (mid + west) * wet_mid * wet_west,
                face,
                shift_down(face),
                latv[1] * mid,
                0.4 * (east - west),
            ))
        for n in range(6):
            for part in range(3):
                coef[i, part, n] = made[part][n]
            coef[i, BESIDE, n] = jnp.where(row < 4, made[EAST][n], made[WEST][n])
        return 0

    lax.fori_loop(0, GROUP_FREQS, prepare, 0)

    held = []
    for s in range(SOURCES):
        held.append(slot_s[((s // SLOTS) * REGIONS + region(1 - s % SLOTS)) * SLOTS + s % SLOTS])
    holder = []
    for v in range(BLOCKS):
        found = jnp.int32(0)
        for s in range(SOURCES):
            found = jnp.where(held[s] == v, jnp.int32(s), found)
        holder.append(found)
    back_row = [jnp.maximum(h, 0) for h in held]
    kept = [jnp.where(h >= 0, jnp.float32(1.0), jnp.float32(0.0)) for h in held]

    def halo_copies(ch):
        freqs = pl.ds(ch * CHUNK, CHUNK)
        return [
            pltpu.make_async_remote_copy(
                field.at[freqs], halo.at[freqs], halo_send.at[n, ch], halo_recv.at[n, ch],
                device_id=(me_c, region(shift)), device_id_type=MESH,
            )
            for n, (halo, shift) in enumerate(((halo_w, 1), (halo_e, -1)))
        ]

    def send_halos(ch):
        for copy in halo_copies(ch):
            copy.start()

    def source_terms(ch):
        wind_x, wind_y, damp = scal[0], scal[1], scal[2]
        for n in range(CHUNK):
            i = ch * CHUNK + n
            f = me_c * GROUP_FREQS + i
            along = table_s[T_ALONG + f]
            gain = table_s[T_GAIN + f]
            scale = 1.0 / (1.0 + damp * table_s[T_SQUARE + f])
            for q in range(DIRS):
                j = ORDER[q]
                energy = ordered[pl.ds(n * DIRS + j, 8, stride=ROWS), :]
                ratio = jnp.maximum((wind_x * float(COS[j]) + wind_y * float(SIN[j])) * along, 1.0)
                field[i, q] = energy * ((1.0 + gain) - gain / ratio) * scale

    def along_lon(q, parts, coefs, ring):
        turn = 2 if q < HALF else 6
        rolled = [pltpu.roll(part, turn, 0) for part in parts]
        edge = row < 2 if q < HALF else row >= 6
        moved = []
        for n, part in enumerate(parts):
            other = n - 1 if q < HALF else n + 1
            if ring:
                beside = jnp.where(edge, rolled[other % len(parts)], rolled[n])
            elif 0 <= other < len(parts):
                beside = jnp.where(edge, rolled[other], rolled[n])
            else:
                beside = rolled[n]
            from_west, from_east = (beside, part) if q < HALF else (part, beside)
            flux = coefs[n][0] * from_east - coefs[n][1] * from_west
            moved.append(part - float(COS[ORDER[q]]) * flux)
        return moved

    def along_lat(q, energy, coefs):
        sine = float(SIN[ORDER[q]])
        if sine > 0:
            share = coefs[2] * energy
            flux = share - shift_down(share)
        else:
            share = coefs[3] * energy
            flux = shift_up(share) - share
        return energy - sine * flux

    def refracted(moved, coefs, store):
        first = moved(0)
        here = first
        opening = before = None
        for q in range(DIRS):
            following = moved(q + 1) if q + 1 < DIRS else first
            j = ORDER[q]
            fluxes = []
            for n, part in enumerate(here):
                rate = coefs[n][4] * float(COS_FACE[j]) + coefs[n][5] * float(SIN_FACE[j])
                fluxes.append(rate * jnp.where(rate > 0.0, part, following[n]))
            if q == 0:
                opening = fluxes
            else:
                for n, part in enumerate(here):
                    store(q, n, part - (fluxes[n] - before[n]))
            before = fluxes
            here = following
        for n, part in enumerate(first):
            store(0, n, part - (opening[n] - before[n]))

    def propagate(ch):
        def one(n, _):
            i = ch * CHUNK + n
            west, mid, east, beside = ([coef[i, part, m] for m in range(6)] for part in range(4))
            wet_here = from_lon(wets, 0)
            wide = (west, mid, east)
            narrow = (mid, beside)

            def first_step(q):
                parts = along_lon(q, (halo_w[i, q], field[i, q], halo_e[i, q]), wide, False)
                return [along_lat(q, part, c) for part, c in zip(parts, wide)]

            def second_step(q):
                parts = along_lon(q, [one_on[part, q] for part in range(3)], wide, False)
                parts = (parts[MID], jnp.where(row < 4, parts[EAST], parts[WEST]))
                return [along_lat(q, part, c) for part, c in zip(parts, narrow)]

            def third_step(q):
                parts = along_lon(q, (two_on[0, q], two_on[1, q]), narrow, True)
                return [along_lat(q, part, c) for part, c in zip(parts, narrow)]

            def fourth_step(q):
                parts = along_lon(q, (three_on[0, q], three_on[1, q]), narrow, True)
                return [along_lat(q, parts[0], mid)]

            def to(buffer):
                def store(q, part, energy):
                    buffer[part, q] = energy
                return store

            def to_back(q, part, energy):
                back[pl.ds(n * DIRS + ORDER[q], 8, stride=ROWS), :] = energy * wet_here

            refracted(first_step, wide, to(one_on))
            refracted(second_step, narrow, to(two_on))
            refracted(third_step, narrow, to(three_on))
            refracted(fourth_step, (mid,), to_back)
            return 0

        lax.fori_loop(0, CHUNK, one, 0)

    def send_back(ch):
        for v in range(BLOCKS):
            blocks[v] = back[v * ROWS:(v + 1) * ROWS, :]
        for s in range(SOURCES):
            outb[ch, s] = blocks[back_row[s]] * kept[s]
        for k, dg in [(k, dg) for k in (2, 0, 1) for dg in (3, 2, 1, 0)]:
            to = across(dg)
            if True:
                src = outb.at[ch, to * SLOTS + k]
                dst = out.at[k, pl.ds(me_c * GROUP_COMPS + ch * ROWS, ROWS)]
                if dg == 0 and k == 1:
                    pltpu.make_async_copy(src, dst, out_recv).start()
                else:
                    pltpu.make_async_remote_copy(
                        src, dst, out_send.at[ch], out_recv, device_id=(to, region(1 - k)), device_id_type=MESH
                    ).start()

    def step(t, _):
        for ch in range(CHUNKS):
            @pl.when(t == ch)
            def _(ch=ch):
                if ch + WINDOW < CHUNKS:
                    wait_bytes(inb[ch].at[0:SOURCES - 1], in_send.at[ch])
                    send_in(ch + WINDOW)
                wait_bytes(inb[ch], in_recv.at[ch])
                for v in range(BLOCKS):
                    ordered[v * ROWS:(v + 1) * ROWS, :] = inb[ch][holder[v]]
                if ch == 0:
                    wait_bytes(aux_in, aux_recv)
                    for v in range(BLOCKS):
                        for n in range(3):
                            scal[n, v:v + 1, :] = aux_in[holder[v]][n:n + 1, :]

        @pl.when(t < CHUNKS)
        def _():
            source_terms(t)
            send_halos(t)

        @pl.when(t >= LAG)
        def _():
            for copy in halo_copies(t - LAG):
                copy.wait_recv()
            propagate(t - LAG)
            send_back(t - LAG)

        return 0

    lax.fori_loop(0, CHUNKS + LAG, step, 0)

    wait_bytes(aux_in.at[0:SOURCES - 1], aux_send)
    for ch in range(CHUNKS):
        if ch + WINDOW >= CHUNKS:
            wait_bytes(inb[ch].at[0:SOURCES - 1], in_send.at[ch])
        wait_bytes(outb.at[ch, 0:SOURCES - 1], out_send.at[ch])

    def drain(n, _):
        for copy in halo_copies(n):
            copy.wait_send()
        return 0

    lax.fori_loop(0, CHUNKS, drain, 0)
    wait_bytes(out, out_recv)


def finish(moved, out, sems):
    copies = [pltpu.make_async_copy(moved.at[k], out.at[k], sems.at[k]) for k in range(SLOTS)]
    for copy in copies:
        copy.start()
    for copy in copies:
        copy.wait()


def per_device(spectra, wind_vectors, slot_block, wet_mask, depth_class):
    hbm = pl.BlockSpec(memory_space=pltpu.HBM)
    vmem = pl.BlockSpec(memory_space=pltpu.VMEM)
    f32 = jnp.float32
    dma = pltpu.SemaphoreType.DMA
    scratch = [
        pltpu.VMEM((SLOTS, COMPS, POINTS), f32),
        pltpu.VMEM((SLOTS, 2, POINTS), f32),
        pltpu.SMEM((GROUPS * REGIONS * SLOTS,), jnp.int32),
        pltpu.VMEM((GRID_LON, 2 * POINTS), jnp.int32),
        pltpu.VMEM((2, GRID_LON), jnp.int32),
        pltpu.SMEM((T_SIZE,), f32),
        pltpu.VMEM((2, 8, POINTS), f32),
        pltpu.VMEM((SLOTS, 4, POINTS), f32),
        pltpu.VMEM((SOURCES, 4, POINTS), f32),
        pltpu.VMEM((3, 8, POINTS), f32),
        pltpu.VMEM((2, 32, POINTS), f32),
        pltpu.VMEM((32, POINTS), f32),
        pltpu.VMEM((GROUP_FREQS, 4, 6, 8, POINTS), f32),
        pltpu.VMEM(((BLOCKS + 1) * ROWS, POINTS), f32),
        pltpu.VMEM((GROUP_FREQS, DIRS, 8, POINTS), f32),
        pltpu.VMEM((GROUP_FREQS, DIRS, 8, POINTS), f32),
        pltpu.VMEM((GROUP_FREQS, DIRS, 8, POINTS), f32),
        pltpu.VMEM((3, DIRS, 8, POINTS), f32),
        pltpu.VMEM((2, DIRS, 8, POINTS), f32),
        pltpu.VMEM((2, DIRS, 8, POINTS), f32),
        pltpu.VMEM(((BLOCKS + 1) * ROWS, POINTS), f32),
        pltpu.VMEM((BLOCKS, ROWS, POINTS), f32),
        pltpu.VMEM((CHUNKS, SOURCES, ROWS, POINTS), f32),
        dma((7,)),
        dma((CHUNKS,)),
        dma((CHUNKS,)),
        dma,
        dma,
        dma((2, CHUNKS)),
        dma((2, CHUNKS)),
        dma((CHUNKS,)),
        dma,
        pltpu.SemaphoreType.REGULAR,
    ] + [pltpu.VMEM((SOURCES, ROWS, POINTS), f32) for _ in range(CHUNKS)]
    given = (spectra, wind_vectors, slot_block, wet_mask, depth_class.T, scalar_table(), latitude_table())
    moved = pl.pallas_call(
        kernel,
        out_shape=pltpu.VMEM((SLOTS, COMPS, POINTS), f32),
        in_specs=[hbm] * 7,
        out_specs=vmem,
        scratch_shapes=scratch,
        compiler_params=pltpu.CompilerParams(
            collective_id=0, has_side_effects=True, vmem_limit_bytes=40 * 1024 * 1024
        ),
        name="wave_step",
    )(*[pltpu.with_memory_space_constraint(jnp.asarray(array), pltpu.HBM) for array in given])
    return pl.pallas_call(
        finish,
        out_shape=jax.ShapeDtypeStruct((SLOTS, COMPS, POINTS), f32),
        in_specs=[vmem],
        out_specs=hbm,
        scratch_shapes=[dma((SLOTS,))],
        compiler_params=pltpu.CompilerParams(vmem_limit_bytes=8 * 1024 * 1024),
        name="finish",
    )(pltpu.with_memory_space_constraint(moved, pltpu.VMEM))


def solution(mesh):
    return jax.shard_map(
        per_device,
        mesh=mesh,
        in_specs=(P(("comp", "lon"), None, None), P(("comp", "lon"), None, None), P(), P(), P()),
        out_specs=P(("comp", "lon"), None, None),
        check_vma=False,
    )
```

```python
import functools

import jax
import jax.numpy as jnp
import numpy as np
from jax import lax
from jax.experimental import pallas as pl
from jax.experimental.pallas import tpu as pltpu
from jax.sharding import PartitionSpec as P

MESH = pl.DeviceIdType.MESH

DIRS = 36
HALF = DIRS // 2
FREQS = 48
GROUPS = 4
REGIONS = 32
SLOTS = 3
SOURCES = GROUPS * SLOTS
POINTS = 128
NDEPTH = 8
NSUB = 4
BLOCKS = 8
GRID_LON = 128
REGION_LONS = GRID_LON // REGIONS
GROUP_FREQS = FREQS // GROUPS
COMPS = FREQS * DIRS
GROUP_COMPS = GROUP_FREQS * DIRS

CHUNK = 2
CHUNKS = GROUP_FREQS // CHUNK
ROWS = CHUNK * DIRS

GRAVITY = 9.81

ORDER = [(q + 27) % DIRS for q in range(DIRS)]
ANGLE = (np.arange(DIRS) + 0.5) * (2.0 * np.pi / DIRS)
COS = np.cos(ANGLE)
SIN = np.sin(ANGLE)
COS_FACE = 0.5 * (COS + np.roll(COS, -1))
SIN_FACE = 0.5 * (SIN + np.roll(SIN, -1))

T_SPEED = 0
T_ALONG = T_SPEED + NDEPTH * FREQS
T_GAIN = T_ALONG + FREQS
T_SQUARE = T_GAIN + FREQS
T_WEIGHT = T_SQUARE + FREQS
T_WEIGHT_FREQ = T_WEIGHT + FREQS
T_SIZE = 640
LAG = 2
WINDOW = 3

WEST, MID, EAST, BESIDE = range(4)


def scalar_table():
    sigma = 2.0 * np.pi * 0.0418 * 1.07 ** np.arange(FREQS, dtype=np.float64)
    depth = 8.0 * 2.0 ** np.arange(NDEPTH, dtype=np.float64)
    deep = sigma * sigma / GRAVITY
    number = deep[None, :] / np.sqrt(np.tanh(deep[None, :] * depth[:, None]))
    twice = 2.0 * number * depth[:, None]
    factor = 2.0 * twice * np.exp(-twice) / (1.0 - np.exp(-2.0 * twice))
    speed = 0.5 * sigma[None, :] / number * (1.0 + factor)
    speed = speed / speed.max()
    weight = sigma / (sigma.sum() * DIRS)
    table = np.zeros(T_SIZE, np.float64)
    table[T_SPEED:T_ALONG] = speed.reshape(-1)
    table[T_ALONG:T_GAIN] = sigma / GRAVITY
    table[T_GAIN:T_SQUARE] = 0.5 * sigma / sigma[-1]
    table[T_SQUARE:T_WEIGHT] = sigma * sigma
    table[T_WEIGHT:T_WEIGHT_FREQ] = weight
    table[T_WEIGHT_FREQ:T_WEIGHT_FREQ + FREQS] = weight * sigma
    return table.astype(np.float32)


def latitude_table():
    count = 2 * POINTS
    phi = (-60.0 + (np.arange(count) + 0.5) * 120.0 / count) * np.pi / 180.0
    rows = np.concatenate([0.5 * 0.45 / np.cos(phi), 0.3 * np.tan(phi)])
    parts = rows.reshape(2, 1, 2, POINTS)
    return np.broadcast_to(parts, (2, REGION_LONS, 2, POINTS)).reshape(2, 8, POINTS).astype(np.float32)


def wait_bytes(ref, sem):
    pltpu.make_async_copy(ref, ref, sem).wait()


def kernel(
    x, wind, slots, wet, depth, table, lat, out,
    xv, windv, slot_s, wetv, depthv, table_s, latv,
    aux_out, aux_in, scal, cells, speeds, coef, ordered, field, halo_w, halo_e, one_on, two_on, three_on, back, blocks, outb,
    local_sem, in_send, in_recv, aux_send, aux_recv, halo_send, halo_recv, out_send, out_recv, ready,
    *inb,
):
    me_c = lax.axis_index("comp")
    me_r = lax.axis_index("lon")

    def region(shift):
        return lax.rem(me_r + (shift + REGIONS), REGIONS)

    def across(dg):
        return lax.rem(me_c + jnp.where(lax.rem(me_r, 2) == 0, dg, (GROUPS - dg) % GROUPS), GROUPS)

    loads = [
        pltpu.make_async_copy(src, dst, local_sem.at[n])
        for n, (src, dst) in enumerate(
            ((x, xv), (wind, windv), (slots, slot_s), (wet, wetv), (depth, depthv), (table, table_s), (lat, latv))
        )
    ]
    barrier = pltpu.get_barrier_semaphore()
    for dg in range(GROUPS):
        for dr in (-1, 0, 1):
            if (dg == 0) != (dr == 0):
                pl.semaphore_signal(
                    barrier, inc=1, device_id=(lax.rem(me_c + dg, GROUPS), region(dr)), device_id_type=MESH
                )
    for load in loads:
        load.start()
    pl.semaphore_wait(barrier, GROUPS + 1)

    def send_in(ch, slots=(0, 2, 1)):
        for k, dg in [(k, dg) for k in slots for dg in (1, 2, 3, 0)]:
            to = across(dg)
            if True:
                src = x.at[k, pl.ds(to * GROUP_COMPS + ch * ROWS, ROWS)]
                dst = inb[ch].at[me_c * SLOTS + k]
                if dg == 0 and k == 1:
                    pltpu.make_async_copy(src, dst, in_recv.at[ch]).start()
                else:
                    pltpu.make_async_remote_copy(
                        src, dst, in_send.at[ch], in_recv.at[ch], device_id=(to, region(k - 1)), device_id_type=MESH
                    ).start()

    for dg in range(1, GROUPS):
        pl.semaphore_signal(ready, inc=1, device_id=(lax.rem(me_c + dg, GROUPS), me_r), device_id_type=MESH)
    for ch in range(2):
        send_in(ch, (1,))
    row = lax.broadcasted_iota(jnp.int32, (8, POINTS), 0)
    lane = lax.broadcasted_iota(jnp.int32, (8, POINTS), 1)

    for load in loads:
        load.wait()
    upper = row < 4
    for k in range(SLOTS):
        def pair(p, sums, k=k):
            total, moment = sums
            tiles = [xv[k, pl.ds(pl.multiple_of(p * 72 + 8 * n, 8), 8), :] for n in range(9)]
            first = (tiles[0] + tiles[1]) + (tiles[2] + tiles[3]) + jnp.where(upper, tiles[4], 0.0)
            second = (tiles[5] + tiles[6]) + (tiles[7] + tiles[8]) + jnp.where(upper, 0.0, tiles[4])
            total = total + first * table_s[T_WEIGHT + 2 * p] + second * table_s[T_WEIGHT + 2 * p + 1]
            moment = moment + first * table_s[T_WEIGHT_FREQ + 2 * p] + second * table_s[T_WEIGHT_FREQ + 2 * p + 1]
            return total, moment

        zero = jnp.zeros((8, POINTS), jnp.float32)
        total, moment = lax.fori_loop(0, FREQS // 2, pair, (zero, zero))
        total = jnp.sum(total, axis=0, keepdims=True)
        moment = jnp.sum(moment, axis=0, keepdims=True)
        mean = moment / (total + 1e-6)
        aux_out[k, 3:4, :] = zero[0:1]
        aux_out[k, 0:2, :] = windv[k]
        aux_out[k, 2:3, :] = 0.3 * (total / (total + 1.0)) / (mean * mean)

    pl.semaphore_wait(ready, GROUPS - 1)
    for ch in range(2):
        send_in(ch, (0, 2))

    for dg in (2, 1, 3, 0):
        to = lax.rem(me_c + dg, GROUPS)
        for k in range(SLOTS):
            dst = aux_in.at[me_c * SLOTS + k]
            if dg == 0 and k == 1:
                pltpu.make_async_copy(aux_out.at[k], dst, aux_recv).start()
            else:
                pltpu.make_async_remote_copy(
                    aux_out.at[k], dst, aux_send, aux_recv, device_id=(to, region(k - 1)), device_id_type=MESH
                ).start()

    for ch in range(2, WINDOW):
        send_in(ch)

    for n in range(16):
        lon = lax.rem(me_r * REGION_LONS + (n - 6 + GRID_LON), GRID_LON)
        levels = jnp.where(lane[0:2] == lon, depthv[...].astype(jnp.float32), 0.0)
        cells[0, 2 * n:2 * n + 2, :] = jnp.broadcast_to(jnp.sum(levels, axis=1, keepdims=True), (2, POINTS))
        rows = pl.ds(pl.multiple_of(lon // 8 * 8, 8), 8)
        here = row == lax.rem(lon, 8)
        for part in range(2):
            wet_rows = wetv[rows, part * POINTS:(part + 1) * POINTS].astype(jnp.float32)
            cells[1, 2 * n + part:2 * n + part + 1, :] = jnp.sum(
                jnp.where(here, wet_rows, 0.0), axis=0, keepdims=True
            )

    def from_lon(values, start):
        return values[2 * (start + 6):2 * (start + 6) + 8]

    def shift_down(value):
        rolled = pltpu.roll(value, 1, 1)
        return jnp.where(lane == 0, pltpu.roll(rolled, 1, 0), rolled)

    def shift_up(value):
        rolled = pltpu.roll(value, POINTS - 1, 1)
        return jnp.where(lane == POINTS - 1, pltpu.roll(rolled, 7, 0), rolled)

    last = (lax.rem(row, 2) == 1) & (lane == POINTS - 1)
    wets = cells.at[1]

    def prepare(i, _):
        for m in range(4):
            level = cells[0, 8 * m:8 * m + 8]
            speed = jnp.zeros((8, POINTS), jnp.float32)
            for d in range(NDEPTH):
                speed = jnp.where(level == float(d), table_s[T_SPEED + d * FREQS + me_c * GROUP_FREQS + i], speed)
            speeds[8 * m:8 * m + 8] = speed
        made = []
        for part, start in enumerate((-REGION_LONS, 0, REGION_LONS)):
            west, mid, east = (from_lon(speeds, start + n) for n in (-1, 0, 1))
            wet_west, wet_mid, wet_east = (from_lon(wets, start + n) for n in (-1, 0, 1))
            face = jnp.where(last, 0.0, 0.45 * (mid + shift_up(mid)) * wet_mid * shift_up(wet_mid))
            made.append((
                latv[0] * (mid + east) * wet_mid * wet_east,
                latv[0] * (mid + west) * wet_mid * wet_west,
                face,
                shift_down(face),
                latv[1] * mid,
                0.4 * (east - west),
            ))
        for n in range(6):
            for part in range(3):
                coef[i, part, n] = made[part][n]
            coef[i, BESIDE, n] = jnp.where(row < 4, made[EAST][n], made[WEST][n])
        return 0

    lax.fori_loop(0, GROUP_FREQS, prepare, 0)

    held = []
    for s in range(SOURCES):
        held.append(slot_s[((s // SLOTS) * REGIONS + region(1 - s % SLOTS)) * SLOTS + s % SLOTS])
    holder = []
    for v in range(BLOCKS):
        found = jnp.int32(0)
        for s in range(SOURCES):
            found = jnp.where(held[s] == v, jnp.int32(s), found)
        holder.append(found)
    back_row = [jnp.maximum(h, 0) for h in held]
    kept = [jnp.where(h >= 0, jnp.float32(1.0), jnp.float32(0.0)) for h in held]

    def halo_copies(ch):
        freqs = pl.ds(ch * CHUNK, CHUNK)
        return [
            pltpu.make_async_remote_copy(
                field.at[freqs], halo.at[freqs], halo_send.at[n, ch], halo_recv.at[n, ch],
                device_id=(me_c, region(shift)), device_id_type=MESH,
            )
            for n, (halo, shift) in enumerate(((halo_w, 1), (halo_e, -1)))
        ]

    def send_halos(ch):
        for copy in halo_copies(ch):
            copy.start()

    def source_terms(ch):
        wind_x, wind_y, damp = scal[0], scal[1], scal[2]
        for n in range(CHUNK):
            i = ch * CHUNK + n
            f = me_c * GROUP_FREQS + i
            along = table_s[T_ALONG + f]
            gain = table_s[T_GAIN + f]
            scale = 1.0 / (1.0 + damp * table_s[T_SQUARE + f])
            for q in range(DIRS):
                j = ORDER[q]
                energy = ordered[pl.ds(n * DIRS + j, 8, stride=ROWS), :]
                ratio = jnp.maximum((wind_x * float(COS[j]) + wind_y * float(SIN[j])) * along, 1.0)
                field[i, q] = energy * ((1.0 + gain) - gain / ratio) * scale

    def along_lon(q, parts, coefs, ring):
        turn = 2 if q < HALF else 6
        rolled = [pltpu.roll(part, turn, 0) for part in parts]
        edge = row < 2 if q < HALF else row >= 6
        moved = []
        for n, part in enumerate(parts):
            other = n - 1 if q < HALF else n + 1
            if ring:
                beside = jnp.where(edge, rolled[other % len(parts)], rolled[n])
            elif 0 <= other < len(parts):
                beside = jnp.where(edge, rolled[other], rolled[n])
            else:
                beside = rolled[n]
            from_west, from_east = (beside, part) if q < HALF else (part, beside)
            flux = coefs[n][0] * from_east - coefs[n][1] * from_west
            moved.append(part - float(COS[ORDER[q]]) * flux)
        return moved

    def along_lat(q, energy, coefs):
        sine = float(SIN[ORDER[q]])
        if sine > 0:
            share = coefs[2] * energy
            flux = share - shift_down(share)
        else:
            share = coefs[3] * energy
            flux = shift_up(share) - share
        return energy - sine * flux

    def refracted(moved, coefs, store):
        first = moved(0)
        here = first
        opening = before = None
        for q in range(DIRS):
            following = moved(q + 1) if q + 1 < DIRS else first
            j = ORDER[q]
            fluxes = []
            for n, part in enumerate(here):
                rate = coefs[n][4] * float(COS_FACE[j]) + coefs[n][5] * float(SIN_FACE[j])
                fluxes.append(rate * jnp.where(rate > 0.0, part, following[n]))
            if q == 0:
                opening = fluxes
            else:
                for n, part in enumerate(here):
                    store(q, n, part - (fluxes[n] - before[n]))
            before = fluxes
            here = following
        for n, part in enumerate(first):
            store(0, n, part - (opening[n] - before[n]))

    def propagate(ch):
        def one(n, _):
            i = ch * CHUNK + n
            west, mid, east, beside = ([coef[i, part, m] for m in range(6)] for part in range(4))
            wet_here = from_lon(wets, 0)
            wide = (west, mid, east)
            narrow = (mid, beside)

            def first_step(q):
                parts = along_lon(q, (halo_w[i, q], field[i, q], halo_e[i, q]), wide, False)
                return [along_lat(q, part, c) for part, c in zip(parts, wide)]

            def second_step(q):
                parts = along_lon(q, [one_on[part, q] for part in range(3)], wide, False)
                parts = (parts[MID], jnp.where(row < 4, parts[EAST], parts[WEST]))
                return [along_lat(q, part, c) for part, c in zip(parts, narrow)]

            def third_step(q):
                parts = along_lon(q, (two_on[0, q], two_on[1, q]), narrow, True)
                return [along_lat(q, part, c) for part, c in zip(parts, narrow)]

            def fourth_step(q):
                parts = along_lon(q, (three_on[0, q], three_on[1, q]), narrow, True)
                return [along_lat(q, parts[0], mid)]

            def to(buffer):
                def store(q, part, energy):
                    buffer[part, q] = energy
                return store

            def to_back(q, part, energy):
                back[pl.ds(n * DIRS + ORDER[q], 8, stride=ROWS), :] = energy * wet_here

            refracted(first_step, wide, to(one_on))
            refracted(second_step, narrow, to(two_on))
            refracted(third_step, narrow, to(three_on))
            refracted(fourth_step, (mid,), to_back)
            return 0

        lax.fori_loop(0, CHUNK, one, 0)

    def send_back(ch):
        for v in range(BLOCKS):
            blocks[v] = back[v * ROWS:(v + 1) * ROWS, :]
        for s in range(SOURCES):
            outb[ch, s] = blocks[back_row[s]] * kept[s]
        for k, dg in [(k, dg) for k in (2, 0, 1) for dg in (3, 2, 1, 0)]:
            to = across(dg)
            if True:
                src = outb.at[ch, to * SLOTS + k]
                dst = out.at[k, pl.ds(me_c * GROUP_COMPS + ch * ROWS, ROWS)]
                if dg == 0 and k == 1:
                    pltpu.make_async_copy(src, dst, out_recv).start()
                else:
                    pltpu.make_async_remote_copy(
                        src, dst, out_send.at[ch], out_recv, device_id=(to, region(1 - k)), device_id_type=MESH
                    ).start()

    def step(t, _):
        for ch in range(CHUNKS):
            @pl.when(t == ch)
            def _(ch=ch):
                if ch + WINDOW < CHUNKS:
                    wait_bytes(inb[ch].at[0:SOURCES - 1], in_send.at[ch])
                    send_in(ch + WINDOW)
                wait_bytes(inb[ch], in_recv.at[ch])
                for v in range(BLOCKS):
                    ordered[v * ROWS:(v + 1) * ROWS, :] = inb[ch][holder[v]]
                if ch == 0:
                    wait_bytes(aux_in, aux_recv)
                    for v in range(BLOCKS):
                        for n in range(3):
                            scal[n, v:v + 1, :] = aux_in[holder[v]][n:n + 1, :]

        @pl.when(t < CHUNKS)
        def _():
            source_terms(t)
            send_halos(t)

        @pl.when(t >= LAG)
        def _():
            for copy in halo_copies(t - LAG):
                copy.wait_recv()
            propagate(t - LAG)
            send_back(t - LAG)

        return 0

    lax.fori_loop(0, CHUNKS + LAG, step, 0)

    wait_bytes(aux_in.at[0:SOURCES - 1], aux_send)
    for ch in range(CHUNKS):
        if ch + WINDOW >= CHUNKS:
            wait_bytes(inb[ch].at[0:SOURCES - 1], in_send.at[ch])
        wait_bytes(outb.at[ch, 0:SOURCES - 1], out_send.at[ch])

    def drain(n, _):
        for copy in halo_copies(n):
            copy.wait_send()
        return 0

    lax.fori_loop(0, CHUNKS, drain, 0)
    wait_bytes(out, out_recv)


def finish(moved, out, sems):
    copies = [pltpu.make_async_copy(moved.at[k], out.at[k], sems.at[k]) for k in range(SLOTS)]
    for copy in copies:
        copy.start()
    for copy in copies:
        copy.wait()


def per_device(spectra, wind_vectors, slot_block, wet_mask, depth_class):
    hbm = pl.BlockSpec(memory_space=pltpu.HBM)
    vmem = pl.BlockSpec(memory_space=pltpu.VMEM)
    f32 = jnp.float32
    dma = pltpu.SemaphoreType.DMA
    scratch = [
        pltpu.VMEM((SLOTS, COMPS, POINTS), f32),
        pltpu.VMEM((SLOTS, 2, POINTS), f32),
        pltpu.SMEM((GROUPS * REGIONS * SLOTS,), jnp.int32),
        pltpu.VMEM((GRID_LON, 2 * POINTS), jnp.int32),
        pltpu.VMEM((2, GRID_LON), jnp.int32),
        pltpu.SMEM((T_SIZE,), f32),
        pltpu.VMEM((2, 8, POINTS), f32),
        pltpu.VMEM((SLOTS, 4, POINTS), f32),
        pltpu.VMEM((SOURCES, 4, POINTS), f32),
        pltpu.VMEM((3, 8, POINTS), f32),
        pltpu.VMEM((2, 32, POINTS), f32),
        pltpu.VMEM((32, POINTS), f32),
        pltpu.VMEM((GROUP_FREQS, 4, 6, 8, POINTS), f32),
        pltpu.VMEM(((BLOCKS + 1) * ROWS, POINTS), f32),
        pltpu.VMEM((GROUP_FREQS, DIRS, 8, POINTS), f32),
        pltpu.VMEM((GROUP_FREQS, DIRS, 8, POINTS), f32),
        pltpu.VMEM((GROUP_FREQS, DIRS, 8, POINTS), f32),
        pltpu.VMEM((3, DIRS, 8, POINTS), f32),
        pltpu.VMEM((2, DIRS, 8, POINTS), f32),
        pltpu.VMEM((2, DIRS, 8, POINTS), f32),
        pltpu.VMEM(((BLOCKS + 1) * ROWS, POINTS), f32),
        pltpu.VMEM((BLOCKS, ROWS, POINTS), f32),
        pltpu.VMEM((CHUNKS, SOURCES, ROWS, POINTS), f32),
        dma((7,)),
        dma((CHUNKS,)),
        dma((CHUNKS,)),
        dma,
        dma,
        dma((2, CHUNKS)),
        dma((2, CHUNKS)),
        dma((CHUNKS,)),
        dma,
        pltpu.SemaphoreType.REGULAR,
    ] + [pltpu.VMEM((SOURCES, ROWS, POINTS), f32) for _ in range(CHUNKS)]
    given = (spectra, wind_vectors, slot_block, wet_mask, depth_class.T, scalar_table(), latitude_table())
    moved = pl.pallas_call(
        kernel,
        out_shape=pltpu.VMEM((SLOTS, COMPS, POINTS), f32),
        in_specs=[hbm] * 7,
        out_specs=vmem,
        scratch_shapes=scratch,
        compiler_params=pltpu.CompilerParams(
            collective_id=0, has_side_effects=True, vmem_limit_bytes=40 * 1024 * 1024
        ),
        name="wave_step",
    )(*[pltpu.with_memory_space_constraint(jnp.asarray(array), pltpu.HBM) for array in given])
    return pl.pallas_call(
        finish,
        out_shape=jax.ShapeDtypeStruct((SLOTS, COMPS, POINTS), f32),
        in_specs=[vmem],
        out_specs=hbm,
        scratch_shapes=[dma((SLOTS,))],
        compiler_params=pltpu.CompilerParams(vmem_limit_bytes=8 * 1024 * 1024),
        name="finish",
    )(pltpu.with_memory_space_constraint(moved, pltpu.VMEM))


def solution(mesh):
    return jax.shard_map(
        per_device,
        mesh=mesh,
        in_specs=(P(("comp", "lon"), None, None), P(("comp", "lon"), None, None), P(), P(), P()),
        out_specs=P(("comp", "lon"), None, None),
        check_vma=False,
    )
```

```python
import functools

import jax
import jax.numpy as jnp
import numpy as np
from jax import lax
from jax.experimental import pallas as pl
from jax.experimental.pallas import tpu as pltpu
from jax.sharding import PartitionSpec as P

MESH = pl.DeviceIdType.MESH

DIRS = 36
HALF = DIRS // 2
FREQS = 48
GROUPS = 4
REGIONS = 32
SLOTS = 3
SOURCES = GROUPS * SLOTS
POINTS = 128
NDEPTH = 8
NSUB = 4
BLOCKS = 8
GRID_LON = 128
REGION_LONS = GRID_LON // REGIONS
GROUP_FREQS = FREQS // GROUPS
COMPS = FREQS * DIRS
GROUP_COMPS = GROUP_FREQS * DIRS

CHUNK = 2
CHUNKS = GROUP_FREQS // CHUNK
ROWS = CHUNK * DIRS

GRAVITY = 9.81

ORDER = [(q + 27) % DIRS for q in range(DIRS)]
ANGLE = (np.arange(DIRS) + 0.5) * (2.0 * np.pi / DIRS)
COS = np.cos(ANGLE)
SIN = np.sin(ANGLE)
COS_FACE = 0.5 * (COS + np.roll(COS, -1))
SIN_FACE = 0.5 * (SIN + np.roll(SIN, -1))

T_SPEED = 0
T_ALONG = T_SPEED + NDEPTH * FREQS
T_GAIN = T_ALONG + FREQS
T_SQUARE = T_GAIN + FREQS
T_WEIGHT = T_SQUARE + FREQS
T_WEIGHT_FREQ = T_WEIGHT + FREQS
T_SIZE = 640
LAG = 2
WINDOW = 3

WEST, MID, EAST, BESIDE = range(4)


def scalar_table():
    sigma = 2.0 * np.pi * 0.0418 * 1.07 ** np.arange(FREQS, dtype=np.float64)
    depth = 8.0 * 2.0 ** np.arange(NDEPTH, dtype=np.float64)
    deep = sigma * sigma / GRAVITY
    number = deep[None, :] / np.sqrt(np.tanh(deep[None, :] * depth[:, None]))
    twice = 2.0 * number * depth[:, None]
    factor = 2.0 * twice * np.exp(-twice) / (1.0 - np.exp(-2.0 * twice))
    speed = 0.5 * sigma[None, :] / number * (1.0 + factor)
    speed = speed / speed.max()
    weight = sigma / (sigma.sum() * DIRS)
    table = np.zeros(T_SIZE, np.float64)
    table[T_SPEED:T_ALONG] = speed.reshape(-1)
    table[T_ALONG:T_GAIN] = sigma / GRAVITY
    table[T_GAIN:T_SQUARE] = 0.5 * sigma / sigma[-1]
    table[T_SQUARE:T_WEIGHT] = sigma * sigma
    table[T_WEIGHT:T_WEIGHT_FREQ] = weight
    table[T_WEIGHT_FREQ:T_WEIGHT_FREQ + FREQS] = weight * sigma
    return table.astype(np.float32)


def latitude_table():
    count = 2 * POINTS
    phi = (-60.0 + (np.arange(count) + 0.5) * 120.0 / count) * np.pi / 180.0
    rows = np.concatenate([0.5 * 0.45 / np.cos(phi), 0.3 * np.tan(phi)])
    parts = rows.reshape(2, 1, 2, POINTS)
    return np.broadcast_to(parts, (2, REGION_LONS, 2, POINTS)).reshape(2, 8, POINTS).astype(np.float32)


def wait_bytes(ref, sem):
    pltpu.make_async_copy(ref, ref, sem).wait()


def kernel(
    x, wind, slots, wet, depth, table, lat, out,
    xv, windv, slot_s, wetv, depthv, table_s, latv,
    aux_out, aux_in, scal, cells, speeds, coef, ordered, field, halo_w, halo_e, one_on, two_on, three_on, back, blocks, outb,
    local_sem, in_send, in_recv, aux_send, aux_recv, halo_send, halo_recv, out_send, out_recv, ready,
    *inb,
):
    me_c = lax.axis_index("comp")
    me_r = lax.axis_index("lon")

    def region(shift):
        return lax.rem(me_r + (shift + REGIONS), REGIONS)

    def across(dg):
        return lax.rem(me_c + jnp.where(lax.rem(me_r, 2) == 0, dg, (GROUPS - dg) % GROUPS), GROUPS)

    loads = [
        pltpu.make_async_copy(src, dst, local_sem.at[n])
        for n, (src, dst) in enumerate(
            ((x, xv), (wind, windv), (slots, slot_s), (wet, wetv), (depth, depthv), (table, table_s), (lat, latv))
        )
    ]
    barrier = pltpu.get_barrier_semaphore()
    for dg in range(GROUPS):
        for dr in (-1, 0, 1):
            if (dg == 0) != (dr == 0):
                pl.semaphore_signal(
                    barrier, inc=1, device_id=(lax.rem(me_c + dg, GROUPS), region(dr)), device_id_type=MESH
                )
    for load in loads:
        load.start()
    pl.semaphore_wait(barrier, GROUPS + 1)

    def send_in(ch, slots=(0, 2, 1)):
        for k, dg in [(k, dg) for k in slots for dg in (1, 2, 3, 0)]:
            to = across(dg)
            if True:
                src = x.at[k, pl.ds(to * GROUP_COMPS + ch * ROWS, ROWS)]
                dst = inb[ch].at[me_c * SLOTS + k]
                if dg == 0 and k == 1:
                    pltpu.make_async_copy(src, dst, in_recv.at[ch]).start()
                else:
                    pltpu.make_async_remote_copy(
                        src, dst, in_send.at[ch], in_recv.at[ch], device_id=(to, region(k - 1)), device_id_type=MESH
                    ).start()

    for dg in range(1, GROUPS):
        pl.semaphore_signal(ready, inc=1, device_id=(lax.rem(me_c + dg, GROUPS), me_r), device_id_type=MESH)
    for ch in range(2):
        send_in(ch, (1,))
    row = lax.broadcasted_iota(jnp.int32, (8, POINTS), 0)
    lane = lax.broadcasted_iota(jnp.int32, (8, POINTS), 1)

    for load in loads:
        load.wait()
    upper = row < 4
    for k in range(SLOTS):
        def pair(p, sums, k=k):
            total, moment = sums
            tiles = [xv[k, pl.ds(pl.multiple_of(p * 72 + 8 * n, 8), 8), :] for n in range(9)]
            first = (tiles[0] + tiles[1]) + (tiles[2] + tiles[3]) + jnp.where(upper, tiles[4], 0.0)
            second = (tiles[5] + tiles[6]) + (tiles[7] + tiles[8]) + jnp.where(upper, 0.0, tiles[4])
            total = total + first * table_s[T_WEIGHT + 2 * p] + second * table_s[T_WEIGHT + 2 * p + 1]
            moment = moment + first * table_s[T_WEIGHT_FREQ + 2 * p] + second * table_s[T_WEIGHT_FREQ + 2 * p + 1]
            return total, moment

        zero = jnp.zeros((8, POINTS), jnp.float32)
        total, moment = lax.fori_loop(0, FREQS // 2, pair, (zero, zero))
        total = jnp.sum(total, axis=0, keepdims=True)
        moment = jnp.sum(moment, axis=0, keepdims=True)
        mean = moment / (total + 1e-6)
        aux_out[k, 3:4, :] = zero[0:1]
        aux_out[k, 0:2, :] = windv[k]
        aux_out[k, 2:3, :] = 0.3 * (total / (total + 1.0)) / (mean * mean)

    pl.semaphore_wait(ready, GROUPS - 1)

    for dg in (2, 1, 3, 0):
        to = lax.rem(me_c + dg, GROUPS)
        for k in range(SLOTS):
            dst = aux_in.at[me_c * SLOTS + k]
            if dg == 0 and k == 1:
                pltpu.make_async_copy(aux_out.at[k], dst, aux_recv).start()
            else:
                pltpu.make_async_remote_copy(
                    aux_out.at[k], dst, aux_send, aux_recv, device_id=(to, region(k - 1)), device_id_type=MESH
                ).start()

    for ch in range(2):
        send_in(ch, (0, 2))
    for ch in range(2, WINDOW):
        send_in(ch)

    for n in range(16):
        lon = lax.rem(me_r * REGION_LONS + (n - 6 + GRID_LON), GRID_LON)
        levels = jnp.where(lane[0:2] == lon, depthv[...].astype(jnp.float32), 0.0)
        cells[0, 2 * n:2 * n + 2, :] = jnp.broadcast_to(jnp.sum(levels, axis=1, keepdims=True), (2, POINTS))
        rows = pl.ds(pl.multiple_of(lon // 8 * 8, 8), 8)
        here = row == lax.rem(lon, 8)
        for part in range(2):
            wet_rows = wetv[rows, part * POINTS:(part + 1) * POINTS].astype(jnp.float32)
            cells[1, 2 * n + part:2 * n + part + 1, :] = jnp.sum(
                jnp.where(here, wet_rows, 0.0), axis=0, keepdims=True
            )

    def from_lon(values, start):
        return values[2 * (start + 6):2 * (start + 6) + 8]

    def shift_down(value):
        rolled = pltpu.roll(value, 1, 1)
        return jnp.where(lane == 0, pltpu.roll(rolled, 1, 0), rolled)

    def shift_up(value):
        rolled = pltpu.roll(value, POINTS - 1, 1)
        return jnp.where(lane == POINTS - 1, pltpu.roll(rolled, 7, 0), rolled)

    last = (lax.rem(row, 2) == 1) & (lane == POINTS - 1)
    wets = cells.at[1]

    def prepare(i, _):
        for m in range(4):
            level = cells[0, 8 * m:8 * m + 8]
            speed = jnp.zeros((8, POINTS), jnp.float32)
            for d in range(NDEPTH):
                speed = jnp.where(level == float(d), table_s[T_SPEED + d * FREQS + me_c * GROUP_FREQS + i], speed)
            speeds[8 * m:8 * m + 8] = speed
        made = []
        for part, start in enumerate((-REGION_LONS, 0, REGION_LONS)):
            west, mid, east = (from_lon(speeds, start + n) for n in (-1, 0, 1))
            wet_west, wet_mid, wet_east = (from_lon(wets, start + n) for n in (-1, 0, 1))
            face = jnp.where(last, 0.0, 0.45 * (mid + shift_up(mid)) * wet_mid * shift_up(wet_mid))
            made.append((
                latv[0] * (mid + east) * wet_mid * wet_east,
                latv[0] * (mid + west) * wet_mid * wet_west,
                face,
                shift_down(face),
                latv[1] * mid,
                0.4 * (east - west),
            ))
        for n in range(6):
            for part in range(3):
                coef[i, part, n] = made[part][n]
            coef[i, BESIDE, n] = jnp.where(row < 4, made[EAST][n], made[WEST][n])
        return 0

    lax.fori_loop(0, GROUP_FREQS, prepare, 0)

    held = []
    for s in range(SOURCES):
        held.append(slot_s[((s // SLOTS) * REGIONS + region(1 - s % SLOTS)) * SLOTS + s % SLOTS])
    holder = []
    for v in range(BLOCKS):
        found = jnp.int32(0)
        for s in range(SOURCES):
            found = jnp.where(held[s] == v, jnp.int32(s), found)
        holder.append(found)
    back_row = [jnp.maximum(h, 0) for h in held]
    kept = [jnp.where(h >= 0, jnp.float32(1.0), jnp.float32(0.0)) for h in held]

    def halo_copies(ch):
        freqs = pl.ds(ch * CHUNK, CHUNK)
        return [
            pltpu.make_async_remote_copy(
                field.at[freqs], halo.at[freqs], halo_send.at[n, ch], halo_recv.at[n, ch],
                device_id=(me_c, region(shift)), device_id_type=MESH,
            )
            for n, (halo, shift) in enumerate(((halo_w, 1), (halo_e, -1)))
        ]

    def send_halos(ch):
        for copy in halo_copies(ch):
            copy.start()

    def source_terms(ch):
        wind_x, wind_y, damp = scal[0], scal[1], scal[2]
        for n in range(CHUNK):
            i = ch * CHUNK + n
            f = me_c * GROUP_FREQS + i
            along = table_s[T_ALONG + f]
            gain = table_s[T_GAIN + f]
            scale = 1.0 / (1.0 + damp * table_s[T_SQUARE + f])
            for q in range(DIRS):
                j = ORDER[q]
                energy = ordered[pl.ds(n * DIRS + j, 8, stride=ROWS), :]
                ratio = jnp.maximum((wind_x * float(COS[j]) + wind_y * float(SIN[j])) * along, 1.0)
                field[i, q] = energy * ((1.0 + gain) - gain / ratio) * scale

    def along_lon(q, parts, coefs, ring):
        turn = 2 if q < HALF else 6
        rolled = [pltpu.roll(part, turn, 0) for part in parts]
        edge = row < 2 if q < HALF else row >= 6
        moved = []
        for n, part in enumerate(parts):
            other = n - 1 if q < HALF else n + 1
            if ring:
                beside = jnp.where(edge, rolled[other % len(parts)], rolled[n])
            elif 0 <= other < len(parts):
                beside = jnp.where(edge, rolled[other], rolled[n])
            else:
                beside = rolled[n]
            from_west, from_east = (beside, part) if q < HALF else (part, beside)
            flux = coefs[n][0] * from_east - coefs[n][1] * from_west
            moved.append(part - float(COS[ORDER[q]]) * flux)
        return moved

    def along_lat(q, energy, coefs):
        sine = float(SIN[ORDER[q]])
        if sine > 0:
            share = coefs[2] * energy
            flux = share - shift_down(share)
        else:
            share = coefs[3] * energy
            flux = shift_up(share) - share
        return energy - sine * flux

    def refracted(moved, coefs, store):
        first = moved(0)
        here = first
        opening = before = None
        for q in range(DIRS):
            following = moved(q + 1) if q + 1 < DIRS else first
            j = ORDER[q]
            fluxes = []
            for n, part in enumerate(here):
                rate = coefs[n][4] * float(COS_FACE[j]) + coefs[n][5] * float(SIN_FACE[j])
                fluxes.append(rate * jnp.where(rate > 0.0, part, following[n]))
            if q == 0:
                opening = fluxes
            else:
                for n, part in enumerate(here):
                    store(q, n, part - (fluxes[n] - before[n]))
            before = fluxes
            here = following
        for n, part in enumerate(first):
            store(0, n, part - (opening[n] - before[n]))

    def propagate(ch):
        def one(n, _):
            i = ch * CHUNK + n
            west, mid, east, beside = ([coef[i, part, m] for m in range(6)] for part in range(4))
            wet_here = from_lon(wets, 0)
            wide = (west, mid, east)
            narrow = (mid, beside)

            def first_step(q):
                parts = along_lon(q, (halo_w[i, q], field[i, q], halo_e[i, q]), wide, False)
                return [along_lat(q, part, c) for part, c in zip(parts, wide)]

            def second_step(q):
                parts = along_lon(q, [one_on[part, q] for part in range(3)], wide, False)
                parts = (parts[MID], jnp.where(row < 4, parts[EAST], parts[WEST]))
                return [along_lat(q, part, c) for part, c in zip(parts, narrow)]

            def third_step(q):
                parts = along_lon(q, (two_on[0, q], two_on[1, q]), narrow, True)
                return [along_lat(q, part, c) for part, c in zip(parts, narrow)]

            def fourth_step(q):
                parts = along_lon(q, (three_on[0, q], three_on[1, q]), narrow, True)
                return [along_lat(q, parts[0], mid)]

            def to(buffer):
                def store(q, part, energy):
                    buffer[part, q] = energy
                return store

            def to_back(q, part, energy):
                back[pl.ds(n * DIRS + ORDER[q], 8, stride=ROWS), :] = energy * wet_here

            refracted(first_step, wide, to(one_on))
            refracted(second_step, narrow, to(two_on))
            refracted(third_step, narrow, to(three_on))
            refracted(fourth_step, (mid,), to_back)
            return 0

        lax.fori_loop(0, CHUNK, one, 0)

    def send_back(ch):
        for v in range(BLOCKS):
            blocks[v] = back[v * ROWS:(v + 1) * ROWS, :]
        for s in range(SOURCES):
            outb[ch, s] = blocks[back_row[s]] * kept[s]
        for k, dg in [(k, dg) for k in (2, 0, 1) for dg in (3, 2, 1, 0)]:
            to = across(dg)
            if True:
                src = outb.at[ch, to * SLOTS + k]
                dst = out.at[k, pl.ds(me_c * GROUP_COMPS + ch * ROWS, ROWS)]
                if dg == 0 and k == 1:
                    pltpu.make_async_copy(src, dst, out_recv).start()
                else:
                    pltpu.make_async_remote_copy(
                        src, dst, out_send.at[ch], out_recv, device_id=(to, region(1 - k)), device_id_type=MESH
                    ).start()

    def step(t, _):
        for ch in range(CHUNKS):
            @pl.when(t == ch)
            def _(ch=ch):
                if ch + WINDOW < CHUNKS:
                    wait_bytes(inb[ch].at[0:SOURCES - 1], in_send.at[ch])
                    send_in(ch + WINDOW)
                wait_bytes(inb[ch], in_recv.at[ch])
                for v in range(BLOCKS):
                    ordered[v * ROWS:(v + 1) * ROWS, :] = inb[ch][holder[v]]
                if ch == 0:
                    wait_bytes(aux_in, aux_recv)
                    for v in range(BLOCKS):
                        for n in range(3):
                            scal[n, v:v + 1, :] = aux_in[holder[v]][n:n + 1, :]

        @pl.when(t < CHUNKS)
        def _():
            source_terms(t)
            send_halos(t)

        @pl.when(t >= LAG)
        def _():
            for copy in halo_copies(t - LAG):
                copy.wait_recv()
            propagate(t - LAG)
            send_back(t - LAG)

        return 0

    lax.fori_loop(0, CHUNKS + LAG, step, 0)

    wait_bytes(aux_in.at[0:SOURCES - 1], aux_send)
    for ch in range(CHUNKS):
        if ch + WINDOW >= CHUNKS:
            wait_bytes(inb[ch].at[0:SOURCES - 1], in_send.at[ch])
        wait_bytes(outb.at[ch, 0:SOURCES - 1], out_send.at[ch])

    def drain(n, _):
        for copy in halo_copies(n):
            copy.wait_send()
        return 0

    lax.fori_loop(0, CHUNKS, drain, 0)
    wait_bytes(out, out_recv)


def finish(moved, out, sems):
    copies = [pltpu.make_async_copy(moved.at[k], out.at[k], sems.at[k]) for k in range(SLOTS)]
    for copy in copies:
        copy.start()
    for copy in copies:
        copy.wait()


def per_device(spectra, wind_vectors, slot_block, wet_mask, depth_class):
    hbm = pl.BlockSpec(memory_space=pltpu.HBM)
    vmem = pl.BlockSpec(memory_space=pltpu.VMEM)
    f32 = jnp.float32
    dma = pltpu.SemaphoreType.DMA
    scratch = [
        pltpu.VMEM((SLOTS, COMPS, POINTS), f32),
        pltpu.VMEM((SLOTS, 2, POINTS), f32),
        pltpu.SMEM((GROUPS * REGIONS * SLOTS,), jnp.int32),
        pltpu.VMEM((GRID_LON, 2 * POINTS), jnp.int32),
        pltpu.VMEM((2, GRID_LON), jnp.int32),
        pltpu.SMEM((T_SIZE,), f32),
        pltpu.VMEM((2, 8, POINTS), f32),
        pltpu.VMEM((SLOTS, 4, POINTS), f32),
        pltpu.VMEM((SOURCES, 4, POINTS), f32),
        pltpu.VMEM((3, 8, POINTS), f32),
        pltpu.VMEM((2, 32, POINTS), f32),
        pltpu.VMEM((32, POINTS), f32),
        pltpu.VMEM((GROUP_FREQS, 4, 6, 8, POINTS), f32),
        pltpu.VMEM(((BLOCKS + 1) * ROWS, POINTS), f32),
        pltpu.VMEM((GROUP_FREQS, DIRS, 8, POINTS), f32),
        pltpu.VMEM((GROUP_FREQS, DIRS, 8, POINTS), f32),
        pltpu.VMEM((GROUP_FREQS, DIRS, 8, POINTS), f32),
        pltpu.VMEM((3, DIRS, 8, POINTS), f32),
        pltpu.VMEM((2, DIRS, 8, POINTS), f32),
        pltpu.VMEM((2, DIRS, 8, POINTS), f32),
        pltpu.VMEM(((BLOCKS + 1) * ROWS, POINTS), f32),
        pltpu.VMEM((BLOCKS, ROWS, POINTS), f32),
        pltpu.VMEM((CHUNKS, SOURCES, ROWS, POINTS), f32),
        dma((7,)),
        dma((CHUNKS,)),
        dma((CHUNKS,)),
        dma,
        dma,
        dma((2, CHUNKS)),
        dma((2, CHUNKS)),
        dma((CHUNKS,)),
        dma,
        pltpu.SemaphoreType.REGULAR,
    ] + [pltpu.VMEM((SOURCES, ROWS, POINTS), f32) for _ in range(CHUNKS)]
    given = (spectra, wind_vectors, slot_block, wet_mask, depth_class.T, scalar_table(), latitude_table())
    moved = pl.pallas_call(
        kernel,
        out_shape=pltpu.VMEM((SLOTS, COMPS, POINTS), f32),
        in_specs=[hbm] * 7,
        out_specs=vmem,
        scratch_shapes=scratch,
        compiler_params=pltpu.CompilerParams(
            collective_id=0, has_side_effects=True, vmem_limit_bytes=40 * 1024 * 1024
        ),
        name="wave_step",
    )(*[pltpu.with_memory_space_constraint(jnp.asarray(array), pltpu.HBM) for array in given])
    return pl.pallas_call(
        finish,
        out_shape=jax.ShapeDtypeStruct((SLOTS, COMPS, POINTS), f32),
        in_specs=[vmem],
        out_specs=hbm,
        scratch_shapes=[dma((SLOTS,))],
        compiler_params=pltpu.CompilerParams(vmem_limit_bytes=8 * 1024 * 1024),
        name="finish",
    )(pltpu.with_memory_space_constraint(moved, pltpu.VMEM))


def solution(mesh):
    return jax.shard_map(
        per_device,
        mesh=mesh,
        in_specs=(P(("comp", "lon"), None, None), P(("comp", "lon"), None, None), P(), P(), P()),
        out_specs=P(("comp", "lon"), None, None),
        check_vma=False,
    )
```
